32 devices in a mesh: cube: 8 (over y, x, core), grid: 4 (over z).
Axes of the slice: x: 2, y: 2, z: 4, core: 2. Of those that a mesh axis runs over, the one named last changes fastest.
Arguments:
- child_update: bfloat16 [512, 2048], P('cube', 'grid'), may hold values from -6 to 6
- child_panel: bfloat16 [512, 512], P('grid', 'cube'), may hold values from -6 to 6
- panel_entries: bfloat16 [512, 4096], P('grid', 'cube'), may hold values from -6 to 6
- panel_inverse: bfloat16 [512, 512], replicated, as said below
- block_owner: int32 [128], replicated, may hold values from 0 to 7, as said below
- child_dest: int32 [32], replicated, may hold values from 0 to 127, as said below
- child_rows: int32 [32, 16], P('cube'), may hold values from 0 to 15, each once within a row
Outputs:
- schur_update: bfloat16 [4096, 2048], P('cube', 'grid')
- panel_factor: bfloat16 [512, 4096], P('grid', 'cube')
The draws below stay inside these ranges and needn't reach their ends.
Inputs may be any that keep to these rules, and one draw needn't show every extreme that they name: `block_owner`: row blocks r*32 to (r+1)*32 - 1 form column range r. One cube index owns at most 8 row blocks of one range, and in every draw some cube index owns exactly 8 of some range. Every cube index owns at least one row block. `child_dest`: entry s*4+k names the parent row block into which child row block k of cube index s adds. The 4 child row blocks of one cube index go to blocks of 4 different owners, and in every draw some owner receives a block from every cube index. `panel_inverse`: zero below the diagonal, positive on it.
All inputs are finite; a program needn't handle non-finite values.
Results may differ from the reference program's by a relative error of at most 0.0057.
Values may be sent and summed in bfloat16 or wider, within the bound.
No kernel may reach another device: no remote copies, remote signals or barrier semaphores. Data moves between devices by JAX's collectives and lax.ppermute only.
A program may use at most 64 MiB of HBM per device.

```python
import math
import jax
import jax.numpy as jnp
from jax import lax

PANEL = 512
BLOCK = 16
RANGE_MEAN = 4
RANGE_CAP = 8
SLOTS = 32
RANGE_BLOCKS = 32
UPDATE = 2048
CHILD_DEV = 4
CHILD_ROWS = 512
SLOT_ROWS = 4096
N_CUBE = 8
N_GRID = 4


def owner_table(key):
    owner_key = jax.random.fold_in(key, 101)
    perm_key, pair_key, order_key = jax.random.split(owner_key, 3)
    pair_count = N_CUBE // 2
    orders = jax.vmap(lambda subkey: jax.random.permutation(subkey, N_CUBE))(jax.random.split(perm_key, N_GRID))
    shifts = jax.random.randint(pair_key, (N_GRID, pair_count), 0, RANGE_MEAN + 1)
    first_range = jnp.arange(N_GRID, dtype=jnp.int32)[:, None] == 0
    shifts = jnp.where(first_range, jnp.minimum(shifts, RANGE_MEAN - 1), shifts)
    leading_pair = jnp.arange(pair_count, dtype=jnp.int32)[None, :] == 0
    shifts = jnp.where(leading_pair & jnp.logical_not(first_range), RANGE_MEAN, shifts)
    values = jnp.concatenate([RANGE_MEAN + shifts, RANGE_MEAN - shifts], axis=1).astype(jnp.int32)
    range_rows = jnp.broadcast_to(jnp.arange(N_GRID, dtype=jnp.int32)[:, None], (N_GRID, N_CUBE))
    counts = jnp.zeros((N_GRID, N_CUBE), jnp.int32).at[range_rows, orders].set(values)
    bounds = jnp.cumsum(counts, axis=1)
    position = jnp.arange(RANGE_BLOCKS, dtype=jnp.int32)
    sorted_owner = jnp.sum((bounds[:, None, :] <= position[None, :, None]).astype(jnp.int32), axis=2)
    shuffled = jax.vmap(lambda subkey, entries: jax.random.permutation(subkey, entries))(jax.random.split(order_key, N_GRID), sorted_owner)
    return shuffled.reshape(-1).astype(jnp.int32)


def draw_block_owner(key, part):
    return owner_table(key)


def draw_child_dest(key, part):
    owners = owner_table(key)
    hub_key, perm_key, pick_key = jax.random.split(jax.random.fold_in(key, 202), 3)
    hub_owner = jax.random.randint(hub_key, (), 0, N_CUBE)
    orders = jax.vmap(lambda subkey: jax.random.permutation(subkey, N_CUBE))(jax.random.split(perm_key, N_CUBE))
    chosen = orders[:, :CHILD_DEV]
    present = jnp.any(chosen == hub_owner, axis=1)
    leading = jnp.where(present, chosen[:, 0], hub_owner)
    chosen = jnp.concatenate([leading[:, None], chosen[:, 1:]], axis=1).reshape(-1)
    member = (owners[None, :] == chosen[:, None]).astype(jnp.int32)
    totals = jnp.sum(member, axis=1)
    picks = jax.random.randint(pick_key, chosen.shape, 0, 1048576) % totals
    running = jnp.cumsum(member, axis=1)
    return jnp.sum((running <= picks[:, None]).astype(jnp.int32), axis=1).astype(jnp.int32)


def draw_panel_inverse(key, part):
    off_key, diag_key = jax.random.split(jax.random.fold_in(key, 303))
    row_ids = jnp.arange(PANEL, dtype=jnp.int32)[:, None]
    col_ids = jnp.arange(PANEL, dtype=jnp.int32)[None, :]
    spread = jax.random.normal(off_key, (PANEL, PANEL), jnp.float32)
    spread = spread * (0.19 / math.sqrt(PANEL))
    diagonal = jnp.exp(jax.random.uniform(diag_key, (PANEL,), jnp.float32, math.log(0.05), math.log(0.2)))
    upper = jnp.where(col_ids > row_ids, spread, 0.0)
    whole = jnp.where(col_ids == row_ids, diagonal[None, :], upper)
    return whole.astype(jnp.bfloat16)


def block_scale(key, dims, pieces, smallest, largest):
    gain, own = 1.0, jax.random.fold_in(key, 6)
    for dim, shards_of in pieces:
        steps = jnp.exp(jax.random.uniform(jax.random.fold_in(own, dim), (shards_of,), jnp.float32, smallest / len(pieces), largest / len(pieces)))
        gain = gain * jnp.repeat(steps, dims[dim] // shards_of).reshape([-1 if axis == dim else 1 for axis in range(len(dims))])
    return gain


def normal_values(key, dims, width, limit, pieces=(), kind=jnp.bfloat16):
    factor_of = block_scale(key, dims, pieces, -0.22, 0.18) if pieces else 1.0
    result = jax.random.normal(key, dims, jnp.float32) * width * factor_of
    return jnp.minimum(jnp.maximum(result, -limit), limit).astype(kind)


def setup_inputs(seed: int = 0) -> dict:
    streams_of = jax.random.split(jax.random.key(seed), 8)
    child_update = normal_values(streams_of[0], (CHILD_ROWS, UPDATE), 1.0, 6.0, ((0, 8), (1, 4)))
    child_panel = normal_values(streams_of[1], (PANEL, CHILD_ROWS), 1.0, 6.0, ((0, 4), (1, 8)))
    panel_entries = normal_values(streams_of[2], (PANEL, SLOT_ROWS), 1.0, 6.0, ((0, 4), (1, 8)))
    panel_inverse = draw_panel_inverse(jax.random.fold_in(streams_of[7], 71), 0)
    block_owner = draw_block_owner(jax.random.fold_in(streams_of[7], 71), 0)
    child_dest = draw_child_dest(jax.random.fold_in(streams_of[7], 71), 0)
    child_rows = jax.vmap(lambda own: jax.random.permutation(own, BLOCK))(jax.random.split(streams_of[6], (N_CUBE * CHILD_DEV))).reshape((N_CUBE * CHILD_DEV, BLOCK)).astype(jnp.int32)
    return {"child_update": child_update, "child_panel": child_panel, "panel_entries": panel_entries, "panel_inverse": panel_inverse, "block_owner": block_owner, "child_dest": child_dest, "child_rows": child_rows}


def slot_of_blocks(block_owner):
    grouped = block_owner.reshape(N_GRID, RANGE_BLOCKS)
    owner_ids = jnp.arange(N_CUBE, dtype=jnp.int32)
    onehot = (grouped[:, :, None] == owner_ids[None, None, :]).astype(jnp.int32)
    running = jnp.cumsum(onehot, axis=1)
    block_rank = jnp.sum(onehot * running, axis=2) - 1
    range_ids = jnp.arange(N_GRID, dtype=jnp.int32)[:, None]
    return (grouped * SLOTS + range_ids * RANGE_CAP + block_rank).reshape(-1)


def reference(child_update, child_panel, panel_entries, panel_inverse, block_owner, child_dest, child_rows):
    within = jnp.arange(BLOCK, dtype=jnp.int32)
    slot_rows = (slot_of_blocks(block_owner)[:, None] * BLOCK + within[None, :]).reshape(-1)
    target = (child_dest[:, None] * BLOCK + child_rows).reshape(-1)
    front_update = jnp.zeros((UPDATE, UPDATE), jnp.float32).at[target].add(child_update.astype(jnp.float32))
    own_panel = jnp.take(panel_entries, slot_rows, axis=1).astype(jnp.float32)
    child_sum = jnp.zeros((PANEL, UPDATE), jnp.float32).at[:, target].add(child_panel.astype(jnp.float32))
    front_panel = (own_panel + child_sum).astype(jnp.bfloat16)
    factor = jnp.dot(panel_inverse.T, front_panel, preferred_element_type=jnp.float32).astype(jnp.bfloat16)
    row_step = math.gcd(UPDATE, 1024)

    def update_rows(first_row):
        factor_rows = lax.dynamic_slice_in_dim(factor, first_row, row_step, 1)
        front_rows = lax.dynamic_slice_in_dim(front_update, first_row, row_step, 0)
        product = jnp.dot(factor_rows.T, factor, preferred_element_type=jnp.float32)
        return (front_rows - product).astype(jnp.bfloat16)

    starts = jnp.arange(UPDATE // row_step, dtype=jnp.int32) * row_step
    schur = lax.map(update_rows, starts).reshape(UPDATE, UPDATE)
    schur_update = jnp.zeros((SLOT_ROWS, UPDATE), jnp.bfloat16).at[slot_rows].set(schur)
    panel_factor = jnp.zeros((PANEL, SLOT_ROWS), jnp.bfloat16).at[:, slot_rows].set(factor)
    return schur_update, panel_factor
```

```python
import functools

import jax
import jax.numpy as jnp
from jax import lax
from jax.experimental import pallas as pl
from jax.experimental.pallas import tpu as pltpu
from jax.sharding import PartitionSpec as P

F32 = jnp.float32
BF16 = jnp.bfloat16
VMEM = pl.BlockSpec(memory_space=pltpu.VMEM)
SMEM = pl.BlockSpec(memory_space=pltpu.SMEM)


def call(body, outs, in_specs, scratch, flops, moved, out_specs=None):
    return pl.pallas_call(
        body,
        out_shape=outs,
        in_specs=in_specs,
        out_specs=[VMEM] * len(outs) if out_specs is None else out_specs,
        scratch_shapes=scratch,
        compiler_params=pltpu.CompilerParams(vmem_limit_bytes=40 * 1024 * 1024),
        cost_estimate=pl.CostEstimate(flops=flops, bytes_accessed=moved, transcendentals=0),
    )


def plan_body(cubes, grids, slots, owner_ref, dest_ref, out_ref, slot_ref, count_ref):
    mine = lax.axis_index("cube")
    column = lax.axis_index("grid")
    blocks = owner_ref.shape[0]
    in_range = blocks // grids
    children = dest_ref.shape[0] // cubes
    places = cubes + grids
    for r in range(grids):

        def count_own(i, seen):
            b = r * in_range + i
            own = owner_ref[b] == mine
            slot_ref[b] = jnp.where(own, r * slots + seen, 0)
            return seen + own.astype(jnp.int32)

        out_ref[cubes + r] = lax.fori_loop(0, in_range, count_own, jnp.int32(0))
    for d in range(cubes):
        source = jnp.bitwise_xor(mine, d)
        slot = jnp.int32(0)
        for k in range(children):
            slot = jnp.maximum(slot, slot_ref[dest_ref[source * children + k]])
        out_ref[d] = slot
        count_ref[d] = 0
        for k in range(slots):
            out_ref[places + d * slots + k] = in_range

    def place(i, carry):
        d = jnp.bitwise_xor(owner_ref[column * in_range + i], mine)
        k = count_ref[d]
        out_ref[places + d * slots + k] = i
        count_ref[d] = k + 1
        return carry

    lax.fori_loop(0, in_range, place, 0)


def route_body(cubes, owner_ref, dest_ref, rows_ref, update_ref, panel_ref, *refs):
    outs, held = refs[:cubes], refs[cubes]
    mine = lax.axis_index("cube")
    children, rows = rows_ref.shape
    width = update_ref.shape[1]
    held[...] = jnp.zeros_like(held)
    for k in range(children):
        want = rows_ref[k : k + 1, :]
        put = (lax.broadcasted_iota(jnp.int32, (rows, rows), 0) == want).astype(BF16)
        d = jnp.bitwise_xor(owner_ref[dest_ref[mine * children + k]], mine)
        at = pl.ds(pl.multiple_of(d * rows, rows), rows)
        part = pl.ds(k * rows, rows)
        held[at, :width] = jnp.dot(put, update_ref[part, :], preferred_element_type=F32).astype(BF16)
        held[at, width:] = jnp.dot(put, panel_ref[part, :], preferred_element_type=F32).astype(BF16)
    for d in range(cubes):
        outs[d][...] = held[pl.ds(d * rows, rows), :]


def assemble_body(cubes, grids, slots, width, plan_ref, entries_ref, *refs):
    got, outs, total = refs[:cubes], refs[cubes:-1], refs[-1]
    column = lax.axis_index("grid")
    rows = got[0].shape[0]
    span = slots * rows
    total[...] = entries_ref[...].astype(F32).T
    for r in range(grids):
        part = pl.ds(r * span, span)
        ids = lax.broadcasted_iota(jnp.int32, (span, total.shape[1]), 0)
        live = ids < plan_ref[cubes + r] * rows
        total[part, :] = jnp.where(live, total[part, :], 0.0)
    for d in range(cubes):
        at = pl.ds(pl.multiple_of(plan_ref[d] * rows, rows), rows)
        total[at, :] += got[d][:, width:].astype(F32)
    for d in range(grids):
        at = pl.ds(pl.multiple_of(jnp.bitwise_xor(column, d) * span, span), span)
        piece = total[at, :].astype(BF16)
        outs[d][...] = piece
        for e in range(1, grids):
            if e != d:
                k = d if d < e else d - 1
                outs[grids + e - 1][pl.ds(k * span, span), :] = piece


def factor_range_body(grids, inverse_ref, *refs):
    parts, out_ref = refs[:grids], refs[grids]
    column = lax.axis_index("grid")
    depth = parts[0].shape[1]
    total = None
    for d in range(grids):
        at = pl.ds(pl.multiple_of(jnp.bitwise_xor(column, d) * depth, depth), depth)
        term = jnp.dot(parts[d][...], inverse_ref[at, :], preferred_element_type=F32)
        total = term if total is None else total + term
    out_ref[...] = total.astype(BF16)


def factor_own_body(grids, inverse_ref, *refs):
    own, small, rest = refs[:grids], refs[grids : 2 * grids - 1], refs[2 * grids - 1 : 3 * grids - 2]
    factor_ref, panel_ref = refs[3 * grids - 2 :]
    column = lax.axis_index("grid")
    span, depth = own[0].shape
    for e in range(grids):
        total = None
        for d in range(grids):
            k = d ^ e
            if d == 0:
                piece = own[e][...]
            elif e == 0:
                piece = small[d - 1][...]
            else:
                piece = rest[d - 1][pl.ds((k if k < d else k - 1) * span, span), :]
            at = pl.ds(pl.multiple_of(jnp.bitwise_xor(column, d) * depth, depth), depth)
            term = jnp.dot(piece, inverse_ref[at, :], preferred_element_type=F32)
            total = term if total is None else total + term
        at = pl.ds(pl.multiple_of(jnp.bitwise_xor(column, e) * span, span), span)
        factor_ref[at, :] = total.astype(BF16)
    if depth % 128 == 0:
        cols = pl.ds(pl.multiple_of(column * depth, depth), depth)
        panel_ref[...] = factor_ref[:, cols].astype(F32).T.astype(BF16)
    else:
        for r in range(grids):

            @pl.when(column == r)
            def _():
                panel_ref[...] = factor_ref[:, r * depth : (r + 1) * depth].astype(F32).T.astype(BF16)


def schur_body(cubes, grids, slots, width, plan_ref, factor_ref, *refs):
    got, pieces, out_ref, total, ranged = refs[:cubes], refs[cubes : 2 * cubes], refs[-3], refs[-2], refs[-1]
    rows = got[0].shape[0]
    places = cubes + grids
    total[...] = jnp.zeros_like(total)
    for d in range(cubes):
        at = pl.ds(pl.multiple_of(plan_ref[d] * rows, rows), rows)
        total[at, :] += got[d][:, :width].astype(F32)
        for k in range(slots):
            at = pl.ds(pl.multiple_of(plan_ref[places + d * slots + k] * rows, rows), rows)
            ranged[at, :] = pieces[d][pl.ds(k * rows, rows), :]
    product = lax.dot_general(
        factor_ref[...], ranged[pl.ds(0, width), :], (((1,), (1,)), ((), ())), preferred_element_type=F32
    )
    out_ref[...] = (total[...] - product).astype(BF16)


def local(
    child_update, child_panel, panel_entries, panel_inverse, block_owner, child_dest, child_rows
):
    cubes = lax.axis_size("cube")
    grids = lax.axis_size("grid")
    rows = child_rows.shape[1]
    width = child_update.shape[1]
    depth = child_panel.shape[0]
    panel = panel_inverse.shape[0]
    own_rows = panel_entries.shape[1]
    slots = own_rows // rows // grids
    span = slots * rows
    like = jax.ShapeDtypeStruct

    def swap(x, axis, d):
        n = lax.axis_size(axis)
        return lax.ppermute(x, axis, [(i, i ^ d) for i in range(n)])

    held = rows * (width + depth)
    sent = call(
        functools.partial(route_body, cubes),
        [like((rows, width + depth), BF16)] * cubes,
        [SMEM, SMEM, VMEM, VMEM, VMEM],
        [pltpu.VMEM((cubes * rows, width + depth), BF16)],
        2 * rows * held,
        4 * cubes * held,
    )(block_owner, child_dest, child_rows, child_update, child_panel.T)
    got = [sent[0]] + [swap(sent[d], "cube", d) for d in range(1, cubes)]
    plan = call(
        functools.partial(plan_body, cubes, grids, slots),
        [like((cubes + grids + cubes * slots,), jnp.int32)],
        [SMEM, SMEM],
        [pltpu.SMEM((block_owner.shape[0],), jnp.int32), pltpu.SMEM((cubes,), jnp.int32)],
        100000,
        4096,
        [SMEM],
    )(block_owner, child_dest)[0]
    parts = call(
        functools.partial(assemble_body, cubes, grids, slots, width),
        [like((span, depth), BF16)] * grids + [like(((grids - 1) * span, depth), BF16)] * (grids - 1),
        [SMEM, VMEM] + [VMEM] * cubes,
        [pltpu.VMEM((own_rows, depth), F32)],
        own_rows * depth * 4,
        own_rows * depth * 10,
    )(plan, panel_entries, *got)
    own, rest = parts[:grids], parts[grids:]
    small = [swap(own[d], "grid", d) for d in range(1, grids)]
    rest = [swap(rest[d - 1], "grid", d) for d in range(1, grids)]
    mine = call(
        functools.partial(factor_range_body, grids),
        [like((span, panel), BF16)],
        [VMEM] * (grids + 1),
        [],
        2 * span * panel * panel,
        2 * (panel * panel + 2 * span * panel),
    )(panel_inverse, own[0], *small)[0]
    pieces = [None] * cubes
    for d in range(0, cubes, 2):
        pieces[d] = mine if d == 0 else swap(mine, "cube", d)
    for d in range(0, cubes, 2):
        pieces[d + 1] = swap(pieces[d], "cube", 1)
    factor, panel_factor = call(
        functools.partial(factor_own_body, grids),
        [like((own_rows, panel), BF16), like((depth, own_rows), BF16)],
        [VMEM] * (3 * grids - 1),
        [],
        2 * own_rows * panel * panel,
        2 * (panel * panel + 2 * own_rows * panel),
    )(panel_inverse, *own, *small, *rest)
    schur_update = call(
        functools.partial(schur_body, cubes, grids, slots, width),
        [like((own_rows, width), BF16)],
        [SMEM] + [VMEM] * (1 + 2 * cubes),
        [pltpu.VMEM((own_rows, width), F32), pltpu.VMEM((width + rows, panel), BF16)],
        2 * own_rows * width * panel,
        2 * (own_rows * width + (own_rows + cubes * span) * panel),
    )(plan, factor, *got, *pieces)[0]
    return (schur_update, panel_factor)


def solution(mesh):
    placed = (
        P("cube", "grid"),
        P("grid", "cube"),
        P("grid", "cube"),
        P(),
        P(),
        P(),
        P("cube", None),
    )
    return jax.shard_map(
        local,
        mesh=mesh,
        in_specs=placed,
        out_specs=(P("cube", "grid"), P("grid", "cube")),
        check_vma=False,
    )
```

```python
import functools

import jax
import jax.numpy as jnp
from jax import lax
from jax.experimental import pallas as pl
from jax.experimental.pallas import tpu as pltpu
from jax.sharding import PartitionSpec as P

F32 = jnp.float32
BF16 = jnp.bfloat16
I32 = jnp.int32
VMEM = pl.BlockSpec(memory_space=pltpu.VMEM)
SMEM = pl.BlockSpec(memory_space=pltpu.SMEM)
ANY = pl.BlockSpec(memory_space=pl.ANY)
MIB = 1024 * 1024


def call(body, outs, in_specs, scratch, flops, moved, out_specs=None, limit=56):
    return pl.pallas_call(
        body,
        out_shape=outs,
        in_specs=in_specs,
        out_specs=[VMEM] * len(outs) if out_specs is None else out_specs,
        scratch_shapes=scratch,
        compiler_params=pltpu.CompilerParams(vmem_limit_bytes=limit * MIB),
        cost_estimate=pl.CostEstimate(flops=flops, bytes_accessed=moved, transcendentals=0),
    )


def rows_at(index, size):
    return pl.ds(pl.multiple_of(index * size, size), size)


def prepare_body(
    cubes, grids, span, owner_hbm, dest_hbm, rows_hbm, update_hbm, panel_hbm, entries_hbm, *refs
):
    firsts, rests = refs[:grids], refs[grids : 2 * grids]
    swap_ref, keep_ref = refs[2 * grids : 2 * grids + 2]
    owner_ref, dest_ref, rows_ref, update_ref, panel_ref, entries_ref, flipped, sems = refs[2 * grids + 2 :]
    copies = [
        pltpu.make_async_copy(source, target, sems.at[i])
        for i, (source, target) in enumerate(
            (
                (entries_hbm, entries_ref),
                (panel_hbm, panel_ref),
                (rows_hbm, rows_ref),
                (update_hbm, update_ref),
                (owner_hbm, owner_ref),
                (dest_hbm, dest_ref),
            )
        )
    ]
    for copy in copies:
        copy.start()
    mine = lax.axis_index("cube")
    column = lax.axis_index("grid")
    children, rows = rows_ref.shape
    swap_ref[...] = jnp.zeros_like(swap_ref)
    keep_ref[...] = jnp.zeros_like(keep_ref)
    copies[0].wait()
    flipped[...] = entries_ref[...].astype(F32).T.astype(BF16)
    for d in range(grids):
        piece = flipped[rows_at(jnp.bitwise_xor(column, d), span), :]
        firsts[d][pl.ds(0, span), :] = piece
        for e in range(grids):
            if e != d:
                k = d if d < e else d - 1
                rests[e][pl.ds(k * span, span), :] = piece
    for copy in copies[1:]:
        copy.wait()
    for k in range(children):
        want = rows_ref[k : k + 1, :]
        put = (lax.broadcasted_iota(I32, (rows, rows), 0) == want).astype(BF16)
        part = pl.ds(k * rows, rows)
        placed = jnp.dot(put, panel_ref[part, :], preferred_element_type=F32).astype(BF16)
        for d in range(grids):
            firsts[d][pl.ds(span + k * rows, rows), :] = placed
        moved = jnp.dot(put, update_ref[part, :], preferred_element_type=F32).astype(BF16)
        d = jnp.bitwise_xor(owner_ref[dest_ref[mine * children + k]], mine)
        chip = jnp.right_shift(d, 1)
        same = jnp.bitwise_and(d, 1) == 0

        @pl.when(same)
        def _():
            keep_ref[rows_at(chip, rows), :] = moved

        @pl.when(jnp.logical_not(same))
        def _():
            swap_ref[rows_at(chip, rows), :] = moved


def pack_body(grids, rows, base, keep_ref, other_ref, *refs):
    firsts, mine_ref, payloads = refs[:grids], refs[grids], refs[grids + 1 :]
    depth = firsts[0].shape[1]
    panel = mine_ref.shape[1]
    chunks = keep_ref.shape[1] // panel
    for d in range(grids):
        lanes = pl.ds(d * depth, depth)
        piece = firsts[d][...]
        mine_ref[:, lanes] = piece
        for payload in payloads:
            payload[pl.ds(0, base), lanes] = piece
    for i, payload in enumerate(payloads):
        part = pl.ds((i + 1) * rows, rows)
        for half, blocks in enumerate((keep_ref, other_ref)):
            for j in range(chunks):
                at = base + (half * chunks + j) * rows
                payload[pl.ds(at, rows), :] = blocks[part, pl.ds(j * panel, panel)]


def plan_body(cubes, grids, slots, owner_ref, dest_ref, after_ref, out_ref, slot_ref, count_ref):
    mine = lax.axis_index("cube")
    column = lax.axis_index("grid")
    blocks = owner_ref.shape[0]
    in_range = blocks // grids
    children = dest_ref.shape[0] // cubes
    none = grids * slots
    places = 2 * cubes + grids
    child_places = places + cubes * slots
    for r in range(grids):

        def count_own(i, seen):
            b = r * in_range + i
            own = owner_ref[b] == mine
            slot_ref[b] = jnp.where(own, r * slots + seen, none)
            return seen + own.astype(I32)

        out_ref[2 * cubes + r] = lax.fori_loop(0, in_range, count_own, I32(0))
    for d in range(cubes):
        source = jnp.bitwise_xor(mine, d)
        slot, which = I32(none), I32(0)
        for k in range(children):
            b = dest_ref[source * children + k]
            here = slot_ref[b]
            which = jnp.where(here < none, k, which)
            slot = jnp.minimum(slot, here)
            local_b = b - column * in_range
            inside = jnp.logical_and(local_b >= 0, local_b < in_range)
            out_ref[child_places + d * children + k] = jnp.where(inside, local_b, in_range)
        out_ref[d] = slot
        out_ref[cubes + d] = which
        count_ref[d] = 0
        for k in range(slots):
            out_ref[places + d * slots + k] = in_range

    def place(i, carry):
        d = jnp.bitwise_xor(owner_ref[column * in_range + i], mine)
        k = count_ref[d]
        out_ref[places + d * slots + k] = i
        count_ref[d] = k + 1
        return carry

    lax.fori_loop(0, in_range, place, 0)


def own_body(cubes, grids, span, rows, plan_ref, inverse_ref, mine_ref, *refs):
    rests = refs[:grids]
    entries_ref, factor_ref, turned_ref = refs[grids:]
    column = lax.axis_index("grid")
    depth = rests[0].shape[1]
    for d in range(grids):
        turned_ref[pl.ds(d * depth, depth), :] = inverse_ref[rows_at(jnp.bitwise_xor(column, d), depth), :]
    for e in range(grids):
        r = jnp.bitwise_xor(column, e)
        ids = lax.broadcasted_iota(I32, (span, depth), 0)
        live = ids < plan_ref[2 * cubes + r] * rows
        for d in range(grids):
            if e == 0:
                piece = mine_ref[pl.ds(0, span), pl.ds(d * depth, depth)]
            else:
                k = d ^ e
                piece = rests[d][pl.ds((k if k < d else k - 1) * span, span), :]
            piece = jnp.where(live, piece.astype(F32), 0.0).astype(BF16)
            entries_ref[rows_at(r, span), pl.ds(d * depth, depth)] = piece
    factor_ref[...] = jnp.dot(entries_ref[...], turned_ref[...], preferred_element_type=F32).astype(BF16)


def schur_body(
    cubes, grids, slots, rows, children, plan_ref, turned_ref, entries_ref, before_ref, keep_ref, other_ref, *refs
):
    pieces = refs[:cubes]
    out_ref, panel_ref, ranged, touched, few, factor_ref, total = refs[cubes:]
    column = lax.axis_index("grid")
    span = slots * rows
    base = span + children * rows
    own_rows, panel = entries_ref.shape
    width = out_ref.shape[1]
    chunks = width // panel
    depth = panel_ref.shape[0]
    places = 2 * cubes + grids
    child_places = places + cubes * slots
    none = own_rows // rows
    total[...] = jnp.zeros_like(total)
    for d in range(cubes):
        at = rows_at(plan_ref[d], rows)
        if d < 2:
            total[at, :] += (keep_ref, other_ref)[d][pl.ds(0, rows), :].astype(F32)
        else:
            for j in range(chunks):
                part = pl.ds(base + ((d & 1) * chunks + j) * rows, rows)
                total[at, pl.ds(j * panel, panel)] += pieces[d & ~1][part, :].astype(F32)
    for d in range(cubes):
        slot = plan_ref[d]
        touched[rows_at(slot, rows), :] = entries_ref[rows_at(jnp.minimum(slot, none - 1), rows), :].astype(F32)
    for d in range(cubes):
        child = pieces[d][rows_at(slots + plan_ref[cubes + d], rows), :]
        touched[rows_at(plan_ref[d], rows), :] += child.astype(F32)
    for d in range(cubes):
        few[pl.ds(d * rows, rows), :] = touched[rows_at(plan_ref[d], rows), :].astype(BF16)
    redone = jnp.dot(few[...], turned_ref[...], preferred_element_type=F32).astype(BF16)
    factor_ref[pl.ds(0, own_rows), :] = before_ref[...]
    for d in range(cubes):
        factor_ref[rows_at(plan_ref[d], rows), :] = redone[d * rows : (d + 1) * rows, :]
    factor = factor_ref[pl.ds(0, own_rows), :]
    for d in range(cubes):
        for k in range(slots):
            at = rows_at(plan_ref[places + d * slots + k], rows)
            ranged[at, :] = pieces[d][pl.ds(k * rows, rows), :].astype(F32)
    for d in range(cubes):
        for k in range(children):
            at = rows_at(plan_ref[child_places + d * children + k], rows)
            ranged[at, :] += pieces[d][pl.ds(span + k * rows, rows), :].astype(F32)
    column_factor = jnp.dot(
        ranged[pl.ds(0, width), :].astype(BF16), turned_ref[...], preferred_element_type=F32
    ).astype(BF16)
    product = lax.dot_general(factor, column_factor, (((1,), (1,)), ((), ())), preferred_element_type=F32)
    out_ref[...] = (total[pl.ds(0, own_rows), :] - product).astype(BF16)
    if depth % 128 == 0:
        cols = pl.ds(pl.multiple_of(column * depth, depth), depth)
        panel_ref[...] = factor_ref[pl.ds(0, own_rows), cols].astype(F32).T.astype(BF16)
    else:
        for r in range(grids):

            @pl.when(column == r)
            def _():
                part = factor_ref[pl.ds(0, own_rows), pl.ds(r * depth, depth)]
                panel_ref[...] = part.astype(F32).T.astype(BF16)


def local(
    child_update, child_panel, panel_entries, panel_inverse, block_owner, child_dest, child_rows
):
    cubes = lax.axis_size("cube")
    grids = lax.axis_size("grid")
    chips = cubes // 2
    children, rows = child_rows.shape
    width = child_update.shape[1]
    depth = child_panel.shape[0]
    panel = panel_inverse.shape[0]
    own_rows = panel_entries.shape[1]
    slots = own_rows // rows // grids
    span = slots * rows
    base = span + children * rows
    sent = base + 2 * rows * (width // panel)
    like = jax.ShapeDtypeStruct

    def swap(x, axis, d):
        n = lax.axis_size(axis)
        return lax.ppermute(x, axis, [(i, i ^ d) for i in range(n)])

    prepared = call(
        functools.partial(prepare_body, cubes, grids, span),
        [like((base, depth), BF16)] * grids
        + [like(((grids - 1) * span, depth), BF16)] * grids
        + [like((chips * rows, width), BF16)] * 2,
        [ANY] * 6,
        [
            pltpu.SMEM(block_owner.shape, I32),
            pltpu.SMEM(child_dest.shape, I32),
            pltpu.VMEM(child_rows.shape, I32),
            pltpu.VMEM(child_update.shape, BF16),
            pltpu.VMEM(child_panel.shape[::-1], BF16),
            pltpu.VMEM(panel_entries.shape, BF16),
            pltpu.VMEM(panel_entries.shape[::-1], BF16),
            pltpu.SemaphoreType.DMA((6,)),
        ],
        2 * rows * rows * children * (width + depth),
        4 * own_rows * depth,
    )(block_owner, child_dest, child_rows, child_update, child_panel.T, panel_entries)
    firsts, rests = prepared[:grids], prepared[grids : 2 * grids]
    to_other, keep = prepared[2 * grids :]
    other = swap(to_other, "cube", 1)
    firsts = [firsts[0]] + [swap(firsts[d], "grid", d) for d in range(1, grids)]
    rests = [rests[0]] + [swap(rests[d], "grid", d) for d in range(1, grids)]
    packed = call(
        functools.partial(pack_body, grids, rows, base),
        [like((base, panel), BF16)] + [like((sent, panel), BF16)] * (chips - 1),
        [VMEM] * (2 + grids),
        [],
        1000,
        2 * chips * sent * panel,
    )(keep, other, *firsts)
    mine = packed[0]
    pieces = []
    for i in range(chips):
        piece = mine if i == 0 else swap(packed[i], "cube", 2 * i)
        pieces += [piece, swap(piece, "cube", 1)]
    plan = call(
        functools.partial(plan_body, cubes, grids, slots),
        [like((2 * cubes + grids + cubes * (slots + children),), I32)],
        [SMEM, SMEM, ANY],
        [pltpu.SMEM(block_owner.shape, I32), pltpu.SMEM((cubes,), I32)],
        100000,
        4096,
        [SMEM],
    )(block_owner, child_dest, mine)[0]
    entries, before, turned = call(
        functools.partial(own_body, cubes, grids, span, rows),
        [like((own_rows, panel), BF16), like((own_rows, panel), BF16), like((panel, panel), BF16)],
        [SMEM] + [VMEM] * (2 + grids),
        [],
        2 * own_rows * panel * panel,
        2 * (panel * panel + 2 * own_rows * panel),
    )(plan, panel_inverse, mine, *rests)
    return tuple(
        call(
            functools.partial(schur_body, cubes, grids, slots, rows, children),
            [like((own_rows, width), BF16), like((depth, own_rows), BF16)],
            [SMEM] + [VMEM] * (5 + cubes),
            [
                pltpu.VMEM((width + rows, panel), F32),
                pltpu.VMEM((own_rows + rows, panel), F32),
                pltpu.VMEM((cubes * rows, panel), BF16),
                pltpu.VMEM((own_rows + rows, panel), BF16),
                pltpu.VMEM((own_rows + rows, width), F32),
            ],
            2 * own_rows * width * panel,
            2 * (own_rows * width + (own_rows + cubes * span) * panel),
        )(plan, turned, entries, before, keep, other, *pieces)
    )


def solution(mesh):
    placed = (
        P("cube", "grid"),
        P("grid", "cube"),
        P("grid", "cube"),
        P(),
        P(),
        P(),
        P("cube", None),
    )
    return jax.shard_map(
        local,
        mesh=mesh,
        in_specs=placed,
        out_specs=(P("cube", "grid"), P("grid", "cube")),
        check_vma=False,
    )
```

```python
import functools

import jax
import jax.numpy as jnp
from jax import lax
from jax.experimental import pallas as pl
from jax.experimental.pallas import tpu as pltpu
from jax.sharding import PartitionSpec as P

F32 = jnp.float32
BF16 = jnp.bfloat16
I32 = jnp.int32
VMEM = pl.BlockSpec(memory_space=pltpu.VMEM)
SMEM = pl.BlockSpec(memory_space=pltpu.SMEM)
ANY = pl.BlockSpec(memory_space=pl.ANY)
HBM = pl.BlockSpec(memory_space=pltpu.HBM)
MIB = 1024 * 1024


def call(body, outs, in_specs, scratch, flops, moved, out_specs=None, limit=16):
    return pl.pallas_call(
        body,
        out_shape=outs,
        in_specs=in_specs,
        out_specs=[VMEM] * len(outs) if out_specs is None else out_specs,
        scratch_shapes=scratch,
        compiler_params=pltpu.CompilerParams(vmem_limit_bytes=limit * MIB),
        cost_estimate=pl.CostEstimate(flops=flops, bytes_accessed=moved, transcendentals=0),
    )


def rows_at(index, size):
    return pl.ds(pl.multiple_of(index * size, size), size)


def prepare_body(
    cubes, grids, span, owner_hbm, dest_hbm, rows_hbm, update_hbm, panel_hbm, entries_hbm, *refs
):
    firsts, rests = refs[:grids], refs[grids : 2 * grids]
    swap_ref, keep_ref = refs[2 * grids : 2 * grids + 2]
    owner_ref, dest_ref, rows_ref, update_ref, panel_ref, entries_ref, flipped, sems = refs[2 * grids + 2 :]
    copies = [
        pltpu.make_async_copy(source, target, sems.at[i])
        for i, (source, target) in enumerate(
            (
                (entries_hbm, entries_ref),
                (panel_hbm, panel_ref),
                (rows_hbm, rows_ref),
                (update_hbm, update_ref),
                (owner_hbm, owner_ref),
                (dest_hbm, dest_ref),
            )
        )
    ]
    for copy in copies:
        copy.start()
    mine = lax.axis_index("cube")
    column = lax.axis_index("grid")
    children, rows = rows_ref.shape
    swap_ref[...] = jnp.zeros_like(swap_ref)
    keep_ref[...] = jnp.zeros_like(keep_ref)
    copies[0].wait()
    flipped[...] = entries_ref[...].astype(F32).T.astype(BF16)
    for d in range(grids):
        piece = flipped[rows_at(jnp.bitwise_xor(column, d), span), :]
        firsts[d][pl.ds(0, span), :] = piece
        for e in range(grids):
            if e != d:
                k = d if d < e else d - 1
                rests[e][pl.ds(k * span, span), :] = piece
    for copy in copies[1:]:
        copy.wait()
    for k in range(children):
        want = rows_ref[k : k + 1, :]
        put = (lax.broadcasted_iota(I32, (rows, rows), 0) == want).astype(BF16)
        part = pl.ds(k * rows, rows)
        placed = jnp.dot(put, panel_ref[part, :], preferred_element_type=F32).astype(BF16)
        for d in range(grids):
            firsts[d][pl.ds(span + k * rows, rows), :] = placed
        moved = jnp.dot(put, update_ref[part, :], preferred_element_type=F32).astype(BF16)
        d = jnp.bitwise_xor(owner_ref[dest_ref[mine * children + k]], mine)
        chip = jnp.right_shift(d, 1)
        same = jnp.bitwise_and(d, 1) == 0

        @pl.when(same)
        def _():
            keep_ref[rows_at(chip, rows), :] = moved

        @pl.when(jnp.logical_not(same))
        def _():
            swap_ref[rows_at(chip, rows), :] = moved


def pack_body(grids, rows, base, keep_ref, other_ref, *refs):
    firsts, mine_ref, payloads = refs[:grids], refs[grids], refs[grids + 1 :]
    depth = firsts[0].shape[1]
    panel = mine_ref.shape[1]
    chunks = keep_ref.shape[1] // panel
    for d in range(grids):
        lanes = pl.ds(d * depth, depth)
        piece = firsts[d][...]
        mine_ref[:, lanes] = piece
        for payload in payloads:
            payload[pl.ds(0, base), lanes] = piece
    for i, payload in enumerate(payloads):
        part = pl.ds((i + 1) * rows, rows)
        for half, blocks in enumerate((keep_ref, other_ref)):
            for j in range(chunks):
                at = base + (half * chunks + j) * rows
                payload[pl.ds(at, rows), :] = blocks[part, pl.ds(j * panel, panel)]


def plan_body(cubes, grids, slots, owner_ref, dest_ref, after_ref, out_ref, slot_ref, count_ref):
    mine = lax.axis_index("cube")
    column = lax.axis_index("grid")
    blocks = owner_ref.shape[0]
    in_range = blocks // grids
    children = dest_ref.shape[0] // cubes
    none = grids * slots
    places = 2 * cubes + grids
    child_places = places + cubes * slots
    for r in range(grids):

        def count_own(i, seen):
            b = r * in_range + i
            own = owner_ref[b] == mine
            slot_ref[b] = jnp.where(own, r * slots + seen, none)
            return seen + own.astype(I32)

        out_ref[2 * cubes + r] = lax.fori_loop(0, in_range, count_own, I32(0))
    for d in range(cubes):
        source = jnp.bitwise_xor(mine, d)
        slot, which = I32(none), I32(0)
        for k in range(children):
            b = dest_ref[source * children + k]
            here = slot_ref[b]
            which = jnp.where(here < none, k, which)
            slot = jnp.minimum(slot, here)
            local_b = b - column * in_range
            inside = jnp.logical_and(local_b >= 0, local_b < in_range)
            out_ref[child_places + d * children + k] = jnp.where(inside, local_b, in_range)
        out_ref[d] = slot
        out_ref[cubes + d] = which
        count_ref[d] = 0
        for k in range(slots):
            out_ref[places + d * slots + k] = in_range

    def place(i, carry):
        d = jnp.bitwise_xor(owner_ref[column * in_range + i], mine)
        k = count_ref[d]
        out_ref[places + d * slots + k] = i
        count_ref[d] = k + 1
        return carry

    lax.fori_loop(0, in_range, place, 0)


def own_body(cubes, grids, span, rows, plan_ref, inverse_ref, mine_ref, *refs):
    rests = refs[:grids]
    entries_ref, factor_ref, turned_ref = refs[grids:]
    column = lax.axis_index("grid")
    depth = rests[0].shape[1]
    for d in range(grids):
        turned_ref[pl.ds(d * depth, depth), :] = inverse_ref[rows_at(jnp.bitwise_xor(column, d), depth), :]
    for e in range(grids):
        r = jnp.bitwise_xor(column, e)
        ids = lax.broadcasted_iota(I32, (span, depth), 0)
        live = ids < plan_ref[2 * cubes + r] * rows
        for d in range(grids):
            if e == 0:
                piece = mine_ref[pl.ds(0, span), pl.ds(d * depth, depth)]
            else:
                k = d ^ e
                piece = rests[d][pl.ds((k if k < d else k - 1) * span, span), :]
            piece = jnp.where(live, piece.astype(F32), 0.0).astype(BF16)
            entries_ref[rows_at(r, span), pl.ds(d * depth, depth)] = piece
    factor_ref[...] = jnp.dot(entries_ref[...], turned_ref[...], preferred_element_type=F32).astype(BF16)


def schur_body(
    cubes, grids, slots, rows, children, plan_ref, turned_ref, entries_ref, before_ref, keep_ref, other_ref, *refs
):
    pieces = refs[:cubes]
    out_ref, panel_ref, ranged, touched, few, factor_ref, total = refs[cubes:]
    column = lax.axis_index("grid")
    span = slots * rows
    base = span + children * rows
    own_rows, panel = entries_ref.shape
    width = out_ref.shape[1]
    chunks = width // panel
    depth = panel_ref.shape[0]
    places = 2 * cubes + grids
    child_places = places + cubes * slots
    none = own_rows // rows
    total[...] = jnp.zeros_like(total)
    for d in range(cubes):
        at = rows_at(plan_ref[d], rows)
        if d < 2:
            total[at, :] += (keep_ref, other_ref)[d][pl.ds(0, rows), :].astype(F32)
        else:
            for j in range(chunks):
                part = pl.ds(base + ((d & 1) * chunks + j) * rows, rows)
                total[at, pl.ds(j * panel, panel)] += pieces[d & ~1][part, :].astype(F32)
    for d in range(cubes):
        slot = plan_ref[d]
        touched[rows_at(slot, rows), :] = entries_ref[rows_at(jnp.minimum(slot, none - 1), rows), :].astype(F32)
    for d in range(cubes):
        child = pieces[d][rows_at(slots + plan_ref[cubes + d], rows), :]
        touched[rows_at(plan_ref[d], rows), :] += child.astype(F32)
    for d in range(cubes):
        few[pl.ds(d * rows, rows), :] = touched[rows_at(plan_ref[d], rows), :].astype(BF16)
    redone = jnp.dot(few[...], turned_ref[...], preferred_element_type=F32).astype(BF16)
    factor_ref[pl.ds(0, own_rows), :] = before_ref[...]
    for d in range(cubes):
        factor_ref[rows_at(plan_ref[d], rows), :] = redone[d * rows : (d + 1) * rows, :]
    factor = factor_ref[pl.ds(0, own_rows), :]
    for d in range(cubes):
        for k in range(slots):
            at = rows_at(plan_ref[places + d * slots + k], rows)
            ranged[at, :] = pieces[d][pl.ds(k * rows, rows), :].astype(F32)
    for d in range(cubes):
        for k in range(children):
            at = rows_at(plan_ref[child_places + d * children + k], rows)
            ranged[at, :] += pieces[d][pl.ds(span + k * rows, rows), :].astype(F32)
    column_factor = jnp.dot(
        ranged[pl.ds(0, width), :].astype(BF16), turned_ref[...], preferred_element_type=F32
    ).astype(BF16)
    product = lax.dot_general(factor, column_factor, (((1,), (1,)), ((), ())), preferred_element_type=F32)
    out_ref[...] = (total[pl.ds(0, own_rows), :] - product).astype(BF16)
    if depth % 128 == 0:
        cols = pl.ds(pl.multiple_of(column * depth, depth), depth)
        panel_ref[...] = factor_ref[pl.ds(0, own_rows), cols].astype(F32).T.astype(BF16)
    else:
        for r in range(grids):

            @pl.when(column == r)
            def _():
                part = factor_ref[pl.ds(0, own_rows), pl.ds(r * depth, depth)]
                panel_ref[...] = part.astype(F32).T.astype(BF16)


def local(
    child_update, child_panel, panel_entries, panel_inverse, block_owner, child_dest, child_rows
):
    cubes = lax.axis_size("cube")
    grids = lax.axis_size("grid")
    chips = cubes // 2
    children, rows = child_rows.shape
    width = child_update.shape[1]
    depth = child_panel.shape[0]
    panel = panel_inverse.shape[0]
    own_rows = panel_entries.shape[1]
    slots = own_rows // rows // grids
    span = slots * rows
    base = span + children * rows
    sent = base + 2 * rows * (width // panel)
    like = jax.ShapeDtypeStruct

    def swap(x, axis, d):
        n = lax.axis_size(axis)
        return lax.ppermute(x, axis, [(i, i ^ d) for i in range(n)])

    prepared = call(
        functools.partial(prepare_body, cubes, grids, span),
        [like((base, depth), BF16)] * grids
        + [like(((grids - 1) * span, depth), BF16)] * grids
        + [like((chips * rows, width), BF16)] * 2,
        [HBM] * 6,
        [
            pltpu.SMEM(block_owner.shape, I32),
            pltpu.SMEM(child_dest.shape, I32),
            pltpu.VMEM(child_rows.shape, I32),
            pltpu.VMEM(child_update.shape, BF16),
            pltpu.VMEM(child_panel.shape[::-1], BF16),
            pltpu.VMEM(panel_entries.shape, BF16),
            pltpu.VMEM(panel_entries.shape[::-1], BF16),
            pltpu.SemaphoreType.DMA((6,)),
        ],
        2 * rows * rows * children * (width + depth),
        4 * own_rows * depth,
        limit=61,
    )(block_owner, child_dest, child_rows, child_update, child_panel.T, panel_entries)
    firsts, rests = prepared[:grids], prepared[grids : 2 * grids]
    to_other, keep = prepared[2 * grids :]
    other = swap(to_other, "cube", 1)
    firsts = [firsts[0]] + [swap(firsts[d], "grid", d) for d in range(1, grids)]
    rests = [rests[0]] + [swap(rests[d], "grid", d) for d in range(1, grids)]
    packed = call(
        functools.partial(pack_body, grids, rows, base),
        [like((base, panel), BF16)] + [like((sent, panel), BF16)] * (chips - 1),
        [VMEM] * (2 + grids),
        [],
        1000,
        2 * chips * sent * panel,
    )(keep, other, *firsts)
    mine = packed[0]
    pieces = []
    for i in range(chips):
        piece = mine if i == 0 else swap(packed[i], "cube", 2 * i)
        pieces += [piece, swap(piece, "cube", 1)]
    plan = call(
        functools.partial(plan_body, cubes, grids, slots),
        [like((2 * cubes + grids + cubes * (slots + children),), I32)],
        [SMEM, SMEM, ANY],
        [pltpu.SMEM(block_owner.shape, I32), pltpu.SMEM((cubes,), I32)],
        100000,
        4096,
        [SMEM],
    )(block_owner, child_dest, mine)[0]
    entries, before, turned = call(
        functools.partial(own_body, cubes, grids, span, rows),
        [like((own_rows, panel), BF16), like((own_rows, panel), BF16), like((panel, panel), BF16)],
        [SMEM] + [VMEM] * (2 + grids),
        [],
        2 * own_rows * panel * panel,
        2 * (panel * panel + 2 * own_rows * panel),
    )(plan, panel_inverse, mine, *rests)
    return tuple(
        call(
            functools.partial(schur_body, cubes, grids, slots, rows, children),
            [like((own_rows, width), BF16), like((depth, own_rows), BF16)],
            [SMEM] + [VMEM] * (5 + cubes),
            [
                pltpu.VMEM((width + rows, panel), F32),
                pltpu.VMEM((own_rows + rows, panel), F32),
                pltpu.VMEM((cubes * rows, panel), BF16),
                pltpu.VMEM((own_rows + rows, panel), BF16),
                pltpu.VMEM((own_rows + rows, width), F32),
            ],
            2 * own_rows * width * panel,
            2 * (own_rows * width + (own_rows + cubes * span) * panel),
            limit=16 if own_rows * width <= 512 * 512 else 56,
        )(plan, turned, entries, before, keep, other, *pieces)
    )


def solution(mesh):
    placed = (
        P("cube", "grid"),
        P("grid", "cube"),
        P("grid", "cube"),
        P(),
        P(),
        P(),
        P("cube", None),
    )
    return jax.shard_map(
        local,
        mesh=mesh,
        in_specs=placed,
        out_specs=(P("cube", "grid"), P("grid", "cube")),
        check_vma=False,
    )
```

```python
import functools

import jax
import jax.numpy as jnp
from jax import lax
from jax.experimental import pallas as pl
from jax.experimental.pallas import tpu as pltpu
from jax.sharding import PartitionSpec as P

F32 = jnp.float32
BF16 = jnp.bfloat16
I32 = jnp.int32
VMEM = pl.BlockSpec(memory_space=pltpu.VMEM)
SMEM = pl.BlockSpec(memory_space=pltpu.SMEM)
ANY = pl.BlockSpec(memory_space=pl.ANY)
MIB = 1024 * 1024


def call(body, outs, in_specs, scratch, flops, moved, out_specs=None, limit=16):
    return pl.pallas_call(
        body,
        out_shape=outs,
        in_specs=in_specs,
        out_specs=[VMEM] * len(outs) if out_specs is None else out_specs,
        scratch_shapes=scratch,
        compiler_params=pltpu.CompilerParams(vmem_limit_bytes=limit * MIB),
        cost_estimate=pl.CostEstimate(flops=flops, bytes_accessed=moved, transcendentals=0),
    )


def rows_at(index, size):
    return pl.ds(pl.multiple_of(index * size, size), size)


def prepare_body(
    cubes, grids, span, owner_hbm, dest_hbm, rows_hbm, update_hbm, panel_hbm, entries_hbm, *refs
):
    firsts = refs[:grids]
    rest_ref, swap_ref, keep_ref = refs[grids : grids + 3]
    owner_ref, dest_ref, rows_ref, update_ref, panel_ref, entries_ref, flipped, sems = refs[grids + 3 :]
    copies = [
        pltpu.make_async_copy(source, target, sems.at[i])
        for i, (source, target) in enumerate(
            (
                (entries_hbm, entries_ref),
                (panel_hbm, panel_ref),
                (rows_hbm, rows_ref),
                (update_hbm, update_ref),
                (owner_hbm, owner_ref),
                (dest_hbm, dest_ref),
            )
        )
    ]
    for copy in copies:
        copy.start()
    mine = lax.axis_index("cube")
    column = lax.axis_index("grid")
    children, rows = rows_ref.shape
    swap_ref[...] = jnp.zeros_like(swap_ref)
    keep_ref[...] = jnp.zeros_like(keep_ref)
    copies[0].wait()
    flipped[...] = entries_ref[...].astype(F32).T.astype(BF16)
    for d in range(grids):
        piece = flipped[rows_at(jnp.bitwise_xor(column, d), span), :]
        firsts[d][pl.ds(0, span), :] = piece
        for e in range(grids):
            if e != d:
                k = d if d < e else d - 1
                rest_ref[jnp.bitwise_xor(column, e), pl.ds(k * span, span), :] = piece
    for copy in copies[1:]:
        copy.wait()
    for k in range(children):
        want = rows_ref[k : k + 1, :]
        put = (lax.broadcasted_iota(I32, (rows, rows), 0) == want).astype(BF16)
        part = pl.ds(k * rows, rows)
        placed = jnp.dot(put, panel_ref[part, :], preferred_element_type=F32).astype(BF16)
        for d in range(grids):
            firsts[d][pl.ds(span + k * rows, rows), :] = placed
        moved = jnp.dot(put, update_ref[part, :], preferred_element_type=F32).astype(BF16)
        d = jnp.bitwise_xor(owner_ref[dest_ref[mine * children + k]], mine)
        chip = jnp.right_shift(d, 1)
        same = jnp.bitwise_and(d, 1) == 0

        @pl.when(same)
        def _():
            keep_ref[rows_at(chip, rows), :] = moved

        @pl.when(jnp.logical_not(same))
        def _():
            swap_ref[rows_at(chip, rows), :] = moved


def pack_body(grids, rows, base, keep_ref, other_ref, *refs):
    firsts, mine_ref, payloads = refs[:grids], refs[grids], refs[grids + 1 :]
    depth = firsts[0].shape[1]
    panel = mine_ref.shape[1]
    chunks = keep_ref.shape[1] // panel
    for d in range(grids):
        lanes = pl.ds(d * depth, depth)
        piece = firsts[d][...]
        mine_ref[:, lanes] = piece
        for payload in payloads:
            payload[pl.ds(0, base), lanes] = piece
    for i, payload in enumerate(payloads):
        part = pl.ds((i + 1) * rows, rows)
        for half, blocks in enumerate((keep_ref, other_ref)):
            for j in range(chunks):
                at = base + (half * chunks + j) * rows
                payload[pl.ds(at, rows), :] = blocks[part, pl.ds(j * panel, panel)]


def plan_body(cubes, grids, slots, owner_ref, dest_ref, after_ref, out_ref, slot_ref, count_ref):
    mine = lax.axis_index("cube")
    column = lax.axis_index("grid")
    blocks = owner_ref.shape[0]
    in_range = blocks // grids
    children = dest_ref.shape[0] // cubes
    none = grids * slots
    places = 2 * cubes + grids
    child_places = places + cubes * slots
    for r in range(grids):

        def count_own(i, seen):
            b = r * in_range + i
            own = owner_ref[b] == mine
            slot_ref[b] = jnp.where(own, r * slots + seen, none)
            return seen + own.astype(I32)

        out_ref[2 * cubes + r] = lax.fori_loop(0, in_range, count_own, I32(0), unroll=8)
    for d in range(cubes):
        source = jnp.bitwise_xor(mine, d)
        slot, which = I32(none), I32(0)
        for k in range(children):
            b = dest_ref[source * children + k]
            here = slot_ref[b]
            which = jnp.where(here < none, k, which)
            slot = jnp.minimum(slot, here)
            local_b = b - column * in_range
            inside = jnp.logical_and(local_b >= 0, local_b < in_range)
            out_ref[child_places + d * children + k] = jnp.where(inside, local_b, in_range)
        out_ref[d] = slot
        out_ref[cubes + d] = which
        count_ref[d] = 0
        for k in range(slots):
            out_ref[places + d * slots + k] = in_range

    def place(i, carry):
        d = jnp.bitwise_xor(owner_ref[column * in_range + i], mine)
        k = count_ref[d]
        out_ref[places + d * slots + k] = i
        count_ref[d] = k + 1
        return carry

    lax.fori_loop(0, in_range, place, 0, unroll=8)


def own_body(cubes, grids, span, rows, plan_ref, inverse_ref, mine_ref, rest_ref, entries_ref, factor_ref, turned_ref):
    column = lax.axis_index("grid")
    depth = rest_ref.shape[2]
    for d in range(grids):
        turned_ref[pl.ds(d * depth, depth), :] = inverse_ref[rows_at(jnp.bitwise_xor(column, d), depth), :]
    for e in range(grids):
        r = jnp.bitwise_xor(column, e)
        ids = lax.broadcasted_iota(I32, (span, depth), 0)
        live = ids < plan_ref[2 * cubes + r] * rows
        for d in range(grids):
            if e == 0:
                piece = mine_ref[pl.ds(0, span), pl.ds(d * depth, depth)]
            else:
                k = d ^ e
                piece = rest_ref[jnp.bitwise_xor(column, d), pl.ds((k if k < d else k - 1) * span, span), :]
            piece = jnp.where(live, piece.astype(F32), 0.0).astype(BF16)
            entries_ref[rows_at(r, span), pl.ds(d * depth, depth)] = piece
    factor_ref[...] = jnp.dot(entries_ref[...], turned_ref[...], preferred_element_type=F32).astype(BF16)


def schur_body(
    cubes, grids, slots, rows, children, plan_ref, turned_ref, entries_ref, before_ref, keep_ref, other_ref, *refs
):
    pieces = refs[:cubes]
    out_ref, panel_ref, ranged, touched, few, factor_ref, total = refs[cubes:]
    column = lax.axis_index("grid")
    span = slots * rows
    base = span + children * rows
    own_rows, panel = entries_ref.shape
    width = out_ref.shape[1]
    chunks = width // panel
    depth = panel_ref.shape[0]
    places = 2 * cubes + grids
    child_places = places + cubes * slots
    none = own_rows // rows
    total[...] = jnp.zeros_like(total)
    for d in range(cubes):
        at = rows_at(plan_ref[d], rows)
        if d < 2:
            total[at, :] += (keep_ref, other_ref)[d][pl.ds(0, rows), :].astype(F32)
        else:
            for j in range(chunks):
                part = pl.ds(base + ((d & 1) * chunks + j) * rows, rows)
                total[at, pl.ds(j * panel, panel)] += pieces[d & ~1][part, :].astype(F32)
    for d in range(cubes):
        slot = plan_ref[d]
        touched[rows_at(slot, rows), :] = entries_ref[rows_at(jnp.minimum(slot, none - 1), rows), :].astype(F32)
    for d in range(cubes):
        child = pieces[d][rows_at(slots + plan_ref[cubes + d], rows), :]
        touched[rows_at(plan_ref[d], rows), :] += child.astype(F32)
    for d in range(cubes):
        few[pl.ds(d * rows, rows), :] = touched[rows_at(plan_ref[d], rows), :].astype(BF16)
    redone = jnp.dot(few[...], turned_ref[...], preferred_element_type=F32).astype(BF16)
    factor_ref[pl.ds(0, own_rows), :] = before_ref[...]
    for d in range(cubes):
        factor_ref[rows_at(plan_ref[d], rows), :] = redone[d * rows : (d + 1) * rows, :]
    factor = factor_ref[pl.ds(0, own_rows), :]
    for d in range(cubes):
        for k in range(slots):
            at = rows_at(plan_ref[places + d * slots + k], rows)
            ranged[at, :] = pieces[d][pl.ds(k * rows, rows), :].astype(F32)
    for d in range(cubes):
        for k in range(children):
            at = rows_at(plan_ref[child_places + d * children + k], rows)
            ranged[at, :] += pieces[d][pl.ds(span + k * rows, rows), :].astype(F32)
    column_factor = jnp.dot(
        ranged[pl.ds(0, width), :].astype(BF16), turned_ref[...], preferred_element_type=F32
    ).astype(BF16)
    product = lax.dot_general(factor, column_factor, (((1,), (1,)), ((), ())), preferred_element_type=F32)
    out_ref[...] = (total[pl.ds(0, own_rows), :] - product).astype(BF16)
    if depth % 128 == 0:
        cols = pl.ds(pl.multiple_of(column * depth, depth), depth)
        panel_ref[...] = factor_ref[pl.ds(0, own_rows), cols].astype(F32).T.astype(BF16)
    else:
        for r in range(grids):

            @pl.when(column == r)
            def _():
                part = factor_ref[pl.ds(0, own_rows), pl.ds(r * depth, depth)]
                panel_ref[...] = part.astype(F32).T.astype(BF16)


def local(
    child_update, child_panel, panel_entries, panel_inverse, block_owner, child_dest, child_rows
):
    cubes = lax.axis_size("cube")
    grids = lax.axis_size("grid")
    chips = cubes // 2
    children, rows = child_rows.shape
    width = child_update.shape[1]
    depth = child_panel.shape[0]
    panel = panel_inverse.shape[0]
    own_rows = panel_entries.shape[1]
    slots = own_rows // rows // grids
    span = slots * rows
    base = span + children * rows
    sent = base + 2 * rows * (width // panel)
    like = jax.ShapeDtypeStruct
    small = own_rows * width <= 512 * 512
    kept = pltpu.VMEM if small else like

    def in_hbm(x):
        return pltpu.with_memory_space_constraint(x, pltpu.HBM)

    def swap(x, axis, d):
        n = lax.axis_size(axis)
        return lax.ppermute(x, axis, [(i, i ^ d) for i in range(n)])

    prepared = call(
        functools.partial(prepare_body, cubes, grids, span),
        [kept((base, depth), BF16)] * grids
        + [kept((grids, (grids - 1) * span, depth), BF16)]
        + [kept((chips * rows, width), BF16)] * 2,
        [ANY] * 6,
        [
            pltpu.SMEM(block_owner.shape, I32),
            pltpu.SMEM(child_dest.shape, I32),
            pltpu.VMEM(child_rows.shape, I32),
            pltpu.VMEM(child_update.shape, BF16),
            pltpu.VMEM(child_panel.shape[::-1], BF16),
            pltpu.VMEM(panel_entries.shape, BF16),
            pltpu.VMEM(panel_entries.shape[::-1], BF16),
            pltpu.SemaphoreType.DMA((6,)),
        ],
        2 * rows * rows * children * (width + depth),
        4 * own_rows * depth,
        limit=61,
    )(*(in_hbm(x) for x in (block_owner, child_dest, child_rows, child_update, child_panel.T, panel_entries)))
    firsts = prepared[:grids]
    rest, to_other, keep = prepared[grids:]
    other = swap(to_other, "cube", 1)
    firsts = [firsts[0]] + [swap(firsts[d], "grid", d) for d in range(1, grids)]
    rest = lax.all_to_all(rest, "grid", split_axis=0, concat_axis=0, tiled=True)
    packed = call(
        functools.partial(pack_body, grids, rows, base),
        [kept((base, panel), BF16)] + [kept((sent, panel), BF16)] * (chips - 1),
        [VMEM] * (2 + grids),
        [],
        1000,
        2 * chips * sent * panel,
    )(keep, other, *firsts)
    mine = packed[0]
    pieces = []
    for i in range(chips):
        piece = mine if i == 0 else swap(packed[i], "cube", 2 * i)
        pieces += [piece, swap(piece, "cube", 1)]
    plan = call(
        functools.partial(plan_body, cubes, grids, slots),
        [like((2 * cubes + grids + cubes * (slots + children),), I32)],
        [SMEM, SMEM, ANY],
        [pltpu.SMEM(block_owner.shape, I32), pltpu.SMEM((cubes,), I32)],
        100000,
        6000000,
        [SMEM],
    )(block_owner, child_dest, mine)[0]
    entries, before, turned = call(
        functools.partial(own_body, cubes, grids, span, rows),
        [like((own_rows, panel), BF16), like((own_rows, panel), BF16), like((panel, panel), BF16)],
        [SMEM] + [VMEM] * 3,
        [],
        2 * own_rows * panel * panel,
        2 * (panel * panel + 2 * own_rows * panel),
    )(plan, panel_inverse, mine, rest)
    return tuple(
        call(
            functools.partial(schur_body, cubes, grids, slots, rows, children),
            [like((own_rows, width), BF16), like((depth, own_rows), BF16)],
            [SMEM] + [VMEM] * (5 + cubes),
            [
                pltpu.VMEM((width + rows, panel), F32),
                pltpu.VMEM((own_rows + rows, panel), F32),
                pltpu.VMEM((cubes * rows, panel), BF16),
                pltpu.VMEM((own_rows + rows, panel), BF16),
                pltpu.VMEM((own_rows + rows, width), F32),
            ],
            2 * own_rows * width * panel,
            2 * (own_rows * width + (own_rows + cubes * span) * panel),
            limit=16 if small else 56,
        )(plan, turned, entries, before, keep, other, *pieces)
    )


def solution(mesh):
    placed = (
        P("cube", "grid"),
        P("grid", "cube"),
        P("grid", "cube"),
        P(),
        P(),
        P(),
        P("cube", None),
    )
    return jax.shard_map(
        local,
        mesh=mesh,
        in_specs=placed,
        out_specs=(P("cube", "grid"), P("grid", "cube")),
        check_vma=False,
    )
```

```python
import functools

import jax
import jax.numpy as jnp
from jax import lax
from jax.experimental import pallas as pl
from jax.experimental.pallas import tpu as pltpu
from jax.sharding import PartitionSpec as P

F32 = jnp.float32
BF16 = jnp.bfloat16
I32 = jnp.int32
VMEM = pl.BlockSpec(memory_space=pltpu.VMEM)
SMEM = pl.BlockSpec(memory_space=pltpu.SMEM)
ANY = pl.BlockSpec(memory_space=pl.ANY)
MIB = 1024 * 1024


def call(body, outs, in_specs, scratch, flops, moved, out_specs=None, limit=16):
    return pl.pallas_call(
        body,
        out_shape=outs,
        in_specs=in_specs,
        out_specs=[VMEM] * len(outs) if out_specs is None else out_specs,
        scratch_shapes=scratch,
        compiler_params=pltpu.CompilerParams(vmem_limit_bytes=limit * MIB),
        cost_estimate=pl.CostEstimate(flops=flops, bytes_accessed=moved, transcendentals=0),
    )


def rows_at(index, size):
    return pl.ds(pl.multiple_of(index * size, size), size)


def prepare_body(
    cubes, grids, span, owner_hbm, dest_hbm, rows_hbm, update_hbm, panel_hbm, entries_hbm, *refs
):
    firsts, rests, blocks_ref = refs[:grids], refs[grids : 2 * grids - 1], refs[2 * grids - 1]
    owner_ref, dest_ref, rows_ref, update_ref, panel_ref, entries_ref, flipped, sems = refs[2 * grids :]
    copies = [
        pltpu.make_async_copy(source, target, sems.at[i])
        for i, (source, target) in enumerate(
            (
                (entries_hbm, entries_ref),
                (panel_hbm, panel_ref),
                (rows_hbm, rows_ref),
                (update_hbm, update_ref),
                (owner_hbm, owner_ref),
                (dest_hbm, dest_ref),
            )
        )
    ]
    for copy in copies:
        copy.start()
    mine = lax.axis_index("cube")
    column = lax.axis_index("grid")
    children, rows = rows_ref.shape
    base = span + children * rows
    blocks_ref[...] = jnp.zeros_like(blocks_ref)
    copies[0].wait()
    flipped[...] = entries_ref[...].astype(F32).T.astype(BF16)
    for d in range(grids):
        piece = flipped[rows_at(jnp.bitwise_xor(column, d), span), :]
        firsts[d][pl.ds(0, span), :] = piece
        for e in range(grids):
            if e != d:
                k = d if d < e else d - 1
                if e == 1:
                    firsts[1][pl.ds(base + k * span, span), :] = piece
                else:
                    rests[max(e - 1, 0)][pl.ds(k * span, span), :] = piece
    for copy in copies[1:]:
        copy.wait()
    for k in range(children):
        want = rows_ref[k : k + 1, :]
        put = (lax.broadcasted_iota(I32, (rows, rows), 0) == want).astype(BF16)
        part = pl.ds(k * rows, rows)
        placed = jnp.dot(put, panel_ref[part, :], preferred_element_type=F32).astype(BF16)
        for d in range(grids):
            firsts[d][pl.ds(span + k * rows, rows), :] = placed
        moved = jnp.dot(put, update_ref[part, :], preferred_element_type=F32).astype(BF16)
        d = jnp.bitwise_xor(owner_ref[dest_ref[mine * children + k]], mine)
        blocks_ref[rows_at(d, rows), :] = moved


def pack_body(grids, rows, base, plan_ref, blocks_ref, *refs):
    firsts, payloads = refs[:grids], refs[grids:]
    depth = firsts[0].shape[1]
    panel = payloads[0].shape[1]
    chunks = blocks_ref.shape[1] // panel
    for d in range(grids):
        piece = firsts[d][pl.ds(0, base), :]
        for payload in payloads:
            payload[pl.ds(0, base), pl.ds(d * depth, depth)] = piece
    for i, payload in enumerate(payloads):
        for half in range(2):
            for j in range(chunks):
                at = base + (half * chunks + j) * rows
                block = blocks_ref[pl.ds((2 * i + half) * rows, rows), pl.ds(j * panel, panel)]
                payload[pl.ds(at, rows), :] = block


def plan_body(cubes, grids, slots, owner_ref, dest_ref, out_ref, slot_ref, count_ref):
    mine = lax.axis_index("cube")
    column = lax.axis_index("grid")
    blocks = owner_ref.shape[0]
    in_range = blocks // grids
    children = dest_ref.shape[0] // cubes
    none = grids * slots
    places = 2 * cubes + grids
    child_places = places + cubes * slots
    for r in range(grids):

        def count_own(i, seen):
            b = r * in_range + i
            own = owner_ref[b] == mine
            slot_ref[b] = jnp.where(own, r * slots + seen, none)
            return seen + own.astype(I32)

        out_ref[2 * cubes + r] = lax.fori_loop(0, in_range, count_own, I32(0), unroll=8)
    for d in range(cubes):
        source = jnp.bitwise_xor(mine, d)
        slot, which = I32(none), I32(0)
        for k in range(children):
            b = dest_ref[source * children + k]
            here = slot_ref[b]
            which = jnp.where(here < none, k, which)
            slot = jnp.minimum(slot, here)
            local_b = b - column * in_range
            inside = jnp.logical_and(local_b >= 0, local_b < in_range)
            out_ref[child_places + d * children + k] = jnp.where(inside, local_b, in_range)
        out_ref[d] = slot
        out_ref[cubes + d] = which
        count_ref[d] = 0
        for k in range(slots):
            out_ref[places + d * slots + k] = in_range

    def place(i, carry):
        d = jnp.bitwise_xor(owner_ref[column * in_range + i], mine)
        k = count_ref[d]
        out_ref[places + d * slots + k] = i
        count_ref[d] = k + 1
        return carry

    lax.fori_loop(0, in_range, place, 0, unroll=8)


def own_body(cubes, grids, span, rows, base, plan_ref, inverse_ref, mine_ref, full_ref, *refs):
    rests = refs[: grids - 1]
    entries_ref, factor_ref, turned_ref = refs[grids - 1 :]
    column = lax.axis_index("grid")
    depth = rests[0].shape[1]
    for d in range(grids):
        turned_ref[pl.ds(d * depth, depth), :] = inverse_ref[rows_at(jnp.bitwise_xor(column, d), depth), :]
    for e in range(grids):
        r = jnp.bitwise_xor(column, e)
        ids = lax.broadcasted_iota(I32, (span, depth), 0)
        live = ids < plan_ref[2 * cubes + r] * rows
        for d in range(grids):
            if e == 0:
                piece = mine_ref[pl.ds(0, span), pl.ds(d * depth, depth)]
            else:
                k = d ^ e
                at = (k if k < d else k - 1) * span
                if d == 1:
                    piece = full_ref[pl.ds(base + at, span), :]
                else:
                    piece = rests[max(d - 1, 0)][pl.ds(at, span), :]
            piece = jnp.where(live, piece.astype(F32), 0.0).astype(BF16)
            entries_ref[rows_at(r, span), pl.ds(d * depth, depth)] = piece
    factor_ref[...] = jnp.dot(entries_ref[...], turned_ref[...], preferred_element_type=F32).astype(BF16)


def join_body(first_ref, second_ref, out_ref):
    pass


def schur_body(
    cubes, grids, slots, rows, children, plan_ref, turned_ref, entries_ref, before_ref, *refs
):
    pieces = refs[:cubes]
    out_ref, panel_ref, ranged, touched, few, factor_ref, total = refs[cubes:]
    column = lax.axis_index("grid")
    span = slots * rows
    base = span + children * rows
    own_rows, panel = entries_ref.shape
    width = out_ref.shape[1]
    chunks = width // panel
    depth = panel_ref.shape[0]
    places = 2 * cubes + grids
    child_places = places + cubes * slots
    none = own_rows // rows
    total[...] = jnp.zeros_like(total)
    for d in range(cubes):
        at = rows_at(plan_ref[d], rows)
        for j in range(chunks):
            part = pl.ds(base + ((d & 1) * chunks + j) * rows, rows)
            total[at, pl.ds(j * panel, panel)] += pieces[d][part, :].astype(F32)
    for d in range(cubes):
        slot = plan_ref[d]
        touched[rows_at(slot, rows), :] = entries_ref[rows_at(jnp.minimum(slot, none - 1), rows), :].astype(F32)
    for d in range(cubes):
        child = pieces[d][rows_at(slots + plan_ref[cubes + d], rows), :]
        touched[rows_at(plan_ref[d], rows), :] += child.astype(F32)
    for d in range(cubes):
        few[pl.ds(d * rows, rows), :] = touched[rows_at(plan_ref[d], rows), :].astype(BF16)
    redone = jnp.dot(few[...], turned_ref[...], preferred_element_type=F32).astype(BF16)
    factor_ref[pl.ds(0, own_rows), :] = before_ref[...]
    for d in range(cubes):
        factor_ref[rows_at(plan_ref[d], rows), :] = redone[d * rows : (d + 1) * rows, :]
    factor = factor_ref[pl.ds(0, own_rows), :]
    for d in range(cubes):
        for k in range(slots):
            at = rows_at(plan_ref[places + d * slots + k], rows)
            ranged[at, :] = pieces[d][pl.ds(k * rows, rows), :].astype(F32)
    for d in range(cubes):
        for k in range(children):
            at = rows_at(plan_ref[child_places + d * children + k], rows)
            ranged[at, :] += pieces[d][pl.ds(span + k * rows, rows), :].astype(F32)
    column_factor = jnp.dot(
        ranged[pl.ds(0, width), :].astype(BF16), turned_ref[...], preferred_element_type=F32
    ).astype(BF16)
    product = lax.dot_general(factor, column_factor, (((1,), (1,)), ((), ())), preferred_element_type=F32)
    out_ref[...] = (total[pl.ds(0, own_rows), :] - product).astype(BF16)
    if depth % 128 == 0:
        cols = pl.ds(pl.multiple_of(column * depth, depth), depth)
        panel_ref[...] = factor_ref[pl.ds(0, own_rows), cols].astype(F32).T.astype(BF16)
    else:
        for r in range(grids):

            @pl.when(column == r)
            def _():
                part = factor_ref[pl.ds(0, own_rows), pl.ds(r * depth, depth)]
                panel_ref[...] = part.astype(F32).T.astype(BF16)


def local(
    child_update, child_panel, panel_entries, panel_inverse, block_owner, child_dest, child_rows
):
    cubes = lax.axis_size("cube")
    grids = lax.axis_size("grid")
    chips = cubes // 2
    children, rows = child_rows.shape
    width = child_update.shape[1]
    depth = child_panel.shape[0]
    panel = panel_inverse.shape[0]
    own_rows = panel_entries.shape[1]
    slots = own_rows // rows // grids
    span = slots * rows
    base = span + children * rows
    sent = base + 2 * rows * (width // panel)
    like = jax.ShapeDtypeStruct
    small = own_rows * width <= 512 * 512
    kept = pltpu.VMEM if small else like

    def in_hbm(x):
        return pltpu.with_memory_space_constraint(x, pltpu.HBM)

    def join(first, second):
        return pl.pallas_call(
            join_body,
            out_shape=like(first.shape, first.dtype),
            in_specs=[ANY, ANY],
            out_specs=ANY,
            input_output_aliases={0: 0},
        )(first, second)

    def swap(x, axis, d):
        n = lax.axis_size(axis)
        return lax.ppermute(x, axis, [(i, i ^ d) for i in range(n)])

    rest_rows = (grids - 1) * span
    prepared = call(
        functools.partial(prepare_body, cubes, grids, span),
        [kept((base + (rest_rows if d == 1 else 0), depth), BF16) for d in range(grids)]
        + [kept((rest_rows, depth), BF16)] * (grids - 1)
        + [kept((cubes * rows, width), BF16)],
        [ANY] * 6,
        [
            pltpu.SMEM(block_owner.shape, I32),
            pltpu.SMEM(child_dest.shape, I32),
            pltpu.VMEM(child_rows.shape, I32),
            pltpu.VMEM(child_update.shape, BF16),
            pltpu.VMEM(child_panel.shape[::-1], BF16),
            pltpu.VMEM(panel_entries.shape, BF16),
            pltpu.VMEM(panel_entries.shape[::-1], BF16),
            pltpu.SemaphoreType.DMA((6,)),
        ],
        2 * rows * rows * children * (width + depth),
        4 * own_rows * depth,
        limit=28,
    )(*(in_hbm(x) for x in (block_owner, child_dest, child_rows, child_update, child_panel.T, panel_entries)))
    firsts, rests, blocks = list(prepared[:grids]), list(prepared[grids:-1]), prepared[-1]
    for d in [*range(2, grids), 1]:
        firsts[d] = swap(firsts[d], "grid", d)
    for d in range(2, grids):
        rests[d - 1] = swap(rests[d - 1], "grid", d)
    plan = call(
        functools.partial(plan_body, cubes, grids, slots),
        [like((2 * cubes + grids + cubes * (slots + children),), I32)],
        [SMEM, SMEM],
        [pltpu.SMEM(block_owner.shape, I32), pltpu.SMEM((cubes,), I32)],
        100000,
        6000000,
        [SMEM],
    )(block_owner, child_dest)[0]
    packed = call(
        functools.partial(pack_body, grids, rows, base),
        [kept((sent, panel), BF16)] * chips,
        [SMEM] + [VMEM] * (1 + grids),
        [],
        1000,
        2 * chips * sent * panel,
    )(plan, blocks, *firsts)
    arrived = [packed[0]] + [swap(packed[i], "cube", 2 * i) for i in range(1, chips)]
    entries, before, turned = call(
        functools.partial(own_body, cubes, grids, span, rows, base),
        [like((own_rows, panel), BF16), like((own_rows, panel), BF16), like((panel, panel), BF16)],
        [SMEM] + [VMEM] * (2 + grids),
        [],
        2 * own_rows * panel * panel,
        2 * (panel * panel + 2 * own_rows * panel),
    )(plan, panel_inverse, packed[0], firsts[1], *rests)
    arrived[-1] = join(arrived[-1], turned)
    pieces = []
    for piece in arrived:
        pieces += [piece, swap(piece, "cube", 1)]
    return tuple(
        call(
            functools.partial(schur_body, cubes, grids, slots, rows, children),
            [like((own_rows, width), BF16), like((depth, own_rows), BF16)],
            [SMEM] + [VMEM] * (3 + cubes),
            [
                pltpu.VMEM((width + rows, panel), F32),
                pltpu.VMEM((own_rows + rows, panel), F32),
                pltpu.VMEM((cubes * rows, panel), BF16),
                pltpu.VMEM((own_rows + rows, panel), BF16),
                pltpu.VMEM((own_rows + rows, width), F32),
            ],
            2 * own_rows * width * panel,
            2 * (own_rows * width + (own_rows + cubes * span) * panel),
            limit=16 if small else 56,
        )(plan, turned, entries, before, *pieces)
    )


def solution(mesh):
    placed = (
        P("cube", "grid"),
        P("grid", "cube"),
        P("grid", "cube"),
        P(),
        P(),
        P(),
        P("cube", None),
    )
    return jax.shard_map(
        local,
        mesh=mesh,
        in_specs=placed,
        out_specs=(P("cube", "grid"), P("grid", "cube")),
        check_vma=False,
    )
```

```python
import functools

import jax
import jax.numpy as jnp
from jax import lax
from jax.experimental import pallas as pl
from jax.experimental.pallas import tpu as pltpu
from jax.sharding import PartitionSpec as P

F32 = jnp.float32
BF16 = jnp.bfloat16
I32 = jnp.int32
VMEM = pl.BlockSpec(memory_space=pltpu.VMEM)
SMEM = pl.BlockSpec(memory_space=pltpu.SMEM)
ANY = pl.BlockSpec(memory_space=pl.ANY)
MIB = 1024 * 1024


def call(body, outs, in_specs, scratch, flops, moved, out_specs=None, limit=16, aliases={}):
    return pl.pallas_call(
        body,
        out_shape=outs,
        in_specs=in_specs,
        out_specs=[VMEM] * len(outs) if out_specs is None else out_specs,
        scratch_shapes=scratch,
        input_output_aliases=aliases,
        compiler_params=pltpu.CompilerParams(vmem_limit_bytes=limit * MIB),
        cost_estimate=pl.CostEstimate(flops=flops, bytes_accessed=moved, transcendentals=0),
    )


def rows_at(index, size):
    return pl.ds(pl.multiple_of(index * size, size), size)


def prepare_body(
    cubes, grids, span, owner_hbm, dest_hbm, rows_hbm, update_hbm, panel_hbm, entries_hbm, *refs
):
    firsts, rests, blocks_ref = refs[:grids], refs[grids : 2 * grids - 1], refs[2 * grids - 1]
    owner_ref, dest_ref, rows_ref, update_ref, panel_ref, entries_ref, flipped, sems = refs[2 * grids :]
    copies = [
        pltpu.make_async_copy(source, target, sems.at[i])
        for i, (source, target) in enumerate(
            (
                (entries_hbm, entries_ref),
                (panel_hbm, panel_ref),
                (rows_hbm, rows_ref),
                (update_hbm, update_ref),
                (owner_hbm, owner_ref),
                (dest_hbm, dest_ref),
            )
        )
    ]
    for copy in copies:
        copy.start()
    mine = lax.axis_index("cube")
    column = lax.axis_index("grid")
    children, rows = rows_ref.shape
    base = span + children * rows
    blocks_ref[...] = jnp.zeros_like(blocks_ref)
    copies[0].wait()
    flipped[...] = entries_ref[...].astype(F32).T.astype(BF16)
    for d in range(grids):
        piece = flipped[rows_at(jnp.bitwise_xor(column, d), span), :]
        firsts[d][pl.ds(0, span), :] = piece
        for e in range(grids):
            if e != d:
                k = d if d < e else d - 1
                if e == 1:
                    firsts[1][pl.ds(base + k * span, span), :] = piece
                else:
                    rests[max(e - 1, 0)][pl.ds(k * span, span), :] = piece
    for copy in copies[1:]:
        copy.wait()
    for k in range(children):
        want = rows_ref[k : k + 1, :]
        put = (lax.broadcasted_iota(I32, (rows, rows), 0) == want).astype(BF16)
        part = pl.ds(k * rows, rows)
        placed = jnp.dot(put, panel_ref[part, :], preferred_element_type=F32).astype(BF16)
        for d in range(grids):
            firsts[d][pl.ds(span + k * rows, rows), :] = placed
        moved = jnp.dot(put, update_ref[part, :], preferred_element_type=F32).astype(BF16)
        d = jnp.bitwise_xor(owner_ref[dest_ref[mine * children + k]], mine)
        blocks_ref[rows_at(d, rows), :] = moved


def pack_body(grids, rows, base, plan_ref, blocks_ref, *refs):
    firsts, payloads = [*refs[grids - 2 : grids], *refs[: grids - 2]], refs[grids:]
    depth = firsts[0].shape[1]
    panel = payloads[0].shape[1]
    chunks = blocks_ref.shape[1] // panel
    for d in range(grids):
        piece = firsts[d][pl.ds(0, base), :]
        for payload in payloads:
            payload[pl.ds(0, base), pl.ds(d * depth, depth)] = piece
    for i, payload in enumerate(payloads):
        for half in range(2):
            for j in range(chunks):
                at = base + (half * chunks + j) * rows
                block = blocks_ref[pl.ds((2 * i + half) * rows, rows), pl.ds(j * panel, panel)]
                payload[pl.ds(at, rows), :] = block


def plan_body(cubes, grids, slots, owner_hbm, dest_hbm, out_ref, owner_ref, dest_ref, slot_ref, count_ref, sems):
    fetches = [
        pltpu.make_async_copy(owner_hbm, owner_ref, sems.at[0]),
        pltpu.make_async_copy(dest_hbm, dest_ref, sems.at[1]),
    ]
    for fetch in fetches:
        fetch.start()
    for fetch in fetches:
        fetch.wait()
    mine = lax.axis_index("cube")
    column = lax.axis_index("grid")
    blocks = owner_ref.shape[0]
    in_range = blocks // grids
    children = dest_ref.shape[0] // cubes
    none = grids * slots
    places = 2 * cubes + grids
    child_places = places + cubes * slots
    for r in range(grids):

        def count_own(i, seen):
            b = r * in_range + i
            own = owner_ref[b] == mine
            slot_ref[b] = jnp.where(own, r * slots + seen, none)
            return seen + own.astype(I32)

        out_ref[2 * cubes + r] = lax.fori_loop(0, in_range, count_own, I32(0), unroll=8)
    for d in range(cubes):
        source = jnp.bitwise_xor(mine, d)
        slot, which = I32(none), I32(0)
        for k in range(children):
            b = dest_ref[source * children + k]
            here = slot_ref[b]
            which = jnp.where(here < none, k, which)
            slot = jnp.minimum(slot, here)
            local_b = b - column * in_range
            inside = jnp.logical_and(local_b >= 0, local_b < in_range)
            out_ref[child_places + d * children + k] = jnp.where(inside, local_b, in_range)
        out_ref[d] = slot
        out_ref[cubes + d] = which
        count_ref[d] = 0
        for k in range(slots):
            out_ref[places + d * slots + k] = in_range

    def place(i, carry):
        d = jnp.bitwise_xor(owner_ref[column * in_range + i], mine)
        k = count_ref[d]
        out_ref[places + d * slots + k] = i
        count_ref[d] = k + 1
        return carry

    lax.fori_loop(0, in_range, place, 0, unroll=8)


def own_body(cubes, grids, span, rows, base, plan_ref, inverse_ref, mine_ref, full_ref, *refs):
    rests = refs[: grids - 1]
    entries_ref, factor_ref, turned_ref = refs[grids - 1 :]
    column = lax.axis_index("grid")
    depth = rests[0].shape[1]
    for d in range(grids):
        turned_ref[pl.ds(d * depth, depth), :] = inverse_ref[rows_at(jnp.bitwise_xor(column, d), depth), :]
    for e in range(grids):
        r = jnp.bitwise_xor(column, e)
        ids = lax.broadcasted_iota(I32, (span, depth), 0)
        live = ids < plan_ref[2 * cubes + r] * rows
        for d in range(grids):
            if e == 0:
                piece = mine_ref[pl.ds(0, span), pl.ds(d * depth, depth)]
            else:
                k = d ^ e
                at = (k if k < d else k - 1) * span
                if d == 1:
                    piece = full_ref[pl.ds(base + at, span), :]
                else:
                    piece = rests[max(d - 1, 0)][pl.ds(at, span), :]
            piece = jnp.where(live, piece.astype(F32), 0.0).astype(BF16)
            entries_ref[rows_at(r, span), pl.ds(d * depth, depth)] = piece
    factor_ref[...] = jnp.dot(entries_ref[...], turned_ref[...], preferred_element_type=F32).astype(BF16)


def join_body(*refs):
    pass


def add_children(cubes, grids, slots, rows, children, plan_ref, pieces, ranged, touched, total):
    span = slots * rows
    base = span + children * rows
    panel = ranged.shape[1]
    chunks = total.shape[1] // panel
    child_places = 2 * cubes + grids + cubes * slots
    in_range = ranged.shape[0] // rows - 1
    for d, piece in pieces.items():
        at = rows_at(plan_ref[d], rows)
        touched[at, :] += piece[rows_at(slots + plan_ref[cubes + d], rows), :].astype(F32)
        for j in range(chunks):
            part = pl.ds(base + ((d & 1) * chunks + j) * rows, rows)
            total[at, pl.ds(j * panel, panel)] += piece[part, :].astype(F32)
        for k in range(children):
            place = plan_ref[child_places + d * children + k]

            @pl.when(place < in_range)
            def _():
                ranged[rows_at(place, rows), :] += piece[pl.ds(span + k * rows, rows), :].astype(F32)


def early_body(cubes, grids, slots, rows, children, plan_ref, entries_ref, *refs):
    pieces = dict(enumerate(refs[:-3]))
    ranged, touched, total = refs[-3:]
    places = 2 * cubes + grids
    none = entries_ref.shape[0] // rows
    ranged[...] = jnp.zeros_like(ranged)
    total[...] = jnp.zeros_like(total)
    for d in range(cubes):
        slot = plan_ref[d]
        touched[rows_at(slot, rows), :] = entries_ref[rows_at(jnp.minimum(slot, none - 1), rows), :].astype(F32)
    for d, piece in pieces.items():
        for k in range(slots):
            at = rows_at(plan_ref[places + d * slots + k], rows)
            ranged[at, :] = piece[pl.ds(k * rows, rows), :].astype(F32)
    add_children(cubes, grids, slots, rows, children, plan_ref, pieces, ranged, touched, total)


def schur_body(cubes, grids, slots, rows, children, plan_ref, turned_ref, before_ref, *refs):
    pieces = {cubes - 2: refs[0], cubes - 1: refs[1]}
    out_ref, panel_ref, ranged, touched, total, few, factor_ref = refs[5:]
    column = lax.axis_index("grid")
    own_rows, width = out_ref.shape
    depth = panel_ref.shape[0]
    places = 2 * cubes + grids
    in_range = width // rows
    for d, piece in pieces.items():
        for k in range(slots):
            place = plan_ref[places + d * slots + k]

            @pl.when(place < in_range)
            def _():
                ranged[rows_at(place, rows), :] += piece[pl.ds(k * rows, rows), :].astype(F32)

    add_children(cubes, grids, slots, rows, children, plan_ref, pieces, ranged, touched, total)
    for d in range(cubes):
        few[pl.ds(d * rows, rows), :] = touched[rows_at(plan_ref[d], rows), :].astype(BF16)
    redone = jnp.dot(few[...], turned_ref[...], preferred_element_type=F32).astype(BF16)
    factor_ref[pl.ds(0, own_rows), :] = before_ref[...]
    for d in range(cubes):
        factor_ref[rows_at(plan_ref[d], rows), :] = redone[d * rows : (d + 1) * rows, :]
    column_factor = jnp.dot(
        ranged[pl.ds(0, width), :].astype(BF16), turned_ref[...], preferred_element_type=F32
    ).astype(BF16)
    product = lax.dot_general(
        factor_ref[pl.ds(0, own_rows), :], column_factor, (((1,), (1,)), ((), ())), preferred_element_type=F32
    )
    out_ref[...] = (total[pl.ds(0, own_rows), :] - product).astype(BF16)
    if depth % 128 == 0:
        cols = pl.ds(pl.multiple_of(column * depth, depth), depth)
        panel_ref[...] = factor_ref[pl.ds(0, own_rows), cols].astype(F32).T.astype(BF16)
    else:
        for r in range(grids):

            @pl.when(column == r)
            def _():
                part = factor_ref[pl.ds(0, own_rows), pl.ds(r * depth, depth)]
                panel_ref[...] = part.astype(F32).T.astype(BF16)


def local(
    child_update, child_panel, panel_entries, panel_inverse, block_owner, child_dest, child_rows
):
    cubes = lax.axis_size("cube")
    grids = lax.axis_size("grid")
    chips = cubes // 2
    children, rows = child_rows.shape
    width = child_update.shape[1]
    depth = child_panel.shape[0]
    panel = panel_inverse.shape[0]
    own_rows = panel_entries.shape[1]
    slots = own_rows // rows // grids
    span = slots * rows
    base = span + children * rows
    sent = base + 2 * rows * (width // panel)
    like = jax.ShapeDtypeStruct
    small = own_rows * width <= 512 * 512
    kept = pltpu.VMEM if small else like

    def in_hbm(x):
        return pltpu.with_memory_space_constraint(x, pltpu.HBM)

    def join(first, *others):
        if small:
            first = pltpu.with_memory_space_constraint(first, pltpu.VMEM)
        return pl.pallas_call(
            join_body,
            out_shape=kept(first.shape, first.dtype),
            in_specs=[ANY] * (1 + len(others)),
            out_specs=ANY,
            input_output_aliases={0: 0},
        )(first, *others)

    def swap(x, axis, d):
        n = lax.axis_size(axis)
        return lax.ppermute(x, axis, [(i, i ^ d) for i in range(n)])

    rest_rows = (grids - 1) * span
    prepared = call(
        functools.partial(prepare_body, cubes, grids, span),
        [kept((base + (rest_rows if d == 1 else 0), depth), BF16) for d in range(grids)]
        + [kept((rest_rows, depth), BF16)] * (grids - 1)
        + [kept((cubes * rows, width), BF16)],
        [ANY] * 6,
        [
            pltpu.SMEM(block_owner.shape, I32),
            pltpu.SMEM(child_dest.shape, I32),
            pltpu.VMEM(child_rows.shape, I32),
            pltpu.VMEM(child_update.shape, BF16),
            pltpu.VMEM(child_panel.shape[::-1], BF16),
            pltpu.VMEM(panel_entries.shape, BF16),
            pltpu.VMEM(panel_entries.shape[::-1], BF16),
            pltpu.SemaphoreType.DMA((6,)),
        ],
        2 * rows * rows * children * (width + depth),
        4 * own_rows * depth,
        limit=28,
    )(*(in_hbm(x) for x in (block_owner, child_dest, child_rows, child_update, child_panel.T, panel_entries)))
    firsts, rests, blocks = list(prepared[:grids]), list(prepared[grids:-1]), prepared[-1]
    for d in [*range(2, grids), 1]:
        firsts[d] = swap(firsts[d], "grid", d)
    for d in range(2, grids):
        rests[d - 1] = swap(rests[d - 1], "grid", d)
    plan = call(
        functools.partial(plan_body, cubes, grids, slots),
        [like((2 * cubes + grids + cubes * (slots + children),), I32)],
        [ANY, ANY],
        [
            pltpu.SMEM(block_owner.shape, I32),
            pltpu.SMEM(child_dest.shape, I32),
            pltpu.SMEM(block_owner.shape, I32),
            pltpu.SMEM((cubes,), I32),
            pltpu.SemaphoreType.DMA((2,)),
        ],
        100000,
        6000000,
        [SMEM],
    )(in_hbm(block_owner), in_hbm(child_dest))[0]
    packed = call(
        functools.partial(pack_body, grids, rows, base),
        [kept((sent, panel), BF16)] * chips,
        [ANY] + [VMEM] * (1 + grids),
        [],
        1000,
        2 * chips * sent * panel,
    )(plan, blocks, *firsts[2:], *firsts[:2])
    arrived = [packed[0]] + [swap(packed[i], "cube", 2 * i) for i in range(1, chips)]
    entries, before, turned = call(
        functools.partial(own_body, cubes, grids, span, rows, base),
        [like((own_rows, panel), BF16), like((own_rows, panel), BF16), like((panel, panel), BF16)],
        [SMEM] + [VMEM] * (2 + grids),
        [],
        2 * own_rows * panel * panel,
        2 * (panel * panel + 2 * own_rows * panel),
    )(plan, panel_inverse, packed[0], firsts[1], *rests)
    arrived[-1] = join(arrived[-1], *rests[1:])
    pieces = []
    for piece in arrived:
        pieces += [piece, swap(piece, "cube", 1)]
    sizes = (cubes, grids, slots, rows, children)
    shapes = [(width + rows, panel), (own_rows + rows, panel), (own_rows + rows, width)]
    early = call(
        functools.partial(early_body, *sizes),
        [kept(shape, F32) for shape in shapes],
        [SMEM] + [VMEM] * (cubes - 1),
        [],
        1000,
        4 * width * panel,
        limit=16 if small else 56,
    )(plan, entries, *pieces[:-2])
    return tuple(
        call(
            functools.partial(schur_body, *sizes),
            [like((own_rows, width), BF16), like((depth, own_rows), BF16)] + [kept(shape, F32) for shape in shapes],
            [SMEM] + [VMEM] * 7,
            [pltpu.VMEM((cubes * rows, panel), BF16), pltpu.VMEM((own_rows + rows, panel), BF16)],
            2 * own_rows * width * panel,
            2 * (own_rows * width + (own_rows + cubes * span) * panel),
            limit=16 if small else 56,
            aliases={5: 2, 6: 3, 7: 4},
        )(plan, turned, before, *pieces[-2:], *early)[:2]
    )


def solution(mesh):
    placed = (
        P("cube", "grid"),
        P("grid", "cube"),
        P("grid", "cube"),
        P(),
        P(),
        P(),
        P("cube", None),
    )
    return jax.shard_map(
        local,
        mesh=mesh,
        in_specs=placed,
        out_specs=(P("cube", "grid"), P("grid", "cube")),
        check_vma=False,
    )
```

```python
import functools

import jax
import jax.numpy as jnp
from jax import lax
from jax.experimental import pallas as pl
from jax.experimental.pallas import tpu as pltpu
from jax.sharding import PartitionSpec as P

F32 = jnp.float32
BF16 = jnp.bfloat16
I32 = jnp.int32
VMEM = pl.BlockSpec(memory_space=pltpu.VMEM)
SMEM = pl.BlockSpec(memory_space=pltpu.SMEM)
ANY = pl.BlockSpec(memory_space=pl.ANY)
MIB = 1024 * 1024


def call(body, outs, in_specs, scratch, flops, moved, out_specs=None, limit=16, aliases={}):
    return pl.pallas_call(
        body,
        out_shape=outs,
        in_specs=in_specs,
        out_specs=[VMEM] * len(outs) if out_specs is None else out_specs,
        scratch_shapes=scratch,
        input_output_aliases=aliases,
        compiler_params=pltpu.CompilerParams(vmem_limit_bytes=limit * MIB),
        cost_estimate=pl.CostEstimate(flops=flops, bytes_accessed=moved, transcendentals=0),
    )


def rows_at(index, size):
    return pl.ds(pl.multiple_of(index * size, size), size)


def prepare_body(
    cubes, grids, span, owner_hbm, dest_hbm, rows_hbm, update_hbm, panel_hbm, entries_hbm, *refs
):
    firsts, rests, blocks_ref = refs[:grids], refs[grids : 2 * grids - 1], refs[2 * grids - 1]
    owner_ref, dest_ref, rows_ref, update_ref, panel_ref, entries_ref, flipped, sems = refs[2 * grids :]
    copies = [
        pltpu.make_async_copy(source, target, sems.at[i])
        for i, (source, target) in enumerate(
            (
                (entries_hbm, entries_ref),
                (panel_hbm, panel_ref),
                (rows_hbm, rows_ref),
                (update_hbm, update_ref),
                (owner_hbm, owner_ref),
                (dest_hbm, dest_ref),
            )
        )
    ]
    for copy in copies:
        copy.start()
    mine = lax.axis_index("cube")
    column = lax.axis_index("grid")
    children, rows = rows_ref.shape
    base = span + children * rows
    blocks_ref[...] = jnp.zeros_like(blocks_ref)
    copies[0].wait()
    flipped[...] = entries_ref[...].astype(F32).T.astype(BF16)
    for d in range(grids):
        piece = flipped[rows_at(jnp.bitwise_xor(column, d), span), :]
        firsts[d][pl.ds(0, span), :] = piece
        for e in range(grids):
            if e != d:
                k = d if d < e else d - 1
                if e == 1:
                    firsts[1][pl.ds(base + k * span, span), :] = piece
                else:
                    rests[max(e - 1, 0)][pl.ds(k * span, span), :] = piece
    for copy in copies[1:]:
        copy.wait()
    for k in range(children):
        want = rows_ref[k : k + 1, :]
        put = (lax.broadcasted_iota(I32, (rows, rows), 0) == want).astype(BF16)
        part = pl.ds(k * rows, rows)
        placed = jnp.dot(put, panel_ref[part, :], preferred_element_type=F32).astype(BF16)
        for d in range(grids):
            firsts[d][pl.ds(span + k * rows, rows), :] = placed
        moved = jnp.dot(put, update_ref[part, :], preferred_element_type=F32).astype(BF16)
        d = jnp.bitwise_xor(owner_ref[dest_ref[mine * children + k]], mine)
        blocks_ref[rows_at(d, rows), :] = moved


def pack_body(grids, rows, base, plan_ref, blocks_ref, *refs):
    firsts, payloads = [*refs[grids - 2 : grids], *refs[: grids - 2]], refs[grids:]
    depth = firsts[0].shape[1]
    panel = payloads[0].shape[1]
    chunks = blocks_ref.shape[1] // panel
    for d in range(grids):
        piece = firsts[d][pl.ds(0, base), :]
        for payload in payloads:
            payload[pl.ds(0, base), pl.ds(d * depth, depth)] = piece
    for i, payload in enumerate(payloads):
        for half in range(2):
            for j in range(chunks):
                at = base + (half * chunks + j) * rows
                block = blocks_ref[pl.ds((2 * i + half) * rows, rows), pl.ds(j * panel, panel)]
                payload[pl.ds(at, rows), :] = block


def plan_body(cubes, grids, slots, owner_hbm, dest_hbm, out_ref, owner_ref, dest_ref, slot_ref, count_ref, sems):
    fetches = [
        pltpu.make_async_copy(owner_hbm, owner_ref, sems.at[0]),
        pltpu.make_async_copy(dest_hbm, dest_ref, sems.at[1]),
    ]
    for fetch in fetches:
        fetch.start()
    for fetch in fetches:
        fetch.wait()
    mine = lax.axis_index("cube")
    column = lax.axis_index("grid")
    blocks = owner_ref.shape[0]
    in_range = blocks // grids
    children = dest_ref.shape[0] // cubes
    none = grids * slots
    places = 2 * cubes + grids
    child_places = places + cubes * slots
    for r in range(grids):

        def count_own(i, seen):
            b = r * in_range + i
            own = owner_ref[b] == mine
            slot_ref[b] = jnp.where(own, r * slots + seen, none)
            return seen + own.astype(I32)

        out_ref[2 * cubes + r] = lax.fori_loop(0, in_range, count_own, I32(0), unroll=8)
    for d in range(cubes):
        source = jnp.bitwise_xor(mine, d)
        slot, which = I32(none), I32(0)
        for k in range(children):
            b = dest_ref[source * children + k]
            here = slot_ref[b]
            which = jnp.where(here < none, k, which)
            slot = jnp.minimum(slot, here)
            local_b = b - column * in_range
            inside = jnp.logical_and(local_b >= 0, local_b < in_range)
            out_ref[child_places + d * children + k] = jnp.where(inside, local_b, in_range)
        out_ref[d] = slot
        out_ref[cubes + d] = which
        count_ref[d] = 0
        for k in range(slots):
            out_ref[places + d * slots + k] = in_range

    def place(i, carry):
        d = jnp.bitwise_xor(owner_ref[column * in_range + i], mine)
        k = count_ref[d]
        out_ref[places + d * slots + k] = i
        count_ref[d] = k + 1
        return carry

    lax.fori_loop(0, in_range, place, 0, unroll=8)


def own_body(cubes, grids, span, rows, base, plan_ref, inverse_ref, mine_ref, full_ref, *refs):
    rests = refs[: grids - 1]
    entries_ref, factor_ref, turned_ref = refs[grids - 1 :]
    column = lax.axis_index("grid")
    depth = rests[0].shape[1]
    for d in range(grids):
        turned_ref[pl.ds(d * depth, depth), :] = inverse_ref[rows_at(jnp.bitwise_xor(column, d), depth), :]
    for e in range(grids):
        r = jnp.bitwise_xor(column, e)
        ids = lax.broadcasted_iota(I32, (span, depth), 0)
        live = ids < plan_ref[2 * cubes + r] * rows
        for d in range(grids):
            if e == 0:
                piece = mine_ref[pl.ds(0, span), pl.ds(d * depth, depth)]
            else:
                k = d ^ e
                at = (k if k < d else k - 1) * span
                if d == 1:
                    piece = full_ref[pl.ds(base + at, span), :]
                else:
                    piece = rests[max(d - 1, 0)][pl.ds(at, span), :]
            piece = jnp.where(live, piece.astype(F32), 0.0).astype(BF16)
            entries_ref[rows_at(r, span), pl.ds(d * depth, depth)] = piece
    factor_ref[...] = jnp.dot(entries_ref[...], turned_ref[...], preferred_element_type=F32).astype(BF16)


def join_body(*refs):
    pass


def add_children(cubes, grids, slots, rows, children, plan_ref, pieces, ranged, touched, total):
    span = slots * rows
    base = span + children * rows
    panel = ranged.shape[1]
    chunks = total.shape[1] // panel
    child_places = 2 * cubes + grids + cubes * slots
    in_range = ranged.shape[0] // rows - 1
    for d, piece in pieces.items():
        at = rows_at(plan_ref[d], rows)
        touched[at, :] += piece[rows_at(slots + plan_ref[cubes + d], rows), :].astype(F32)
        for j in range(chunks):
            part = pl.ds(base + ((d & 1) * chunks + j) * rows, rows)
            total[at, pl.ds(j * panel, panel)] += piece[part, :].astype(F32)
        for k in range(children):
            place = plan_ref[child_places + d * children + k]

            @pl.when(place < in_range)
            def _():
                ranged[rows_at(place, rows), :] += piece[pl.ds(span + k * rows, rows), :].astype(F32)


def early_body(cubes, grids, slots, rows, children, plan_ref, entries_ref, *refs):
    pieces = dict(enumerate(refs[:-3]))
    ranged, touched, total = refs[-3:]
    places = 2 * cubes + grids
    none = entries_ref.shape[0] // rows
    ranged[...] = jnp.zeros_like(ranged)
    total[...] = jnp.zeros_like(total)
    for d in range(cubes):
        slot = plan_ref[d]
        touched[rows_at(slot, rows), :] = entries_ref[rows_at(jnp.minimum(slot, none - 1), rows), :].astype(F32)
    for d, piece in pieces.items():
        for k in range(slots):
            at = rows_at(plan_ref[places + d * slots + k], rows)
            ranged[at, :] = piece[pl.ds(k * rows, rows), :].astype(F32)
    add_children(cubes, grids, slots, rows, children, plan_ref, pieces, ranged, touched, total)


def schur_body(cubes, grids, slots, rows, children, plan_ref, turned_ref, before_ref, *refs):
    pieces = {cubes - 2: refs[0], cubes - 1: refs[1]}
    out_ref, panel_ref, ranged, touched, total, few, factor_ref = refs[5:]
    column = lax.axis_index("grid")
    own_rows, width = out_ref.shape
    depth = panel_ref.shape[0]
    places = 2 * cubes + grids
    in_range = width // rows
    for d, piece in pieces.items():
        for k in range(slots):
            place = plan_ref[places + d * slots + k]

            @pl.when(place < in_range)
            def _():
                ranged[rows_at(place, rows), :] += piece[pl.ds(k * rows, rows), :].astype(F32)

    add_children(cubes, grids, slots, rows, children, plan_ref, pieces, ranged, touched, total)
    for d in range(cubes):
        few[pl.ds(d * rows, rows), :] = touched[rows_at(plan_ref[d], rows), :].astype(BF16)
    redone = jnp.dot(few[...], turned_ref[...], preferred_element_type=F32).astype(BF16)
    factor_ref[pl.ds(0, own_rows), :] = before_ref[...]
    for d in range(cubes):
        factor_ref[rows_at(plan_ref[d], rows), :] = redone[d * rows : (d + 1) * rows, :]
    column_factor = jnp.dot(
        ranged[pl.ds(0, width), :].astype(BF16), turned_ref[...], preferred_element_type=F32
    ).astype(BF16)
    product = lax.dot_general(
        factor_ref[pl.ds(0, own_rows), :], column_factor, (((1,), (1,)), ((), ())), preferred_element_type=F32
    )
    out_ref[...] = (total[pl.ds(0, own_rows), :] - product).astype(BF16)
    if depth % 128 == 0:
        cols = pl.ds(pl.multiple_of(column * depth, depth), depth)
        panel_ref[...] = factor_ref[pl.ds(0, own_rows), cols].astype(F32).T.astype(BF16)
    else:
        for r in range(grids):

            @pl.when(column == r)
            def _():
                part = factor_ref[pl.ds(0, own_rows), pl.ds(r * depth, depth)]
                panel_ref[...] = part.astype(F32).T.astype(BF16)


def local(
    child_update, child_panel, panel_entries, panel_inverse, block_owner, child_dest, child_rows
):
    cubes = lax.axis_size("cube")
    grids = lax.axis_size("grid")
    chips = cubes // 2
    children, rows = child_rows.shape
    width = child_update.shape[1]
    depth = child_panel.shape[0]
    panel = panel_inverse.shape[0]
    own_rows = panel_entries.shape[1]
    slots = own_rows // rows // grids
    span = slots * rows
    base = span + children * rows
    sent = base + 2 * rows * (width // panel)
    like = jax.ShapeDtypeStruct
    small = own_rows * width <= 512 * 512
    kept = pltpu.VMEM if small else like

    def in_hbm(x):
        return pltpu.with_memory_space_constraint(x, pltpu.HBM)

    def join(first, *others):
        if small:
            first, *others = (pltpu.with_memory_space_constraint(x, pltpu.VMEM) for x in (first, *others))
        return pl.pallas_call(
            join_body,
            out_shape=kept(first.shape, first.dtype),
            in_specs=[ANY] * (1 + len(others)),
            out_specs=ANY,
            input_output_aliases={0: 0},
        )(first, *others)

    def swap(x, axis, d):
        n = lax.axis_size(axis)
        return lax.ppermute(x, axis, [(i, i ^ d) for i in range(n)])

    rest_rows = (grids - 1) * span
    prepared = call(
        functools.partial(prepare_body, cubes, grids, span),
        [kept((base + (rest_rows if d == 1 else 0), depth), BF16) for d in range(grids)]
        + [kept((rest_rows, depth), BF16)] * (grids - 1)
        + [kept((cubes * rows, width), BF16)],
        [ANY] * 6,
        [
            pltpu.SMEM(block_owner.shape, I32),
            pltpu.SMEM(child_dest.shape, I32),
            pltpu.VMEM(child_rows.shape, I32),
            pltpu.VMEM(child_update.shape, BF16),
            pltpu.VMEM(child_panel.shape[::-1], BF16),
            pltpu.VMEM(panel_entries.shape, BF16),
            pltpu.VMEM(panel_entries.shape[::-1], BF16),
            pltpu.SemaphoreType.DMA((6,)),
        ],
        2 * rows * rows * children * (width + depth),
        4 * own_rows * depth,
        limit=28,
    )(*(in_hbm(x) for x in (block_owner, child_dest, child_rows, child_update, child_panel.T, panel_entries)))
    firsts, rests, blocks = list(prepared[:grids]), list(prepared[grids:-1]), prepared[-1]
    for d in [*range(2, grids), 1]:
        firsts[d] = swap(firsts[d], "grid", d)
    for d in range(2, grids):
        rests[d - 1] = swap(rests[d - 1], "grid", d)
    plan = call(
        functools.partial(plan_body, cubes, grids, slots),
        [pltpu.SMEM((2 * cubes + grids + cubes * (slots + children),), I32)],
        [ANY, ANY],
        [
            pltpu.SMEM(block_owner.shape, I32),
            pltpu.SMEM(child_dest.shape, I32),
            pltpu.SMEM(block_owner.shape, I32),
            pltpu.SMEM((cubes,), I32),
            pltpu.SemaphoreType.DMA((2,)),
        ],
        100000,
        6000000,
        [SMEM],
    )(in_hbm(block_owner), in_hbm(child_dest))[0]
    plan = pltpu.with_memory_space_constraint(plan, pltpu.SMEM)
    packed = call(
        functools.partial(pack_body, grids, rows, base),
        [kept((sent, panel), BF16)] * chips,
        [ANY] + [VMEM] * (1 + grids),
        [],
        1000,
        2 * chips * sent * panel,
    )(plan, blocks, *firsts[2:], *firsts[:2])
    arrived = [packed[0]] + [swap(packed[i], "cube", 2 * i) for i in range(1, chips)]
    entries, before, turned = call(
        functools.partial(own_body, cubes, grids, span, rows, base),
        [like((own_rows, panel), BF16), like((own_rows, panel), BF16), like((panel, panel), BF16)],
        [SMEM] + [VMEM] * (2 + grids),
        [],
        2 * own_rows * panel * panel,
        2 * (panel * panel + 2 * own_rows * panel),
    )(plan, panel_inverse, packed[0], firsts[1], *rests)
    arrived[-1] = join(arrived[-1], *rests[1:])
    pieces = []
    for piece in arrived:
        pieces += [piece, swap(piece, "cube", 1)]
    sizes = (cubes, grids, slots, rows, children)
    shapes = [(width + rows, panel), (own_rows + rows, panel), (own_rows + rows, width)]
    early = call(
        functools.partial(early_body, *sizes),
        [kept(shape, F32) for shape in shapes],
        [SMEM] + [VMEM] * (cubes - 1),
        [],
        1000,
        4 * width * panel,
        limit=16 if small else 56,
    )(plan, entries, *pieces[:-2])
    return tuple(
        call(
            functools.partial(schur_body, *sizes),
            [like((own_rows, width), BF16), like((depth, own_rows), BF16)] + [kept(shape, F32) for shape in shapes],
            [SMEM] + [VMEM] * 7,
            [pltpu.VMEM((cubes * rows, panel), BF16), pltpu.VMEM((own_rows + rows, panel), BF16)],
            2 * own_rows * width * panel,
            2 * (own_rows * width + (own_rows + cubes * span) * panel),
            limit=16 if small else 56,
            aliases={5: 2, 6: 3, 7: 4},
        )(plan, turned, before, *pieces[-2:], *early)[:2]
    )


def solution(mesh):
    placed = (
        P("cube", "grid"),
        P("grid", "cube"),
        P("grid", "cube"),
        P(),
        P(),
        P(),
        P("cube", None),
    )
    return jax.shard_map(
        local,
        mesh=mesh,
        in_specs=placed,
        out_specs=(P("cube", "grid"), P("grid", "cube")),
        check_vma=False,
    )
```

```python
import functools

import jax
import jax.numpy as jnp
from jax import lax
from jax.experimental import pallas as pl
from jax.experimental.pallas import tpu as pltpu
from jax.sharding import PartitionSpec as P

F32 = jnp.float32
BF16 = jnp.bfloat16
I32 = jnp.int32
VMEM = pl.BlockSpec(memory_space=pltpu.VMEM)
SMEM = pl.BlockSpec(memory_space=pltpu.SMEM)
ANY = pl.BlockSpec(memory_space=pl.ANY)
MIB = 1024 * 1024


def call(body, outs, in_specs, scratch, flops, moved, out_specs=None, limit=16, aliases={}):
    return pl.pallas_call(
        body,
        out_shape=outs,
        in_specs=in_specs,
        out_specs=[VMEM] * len(outs) if out_specs is None else out_specs,
        scratch_shapes=scratch,
        input_output_aliases=aliases,
        compiler_params=pltpu.CompilerParams(vmem_limit_bytes=limit * MIB),
        cost_estimate=pl.CostEstimate(flops=flops, bytes_accessed=moved, transcendentals=0),
    )


def rows_at(index, size):
    return pl.ds(pl.multiple_of(index * size, size), size)


def prepare_body(
    cubes, grids, span, owner_hbm, dest_hbm, rows_hbm, update_hbm, panel_hbm, entries_hbm, *refs
):
    firsts, rests, blocks_ref = refs[:grids], refs[grids : 2 * grids - 1], refs[2 * grids - 1]
    owner_ref, dest_ref, rows_ref, update_ref, panel_ref, entries_ref, flipped, sems = refs[2 * grids :]
    copies = [
        pltpu.make_async_copy(source, target, sems.at[i])
        for i, (source, target) in enumerate(
            (
                (entries_hbm, entries_ref),
                (panel_hbm, panel_ref),
                (rows_hbm, rows_ref),
                (update_hbm, update_ref),
                (owner_hbm, owner_ref),
                (dest_hbm, dest_ref),
            )
        )
    ]
    for copy in copies:
        copy.start()
    mine = lax.axis_index("cube")
    column = lax.axis_index("grid")
    children, rows = rows_ref.shape
    base = span + children * rows
    blocks_ref[...] = jnp.zeros_like(blocks_ref)
    copies[0].wait()
    flipped[...] = entries_ref[...].astype(F32).T.astype(BF16)
    for d in range(grids):
        piece = flipped[rows_at(jnp.bitwise_xor(column, d), span), :]
        firsts[d][pl.ds(0, span), :] = piece
        for e in range(grids):
            if e != d:
                k = d if d < e else d - 1
                if e == 1:
                    firsts[1][pl.ds(base + k * span, span), :] = piece
                else:
                    rests[max(e - 1, 0)][pl.ds(k * span, span), :] = piece
    for copy in copies[1:]:
        copy.wait()
    for k in range(children):
        want = rows_ref[k : k + 1, :]
        put = (lax.broadcasted_iota(I32, (rows, rows), 0) == want).astype(BF16)
        part = pl.ds(k * rows, rows)
        placed = jnp.dot(put, panel_ref[part, :], preferred_element_type=F32).astype(BF16)
        for d in range(grids):
            firsts[d][pl.ds(span + k * rows, rows), :] = placed
        moved = jnp.dot(put, update_ref[part, :], preferred_element_type=F32).astype(BF16)
        d = jnp.bitwise_xor(owner_ref[dest_ref[mine * children + k]], mine)
        blocks_ref[rows_at(d, rows), :] = moved


def pack_body(grids, rows, base, plan_ref, blocks_ref, *refs):
    firsts, payloads = [*refs[grids - 2 : grids], *refs[: grids - 2]], refs[grids:]
    depth = firsts[0].shape[1]
    panel = payloads[0].shape[1]
    chunks = blocks_ref.shape[1] // panel
    for d in range(grids):
        piece = firsts[d][pl.ds(0, base), :]
        for payload in payloads:
            payload[pl.ds(0, base), pl.ds(d * depth, depth)] = piece
    for i, payload in enumerate(payloads):
        for half in range(2):
            for j in range(chunks):
                at = base + (half * chunks + j) * rows
                block = blocks_ref[pl.ds((2 * i + half) * rows, rows), pl.ds(j * panel, panel)]
                payload[pl.ds(at, rows), :] = block


def plan_body(cubes, grids, slots, owner_hbm, dest_hbm, out_ref, owner_ref, dest_ref, slot_ref, count_ref, sems):
    fetches = [
        pltpu.make_async_copy(owner_hbm, owner_ref, sems.at[0]),
        pltpu.make_async_copy(dest_hbm, dest_ref, sems.at[1]),
    ]
    for fetch in fetches:
        fetch.start()
    for fetch in fetches:
        fetch.wait()
    mine = lax.axis_index("cube")
    column = lax.axis_index("grid")
    blocks = owner_ref.shape[0]
    in_range = blocks // grids
    children = dest_ref.shape[0] // cubes
    none = grids * slots
    places = 2 * cubes + grids
    child_places = places + cubes * slots
    for r in range(grids):

        def count_own(i, seen):
            b = r * in_range + i
            own = owner_ref[b] == mine
            slot_ref[b] = jnp.where(own, r * slots + seen, none)
            return seen + own.astype(I32)

        out_ref[2 * cubes + r] = lax.fori_loop(0, in_range, count_own, I32(0), unroll=8)
    for d in range(cubes):
        source = jnp.bitwise_xor(mine, d)
        slot, which = I32(none), I32(0)
        for k in range(children):
            b = dest_ref[source * children + k]
            here = slot_ref[b]
            which = jnp.where(here < none, k, which)
            slot = jnp.minimum(slot, here)
            local_b = b - column * in_range
            inside = jnp.logical_and(local_b >= 0, local_b < in_range)
            out_ref[child_places + d * children + k] = jnp.where(inside, local_b, in_range)
        out_ref[d] = slot
        out_ref[cubes + d] = which
        count_ref[d] = 0
        for k in range(slots):
            out_ref[places + d * slots + k] = in_range

    def place(i, carry):
        d = jnp.bitwise_xor(owner_ref[column * in_range + i], mine)
        k = count_ref[d]
        out_ref[places + d * slots + k] = i
        count_ref[d] = k + 1
        return carry

    lax.fori_loop(0, in_range, place, 0, unroll=8)


def own_body(cubes, grids, span, rows, base, plan_ref, inverse_ref, mine_ref, full_ref, *refs):
    rests = refs[: grids - 1]
    entries_ref, factor_ref, turned_ref = refs[grids - 1 :]
    column = lax.axis_index("grid")
    depth = rests[0].shape[1]
    for d in range(grids):
        turned_ref[pl.ds(d * depth, depth), :] = inverse_ref[rows_at(jnp.bitwise_xor(column, d), depth), :]
    for e in range(grids):
        r = jnp.bitwise_xor(column, e)
        ids = lax.broadcasted_iota(I32, (span, depth), 0)
        live = ids < plan_ref[2 * cubes + r] * rows
        for d in range(grids):
            if e == 0:
                piece = mine_ref[pl.ds(0, span), pl.ds(d * depth, depth)]
            else:
                k = d ^ e
                at = (k if k < d else k - 1) * span
                if d == 1:
                    piece = full_ref[pl.ds(base + at, span), :]
                else:
                    piece = rests[max(d - 1, 0)][pl.ds(at, span), :]
            piece = jnp.where(live, piece.astype(F32), 0.0).astype(BF16)
            entries_ref[rows_at(r, span), pl.ds(d * depth, depth)] = piece
    factor_ref[...] = jnp.dot(entries_ref[...], turned_ref[...], preferred_element_type=F32).astype(BF16)


def join_body(*refs):
    pass


def add_children(cubes, grids, slots, rows, children, plan_ref, pieces, ranged, touched, total):
    span = slots * rows
    base = span + children * rows
    panel = ranged.shape[1]
    chunks = total.shape[1] // panel
    child_places = 2 * cubes + grids + cubes * slots
    in_range = ranged.shape[0] // rows - 1
    for d, piece in pieces.items():
        at = rows_at(plan_ref[d], rows)
        touched[at, :] += piece[rows_at(slots + plan_ref[cubes + d], rows), :].astype(F32)
        for j in range(chunks):
            part = pl.ds(base + ((d & 1) * chunks + j) * rows, rows)
            total[at, pl.ds(j * panel, panel)] += piece[part, :].astype(F32)
        for k in range(children):
            place = plan_ref[child_places + d * children + k]

            @pl.when(place < in_range)
            def _():
                ranged[rows_at(place, rows), :] += piece[pl.ds(span + k * rows, rows), :].astype(F32)


def early_body(cubes, grids, slots, rows, children, plan_ref, entries_ref, *refs):
    pieces = dict(enumerate(refs[:-3]))
    ranged, touched, total = refs[-3:]
    places = 2 * cubes + grids
    none = entries_ref.shape[0] // rows
    ranged[...] = jnp.zeros_like(ranged)
    total[...] = jnp.zeros_like(total)
    for d in range(cubes):
        slot = plan_ref[d]
        touched[rows_at(slot, rows), :] = entries_ref[rows_at(jnp.minimum(slot, none - 1), rows), :].astype(F32)
    for d, piece in pieces.items():
        for k in range(slots):
            at = rows_at(plan_ref[places + d * slots + k], rows)
            ranged[at, :] = piece[pl.ds(k * rows, rows), :].astype(F32)
    add_children(cubes, grids, slots, rows, children, plan_ref, pieces, ranged, touched, total)


def schur_body(cubes, grids, slots, rows, children, plan_ref, turned_ref, before_ref, *refs):
    pieces = {cubes - 2: refs[0], cubes - 1: refs[1]}
    out_ref, panel_ref, ranged, touched, total, few, factor_ref = refs[5:]
    column = lax.axis_index("grid")
    own_rows, width = out_ref.shape
    depth = panel_ref.shape[0]
    places = 2 * cubes + grids
    in_range = width // rows
    for d, piece in pieces.items():
        for k in range(slots):
            place = plan_ref[places + d * slots + k]

            @pl.when(place < in_range)
            def _():
                ranged[rows_at(place, rows), :] += piece[pl.ds(k * rows, rows), :].astype(F32)

    add_children(cubes, grids, slots, rows, children, plan_ref, pieces, ranged, touched, total)
    for d in range(cubes):
        few[pl.ds(d * rows, rows), :] = touched[rows_at(plan_ref[d], rows), :].astype(BF16)
    redone = jnp.dot(few[...], turned_ref[...], preferred_element_type=F32).astype(BF16)
    factor_ref[pl.ds(0, own_rows), :] = before_ref[...]
    for d in range(cubes):
        factor_ref[rows_at(plan_ref[d], rows), :] = redone[d * rows : (d + 1) * rows, :]
    column_factor = jnp.dot(
        ranged[pl.ds(0, width), :].astype(BF16), turned_ref[...], preferred_element_type=F32
    ).astype(BF16)
    product = lax.dot_general(
        factor_ref[pl.ds(0, own_rows), :], column_factor, (((1,), (1,)), ((), ())), preferred_element_type=F32
    )
    out_ref[...] = (total[pl.ds(0, own_rows), :] - product).astype(BF16)
    if depth % 128 == 0:
        cols = pl.ds(pl.multiple_of(column * depth, depth), depth)
        panel_ref[...] = factor_ref[pl.ds(0, own_rows), cols].astype(F32).T.astype(BF16)
    else:
        for r in range(grids):

            @pl.when(column == r)
            def _():
                part = factor_ref[pl.ds(0, own_rows), pl.ds(r * depth, depth)]
                panel_ref[...] = part.astype(F32).T.astype(BF16)


def local(
    child_update, child_panel, panel_entries, panel_inverse, block_owner, child_dest, child_rows
):
    cubes = lax.axis_size("cube")
    grids = lax.axis_size("grid")
    chips = cubes // 2
    children, rows = child_rows.shape
    width = child_update.shape[1]
    depth = child_panel.shape[0]
    panel = panel_inverse.shape[0]
    own_rows = panel_entries.shape[1]
    slots = own_rows // rows // grids
    span = slots * rows
    base = span + children * rows
    sent = base + 2 * rows * (width // panel)
    like = jax.ShapeDtypeStruct
    small = own_rows * width <= 512 * 512
    kept = pltpu.VMEM if small else like

    def in_hbm(x):
        return pltpu.with_memory_space_constraint(x, pltpu.HBM)

    def join(first, *others):
        if small:
            first, *others = (
                pltpu.with_memory_space_constraint(x, pltpu.SMEM if x.dtype == I32 else pltpu.VMEM)
                for x in (first, *others)
            )
        return pl.pallas_call(
            join_body,
            out_shape=kept(first.shape, first.dtype),
            in_specs=[ANY] * (1 + len(others)),
            out_specs=ANY,
            input_output_aliases={0: 0},
        )(first, *others)

    def swap(x, axis, d):
        n = lax.axis_size(axis)
        return lax.ppermute(x, axis, [(i, i ^ d) for i in range(n)])

    rest_rows = (grids - 1) * span
    prepared = call(
        functools.partial(prepare_body, cubes, grids, span),
        [kept((base + (rest_rows if d == 1 else 0), depth), BF16) for d in range(grids)]
        + [kept((rest_rows, depth), BF16)] * (grids - 1)
        + [kept((cubes * rows, width), BF16)],
        [ANY] * 6,
        [
            pltpu.SMEM(block_owner.shape, I32),
            pltpu.SMEM(child_dest.shape, I32),
            pltpu.VMEM(child_rows.shape, I32),
            pltpu.VMEM(child_update.shape, BF16),
            pltpu.VMEM(child_panel.shape[::-1], BF16),
            pltpu.VMEM(panel_entries.shape, BF16),
            pltpu.VMEM(panel_entries.shape[::-1], BF16),
            pltpu.SemaphoreType.DMA((6,)),
        ],
        2 * rows * rows * children * (width + depth),
        4 * own_rows * depth,
        limit=28,
    )(*(in_hbm(x) for x in (block_owner, child_dest, child_rows, child_update, child_panel.T, panel_entries)))
    firsts, rests, blocks = list(prepared[:grids]), list(prepared[grids:-1]), prepared[-1]
    for d in [*range(2, grids), 1]:
        firsts[d] = swap(firsts[d], "grid", d)
    plan = call(
        functools.partial(plan_body, cubes, grids, slots),
        [pltpu.SMEM((2 * cubes + grids + cubes * (slots + children),), I32)],
        [ANY, ANY],
        [
            pltpu.SMEM(block_owner.shape, I32),
            pltpu.SMEM(child_dest.shape, I32),
            pltpu.SMEM(block_owner.shape, I32),
            pltpu.SMEM((cubes,), I32),
            pltpu.SemaphoreType.DMA((2,)),
        ],
        100000,
        6000000,
        [SMEM],
    )(in_hbm(block_owner), in_hbm(child_dest))[0]
    for d in range(2, grids):
        rests[d - 1] = swap(join(rests[d - 1], plan), "grid", d)
    plan = pltpu.with_memory_space_constraint(plan, pltpu.SMEM)
    packed = call(
        functools.partial(pack_body, grids, rows, base),
        [kept((sent, panel), BF16)] * chips,
        [ANY] + [VMEM] * (1 + grids),
        [],
        1000,
        2 * chips * sent * panel,
    )(plan, blocks, *firsts[2:], *firsts[:2])
    arrived = [packed[0]] + [swap(packed[i], "cube", 2 * i) for i in range(1, chips)]
    entries, before, turned = call(
        functools.partial(own_body, cubes, grids, span, rows, base),
        [like((own_rows, panel), BF16), like((own_rows, panel), BF16), like((panel, panel), BF16)],
        [SMEM] + [VMEM] * (2 + grids),
        [],
        1650000000,
        2 * own_rows * panel * panel,
    )(plan, panel_inverse, packed[0], firsts[1], *rests)
    arrived[1] = join(arrived[1], turned)
    pieces = []
    for piece in arrived:
        pieces += [piece, swap(piece, "cube", 1)]
    sizes = (cubes, grids, slots, rows, children)
    shapes = [(width + rows, panel), (own_rows + rows, panel), (own_rows + rows, width)]
    early = call(
        functools.partial(early_body, *sizes),
        [kept(shape, F32) for shape in shapes],
        [SMEM] + [VMEM] * (cubes - 1),
        [],
        1000,
        4 * width * panel,
        limit=16 if small else 56,
    )(plan, entries, *pieces[:-2])
    return tuple(
        call(
            functools.partial(schur_body, *sizes),
            [like((own_rows, width), BF16), like((depth, own_rows), BF16)] + [kept(shape, F32) for shape in shapes],
            [SMEM] + [VMEM] * 7,
            [pltpu.VMEM((cubes * rows, panel), BF16), pltpu.VMEM((own_rows + rows, panel), BF16)],
            2 * own_rows * width * panel,
            2 * (own_rows * width + (own_rows + cubes * span) * panel),
            limit=16 if small else 56,
            aliases={5: 2, 6: 3, 7: 4},
        )(plan, turned, before, *pieces[-2:], *early)[:2]
    )


def solution(mesh):
    placed = (
        P("cube", "grid"),
        P("grid", "cube"),
        P("grid", "cube"),
        P(),
        P(),
        P(),
        P("cube", None),
    )
    return jax.shard_map(
        local,
        mesh=mesh,
        in_specs=placed,
        out_specs=(P("cube", "grid"), P("grid", "cube")),
        check_vma=False,
    )
```

```python
import functools

import jax
import jax.numpy as jnp
from jax import lax
from jax.experimental import pallas as pl
from jax.experimental.pallas import tpu as pltpu
from jax.sharding import PartitionSpec as P

F32 = jnp.float32
BF16 = jnp.bfloat16
I32 = jnp.int32
VMEM = pl.BlockSpec(memory_space=pltpu.VMEM)
SMEM = pl.BlockSpec(memory_space=pltpu.SMEM)
ANY = pl.BlockSpec(memory_space=pl.ANY)
MIB = 1024 * 1024
PACK_COST = 1500000000


def call(body, outs, in_specs, scratch, flops, moved, out_specs=None, limit=16, aliases={}):
    return pl.pallas_call(
        body,
        out_shape=outs,
        in_specs=in_specs,
        out_specs=[VMEM] * len(outs) if out_specs is None else out_specs,
        scratch_shapes=scratch,
        input_output_aliases=aliases,
        compiler_params=pltpu.CompilerParams(vmem_limit_bytes=limit * MIB),
        cost_estimate=pl.CostEstimate(flops=flops, bytes_accessed=moved, transcendentals=0),
    )


def rows_at(index, size):
    return pl.ds(pl.multiple_of(index * size, size), size)


def prepare_body(
    cubes, grids, span, owner_hbm, dest_hbm, rows_hbm, update_hbm, panel_hbm, entries_hbm, inverse_hbm, *refs
):
    firsts, rests, blocks_ref, turned_ref = refs[:grids], refs[grids : 2 * grids - 1], *refs[2 * grids - 1 : 2 * grids + 1]
    owner_ref, dest_ref, rows_ref, update_ref, panel_ref, entries_ref, flipped, sems = refs[2 * grids + 1 :]
    copies = [
        pltpu.make_async_copy(source, target, sems.at[i])
        for i, (source, target) in enumerate(
            (
                (entries_hbm, entries_ref),
                (panel_hbm, panel_ref),
                (rows_hbm, rows_ref),
                (update_hbm, update_ref),
                (owner_hbm, owner_ref),
                (dest_hbm, dest_ref),
            )
        )
    ]
    mine = lax.axis_index("cube")
    column = lax.axis_index("grid")
    depth = entries_ref.shape[0]
    for d in range(grids):
        part = inverse_hbm.at[rows_at(jnp.bitwise_xor(column, d), depth), :]
        copies.append(pltpu.make_async_copy(part, turned_ref.at[pl.ds(d * depth, depth), :], sems.at[6 + d]))
    for copy in copies:
        copy.start()
    children, rows = rows_ref.shape
    base = span + children * rows
    blocks_ref[...] = jnp.zeros_like(blocks_ref)
    copies[0].wait()
    flipped[...] = entries_ref[...].astype(F32).T.astype(BF16)
    for d in range(grids):
        piece = flipped[rows_at(jnp.bitwise_xor(column, d), span), :]
        firsts[d][pl.ds(0, span), :] = piece
        for e in range(grids):
            if e != d:
                k = d if d < e else d - 1
                if e == 1:
                    firsts[1][pl.ds(base + k * span, span), :] = piece
                else:
                    rests[max(e - 1, 0)][pl.ds(k * span, span), :] = piece
    for copy in copies[1:6]:
        copy.wait()
    for k in range(children):
        want = rows_ref[k : k + 1, :]
        put = (lax.broadcasted_iota(I32, (rows, rows), 0) == want).astype(BF16)
        part = pl.ds(k * rows, rows)
        placed = jnp.dot(put, panel_ref[part, :], preferred_element_type=F32).astype(BF16)
        for d in range(grids):
            firsts[d][pl.ds(span + k * rows, rows), :] = placed
        moved = jnp.dot(put, update_ref[part, :], preferred_element_type=F32).astype(BF16)
        d = jnp.bitwise_xor(owner_ref[dest_ref[mine * children + k]], mine)
        blocks_ref[rows_at(d, rows), :] = moved
    for copy in copies[6:]:
        copy.wait()


def pack_body(parts, rows, base, blocks_ref, *refs):
    firsts, payloads = refs[: len(parts)], refs[len(parts) :]
    depth = firsts[0].shape[1]
    panel = payloads[0].shape[1]
    chunks = blocks_ref.shape[1] // panel
    for d, first in zip(parts, firsts):
        piece = first[...]
        for payload in payloads:
            payload[pl.ds(0, base), pl.ds(d * depth, depth)] = piece
    for i, payload in enumerate(payloads):
        for half in range(2):
            for j in range(chunks):
                at = base + (half * chunks + j) * rows
                block = blocks_ref[pl.ds((2 * i + half) * rows, rows), pl.ds(j * panel, panel)]
                payload[pl.ds(at, rows), :] = block


def complete_body(base, plan_ref, first_ref, *refs):
    depth = first_ref.shape[1]
    piece = first_ref[pl.ds(0, base), :]
    for payload in refs[len(refs) // 2 :]:
        payload[pl.ds(0, base), pl.ds(depth, depth)] = piece


def plan_body(cubes, grids, slots, owner_hbm, dest_hbm, out_ref, owner_ref, dest_ref, slot_ref, count_ref, sems):
    fetches = [
        pltpu.make_async_copy(owner_hbm, owner_ref, sems.at[0]),
        pltpu.make_async_copy(dest_hbm, dest_ref, sems.at[1]),
    ]
    for fetch in fetches:
        fetch.start()
    for fetch in fetches:
        fetch.wait()
    mine = lax.axis_index("cube")
    column = lax.axis_index("grid")
    blocks = owner_ref.shape[0]
    in_range = blocks // grids
    children = dest_ref.shape[0] // cubes
    none = grids * slots
    places = 2 * cubes + grids
    child_places = places + cubes * slots
    for r in range(grids):

        def count_own(i, seen):
            b = r * in_range + i
            own = owner_ref[b] == mine
            slot_ref[b] = jnp.where(own, r * slots + seen, none)
            return seen + own.astype(I32)

        out_ref[2 * cubes + r] = lax.fori_loop(0, in_range, count_own, I32(0), unroll=8)
    for d in range(cubes):
        source = jnp.bitwise_xor(mine, d)
        slot, which = I32(none), I32(0)
        for k in range(children):
            b = dest_ref[source * children + k]
            here = slot_ref[b]
            which = jnp.where(here < none, k, which)
            slot = jnp.minimum(slot, here)
            local_b = b - column * in_range
            inside = jnp.logical_and(local_b >= 0, local_b < in_range)
            out_ref[child_places + d * children + k] = jnp.where(inside, local_b, in_range)
        out_ref[d] = slot
        out_ref[cubes + d] = which
        count_ref[d] = 0
        for k in range(slots):
            out_ref[places + d * slots + k] = in_range

    def place(i, carry):
        d = jnp.bitwise_xor(owner_ref[column * in_range + i], mine)
        k = count_ref[d]
        out_ref[places + d * slots + k] = i
        count_ref[d] = k + 1
        return carry

    lax.fori_loop(0, in_range, place, 0, unroll=8)


def own_body(cubes, grids, span, rows, base, plan_ref, turned_ref, mine_ref, full_ref, *refs):
    rests = refs[: grids - 1]
    entries_ref, factor_ref = refs[grids - 1 :]
    column = lax.axis_index("grid")
    depth = rests[0].shape[1]
    for e in range(grids):
        r = jnp.bitwise_xor(column, e)
        ids = lax.broadcasted_iota(I32, (span, depth), 0)
        live = ids < plan_ref[2 * cubes + r] * rows
        for d in range(grids):
            if e == 0:
                piece = mine_ref[pl.ds(0, span), pl.ds(d * depth, depth)]
            else:
                k = d ^ e
                at = (k if k < d else k - 1) * span
                if d == 1:
                    piece = full_ref[pl.ds(base + at, span), :]
                else:
                    piece = rests[max(d - 1, 0)][pl.ds(at, span), :]
            piece = jnp.where(live, piece.astype(F32), 0.0).astype(BF16)
            entries_ref[rows_at(r, span), pl.ds(d * depth, depth)] = piece
    factor_ref[...] = jnp.dot(entries_ref[...], turned_ref[...], preferred_element_type=F32).astype(BF16)


def join_body(*refs):
    pass


def add_children(cubes, grids, slots, rows, children, plan_ref, pieces, ranged, touched, total):
    span = slots * rows
    base = span + children * rows
    panel = ranged.shape[1]
    chunks = total.shape[1] // panel
    child_places = 2 * cubes + grids + cubes * slots
    in_range = ranged.shape[0] // rows - 1
    for d, piece in pieces.items():
        at = rows_at(plan_ref[d], rows)
        touched[at, :] += piece[rows_at(slots + plan_ref[cubes + d], rows), :].astype(F32)
        for j in range(chunks):
            part = pl.ds(base + ((d & 1) * chunks + j) * rows, rows)
            total[at, pl.ds(j * panel, panel)] += piece[part, :].astype(F32)
        for k in range(children):
            place = plan_ref[child_places + d * children + k]

            @pl.when(place < in_range)
            def _():
                ranged[rows_at(place, rows), :] += piece[pl.ds(span + k * rows, rows), :].astype(F32)


def early_body(cubes, grids, slots, rows, children, plan_ref, entries_ref, *refs):
    pieces = dict(enumerate(refs[:-3]))
    ranged, touched, total = refs[-3:]
    places = 2 * cubes + grids
    none = entries_ref.shape[0] // rows
    ranged[...] = jnp.zeros_like(ranged)
    total[...] = jnp.zeros_like(total)
    for d in range(cubes):
        slot = plan_ref[d]
        touched[rows_at(slot, rows), :] = entries_ref[rows_at(jnp.minimum(slot, none - 1), rows), :].astype(F32)
    for d, piece in pieces.items():
        for k in range(slots):
            at = rows_at(plan_ref[places + d * slots + k], rows)
            ranged[at, :] = piece[pl.ds(k * rows, rows), :].astype(F32)
    add_children(cubes, grids, slots, rows, children, plan_ref, pieces, ranged, touched, total)


def schur_body(cubes, grids, slots, rows, children, plan_ref, turned_ref, before_ref, *refs):
    pieces = {cubes - 2: refs[0], cubes - 1: refs[1]}
    out_ref, panel_ref, ranged, touched, total, few, factor_ref = refs[5:]
    column = lax.axis_index("grid")
    own_rows, width = out_ref.shape
    depth = panel_ref.shape[0]
    places = 2 * cubes + grids
    in_range = width // rows
    for d, piece in pieces.items():
        for k in range(slots):
            place = plan_ref[places + d * slots + k]

            @pl.when(place < in_range)
            def _():
                ranged[rows_at(place, rows), :] += piece[pl.ds(k * rows, rows), :].astype(F32)

    add_children(cubes, grids, slots, rows, children, plan_ref, pieces, ranged, touched, total)
    for d in range(cubes):
        few[pl.ds(d * rows, rows), :] = touched[rows_at(plan_ref[d], rows), :].astype(BF16)
    redone = jnp.dot(few[...], turned_ref[...], preferred_element_type=F32).astype(BF16)
    factor_ref[pl.ds(0, own_rows), :] = before_ref[...]
    for d in range(cubes):
        factor_ref[rows_at(plan_ref[d], rows), :] = redone[d * rows : (d + 1) * rows, :]
    column_factor = jnp.dot(
        ranged[pl.ds(0, width), :].astype(BF16), turned_ref[...], preferred_element_type=F32
    ).astype(BF16)
    product = lax.dot_general(
        factor_ref[pl.ds(0, own_rows), :], column_factor, (((1,), (1,)), ((), ())), preferred_element_type=F32
    )
    out_ref[...] = (total[pl.ds(0, own_rows), :] - product).astype(BF16)
    if depth % 128 == 0:
        cols = pl.ds(pl.multiple_of(column * depth, depth), depth)
        panel_ref[...] = factor_ref[pl.ds(0, own_rows), cols].astype(F32).T.astype(BF16)
    else:
        for r in range(grids):

            @pl.when(column == r)
            def _():
                part = factor_ref[pl.ds(0, own_rows), pl.ds(r * depth, depth)]
                panel_ref[...] = part.astype(F32).T.astype(BF16)


def local(
    child_update, child_panel, panel_entries, panel_inverse, block_owner, child_dest, child_rows
):
    cubes = lax.axis_size("cube")
    grids = lax.axis_size("grid")
    chips = cubes // 2
    children, rows = child_rows.shape
    width = child_update.shape[1]
    depth = child_panel.shape[0]
    panel = panel_inverse.shape[0]
    own_rows = panel_entries.shape[1]
    slots = own_rows // rows // grids
    span = slots * rows
    base = span + children * rows
    sent = base + 2 * rows * (width // panel)
    like = jax.ShapeDtypeStruct
    small = own_rows * width <= 512 * 512
    kept = pltpu.VMEM if small else like

    def in_hbm(x):
        return pltpu.with_memory_space_constraint(x, pltpu.HBM)

    def join(first, *others):
        if small:
            first, *others = (
                pltpu.with_memory_space_constraint(x, pltpu.SMEM if x.dtype == I32 else pltpu.VMEM)
                for x in (first, *others)
            )
        return pl.pallas_call(
            join_body,
            out_shape=kept(first.shape, first.dtype),
            in_specs=[ANY] * (1 + len(others)),
            out_specs=ANY,
            input_output_aliases={0: 0},
        )(first, *others)

    def swap(x, axis, d):
        n = lax.axis_size(axis)
        return lax.ppermute(x, axis, [(i, i ^ d) for i in range(n)])

    rest_rows = (grids - 1) * span
    prepared = call(
        functools.partial(prepare_body, cubes, grids, span),
        [kept((base + (rest_rows if d == 1 else 0), depth), BF16) for d in range(grids)]
        + [kept((rest_rows, depth), BF16)] * (grids - 1)
        + [kept((cubes * rows, width), BF16), kept((panel, panel), BF16)],
        [ANY] * 7,
        [
            pltpu.SMEM(block_owner.shape, I32),
            pltpu.SMEM(child_dest.shape, I32),
            pltpu.VMEM(child_rows.shape, I32),
            pltpu.VMEM(child_update.shape, BF16),
            pltpu.VMEM(child_panel.shape[::-1], BF16),
            pltpu.VMEM(panel_entries.shape, BF16),
            pltpu.VMEM(panel_entries.shape[::-1], BF16),
            pltpu.SemaphoreType.DMA((6 + grids,)),
        ],
        2 * rows * rows * children * (width + depth),
        4 * own_rows * depth,
        limit=28,
    )(*(in_hbm(x) for x in (block_owner, child_dest, child_rows, child_update, child_panel.T, panel_entries, panel_inverse)))
    firsts, rests = list(prepared[:grids]), list(prepared[grids:-2])
    blocks, turned = prepared[-2:]
    for d in [*range(2, grids), 1]:
        firsts[d] = swap(firsts[d], "grid", d)
    plan = call(
        functools.partial(plan_body, cubes, grids, slots),
        [pltpu.SMEM((2 * cubes + grids + cubes * (slots + children),), I32)],
        [ANY, ANY],
        [
            pltpu.SMEM(block_owner.shape, I32),
            pltpu.SMEM(child_dest.shape, I32),
            pltpu.SMEM(block_owner.shape, I32),
            pltpu.SMEM((cubes,), I32),
            pltpu.SemaphoreType.DMA((2,)),
        ],
        100000,
        6000000,
        [SMEM],
    )(in_hbm(block_owner), in_hbm(child_dest))[0]
    for d in range(2, grids):
        rests[d - 1] = swap(join(rests[d - 1], plan), "grid", d)
    plan = pltpu.with_memory_space_constraint(plan, pltpu.SMEM)
    parts = [*range(2, grids), 0]
    packed = call(
        functools.partial(pack_body, parts, rows, base),
        [kept((sent, panel), BF16)] * chips,
        [VMEM] * (1 + len(parts)),
        [],
        PACK_COST,
        2 * chips * sent * panel,
    )(blocks, *(firsts[d] for d in parts))
    packed = call(
        functools.partial(complete_body, base),
        [kept((sent, panel), BF16)] * chips,
        [ANY] + [VMEM] * (1 + chips),
        [],
        1000,
        2 * chips * base * depth,
        aliases={2 + i: i for i in range(chips)},
    )(plan, firsts[1], *packed)
    arrived = [packed[0]] + [swap(packed[i], "cube", 2 * i) for i in range(1, chips)]
    entries, before = call(
        functools.partial(own_body, cubes, grids, span, rows, base),
        [kept((own_rows, panel), BF16), kept((own_rows, panel), BF16)],
        [SMEM] + [VMEM] * (2 + grids),
        [],
        1650000000,
        2 * own_rows * panel * panel,
    )(plan, turned, packed[0], firsts[1], *rests)
    arrived[1] = join(arrived[1], before)
    pieces = []
    for piece in arrived:
        pieces += [piece, swap(piece, "cube", 1)]
    sizes = (cubes, grids, slots, rows, children)
    shapes = [(width + rows, panel), (own_rows + rows, panel), (own_rows + rows, width)]
    early = call(
        functools.partial(early_body, *sizes),
        [kept(shape, F32) for shape in shapes],
        [SMEM] + [VMEM] * (cubes - 1),
        [],
        1000,
        4 * width * panel,
        limit=16 if small else 56,
    )(plan, entries, *pieces[:-2])
    return tuple(
        call(
            functools.partial(schur_body, *sizes),
            [like((own_rows, width), BF16), like((depth, own_rows), BF16)] + [kept(shape, F32) for shape in shapes],
            [SMEM] + [VMEM] * 7,
            [pltpu.VMEM((cubes * rows, panel), BF16), pltpu.VMEM((own_rows + rows, panel), BF16)],
            2 * own_rows * width * panel,
            2 * (own_rows * width + (own_rows + cubes * span) * panel),
            limit=16 if small else 56,
            aliases={5: 2, 6: 3, 7: 4},
        )(plan, turned, before, *pieces[-2:], *early)[:2]
    )


def solution(mesh):
    placed = (
        P("cube", "grid"),
        P("grid", "cube"),
        P("grid", "cube"),
        P(),
        P(),
        P(),
        P("cube", None),
    )
    return jax.shard_map(
        local,
        mesh=mesh,
        in_specs=placed,
        out_specs=(P("cube", "grid"), P("grid", "cube")),
        check_vma=False,
    )
```

```python
import functools

import jax
import jax.numpy as jnp
from jax import lax
from jax.experimental import pallas as pl
from jax.experimental.pallas import tpu as pltpu
from jax.sharding import PartitionSpec as P

F32 = jnp.float32
BF16 = jnp.bfloat16
I32 = jnp.int32
VMEM = pl.BlockSpec(memory_space=pltpu.VMEM)
SMEM = pl.BlockSpec(memory_space=pltpu.SMEM)
ANY = pl.BlockSpec(memory_space=pl.ANY)
MIB = 1024 * 1024


def call(body, outs, in_specs, scratch, flops, moved, out_specs=None, limit=16, aliases={}):
    return pl.pallas_call(
        body,
        out_shape=outs,
        in_specs=in_specs,
        out_specs=[VMEM] * len(outs) if out_specs is None else out_specs,
        scratch_shapes=scratch,
        input_output_aliases=aliases,
        compiler_params=pltpu.CompilerParams(vmem_limit_bytes=limit * MIB),
        cost_estimate=pl.CostEstimate(flops=flops, bytes_accessed=moved, transcendentals=0),
    )


def rows_at(index, size):
    return pl.ds(pl.multiple_of(index * size, size), size)


def prepare_body(
    cubes, grids, span, owner_hbm, dest_hbm, rows_hbm, update_hbm, panel_hbm, entries_hbm, inverse_hbm, *refs
):
    firsts, rests, blocks_ref, turned_ref = refs[:grids], refs[grids : 2 * grids], *refs[2 * grids : 2 * grids + 2]
    owner_ref, dest_ref, rows_ref, update_ref, panel_ref, entries_ref, flipped, sems = refs[2 * grids + 2 :]
    copies = [
        pltpu.make_async_copy(source, target, sems.at[i])
        for i, (source, target) in enumerate(
            (
                (entries_hbm, entries_ref),
                (panel_hbm, panel_ref),
                (rows_hbm, rows_ref),
                (update_hbm, update_ref),
                (owner_hbm, owner_ref),
                (dest_hbm, dest_ref),
            )
        )
    ]
    mine = lax.axis_index("cube")
    column = lax.axis_index("grid")
    depth = entries_ref.shape[0]
    for d in range(grids):
        part = inverse_hbm.at[rows_at(jnp.bitwise_xor(column, d), depth), :]
        copies.append(pltpu.make_async_copy(part, turned_ref.at[pl.ds(d * depth, depth), :], sems.at[6 + d]))
    for copy in copies:
        copy.start()
    children, rows = rows_ref.shape
    blocks_ref[...] = jnp.zeros_like(blocks_ref)
    copies[0].wait()
    flipped[...] = entries_ref[...].astype(F32).T.astype(BF16)
    for d in range(grids):
        piece = flipped[rows_at(jnp.bitwise_xor(column, d), span), :]
        firsts[d][pl.ds(0, span), :] = piece
        for e in range(grids):
            if e != d:
                k = d if d < e else d - 1
                rests[e][pl.ds(k * span, span), :] = piece
    for copy in copies[1:6]:
        copy.wait()
    for k in range(children):
        want = rows_ref[k : k + 1, :]
        put = (lax.broadcasted_iota(I32, (rows, rows), 0) == want).astype(BF16)
        part = pl.ds(k * rows, rows)
        placed = jnp.dot(put, panel_ref[part, :], preferred_element_type=F32).astype(BF16)
        for d in range(grids):
            firsts[d][pl.ds(span + k * rows, rows), :] = placed
        moved = jnp.dot(put, update_ref[part, :], preferred_element_type=F32).astype(BF16)
        d = jnp.bitwise_xor(owner_ref[dest_ref[mine * children + k]], mine)
        blocks_ref[rows_at(d, rows), :] = moved
    for copy in copies[6:]:
        copy.wait()


def pack_body(parts, rows, base, blocks_ref, *refs):
    firsts, payloads = refs[: len(parts)], refs[len(parts) :]
    depth = firsts[0].shape[1]
    panel = payloads[0].shape[1]
    chunks = blocks_ref.shape[1] // panel
    for d, first in zip(parts, firsts):
        piece = first[...]
        for payload in payloads:
            payload[pl.ds(0, base), pl.ds(d * depth, depth)] = piece
    for i, payload in enumerate(payloads):
        for half in range(2):
            for j in range(chunks):
                at = base + (half * chunks + j) * rows
                block = blocks_ref[pl.ds((2 * i + half) * rows, rows), pl.ds(j * panel, panel)]
                payload[pl.ds(at, rows), :] = block


def plan_body(cubes, grids, slots, owner_hbm, dest_hbm, out_ref, owner_ref, dest_ref, slot_ref, count_ref, sems):
    fetches = [
        pltpu.make_async_copy(owner_hbm, owner_ref, sems.at[0]),
        pltpu.make_async_copy(dest_hbm, dest_ref, sems.at[1]),
    ]
    for fetch in fetches:
        fetch.start()
    for fetch in fetches:
        fetch.wait()
    mine = lax.axis_index("cube")
    column = lax.axis_index("grid")
    blocks = owner_ref.shape[0]
    in_range = blocks // grids
    children = dest_ref.shape[0] // cubes
    none = grids * slots
    places = 2 * cubes + grids
    child_places = places + cubes * slots
    for r in range(grids):

        def count_own(i, seen):
            b = r * in_range + i
            own = owner_ref[b] == mine
            slot_ref[b] = jnp.where(own, r * slots + seen, none)
            return seen + own.astype(I32)

        out_ref[2 * cubes + r] = lax.fori_loop(0, in_range, count_own, I32(0), unroll=8)
    for d in range(cubes):
        source = jnp.bitwise_xor(mine, d)
        slot, which = I32(none), I32(0)
        for k in range(children):
            b = dest_ref[source * children + k]
            here = slot_ref[b]
            which = jnp.where(here < none, k, which)
            slot = jnp.minimum(slot, here)
            local_b = b - column * in_range
            inside = jnp.logical_and(local_b >= 0, local_b < in_range)
            out_ref[child_places + d * children + k] = jnp.where(inside, local_b, in_range)
        out_ref[d] = slot
        out_ref[cubes + d] = which
        count_ref[d] = 0
        for k in range(slots):
            out_ref[places + d * slots + k] = in_range

    def place(i, carry):
        d = jnp.bitwise_xor(owner_ref[column * in_range + i], mine)
        k = count_ref[d]
        out_ref[places + d * slots + k] = i
        count_ref[d] = k + 1
        return carry

    lax.fori_loop(0, in_range, place, 0, unroll=8)


def own_body(cubes, grids, span, rows, plan_ref, turned_ref, mine_ref, *refs):
    rests = refs[:grids]
    entries_ref, factor_ref = refs[grids:]
    column = lax.axis_index("grid")
    depth = rests[0].shape[1]
    for e in range(grids):
        r = jnp.bitwise_xor(column, e)
        ids = lax.broadcasted_iota(I32, (span, depth), 0)
        live = ids < plan_ref[2 * cubes + r] * rows
        for d in range(grids):
            if e == 0:
                piece = mine_ref[pl.ds(0, span), pl.ds(d * depth, depth)]
            else:
                k = d ^ e
                at = (k if k < d else k - 1) * span
                piece = rests[d][pl.ds(at, span), :]
            piece = jnp.where(live, piece.astype(F32), 0.0).astype(BF16)
            entries_ref[rows_at(r, span), pl.ds(d * depth, depth)] = piece
    factor_ref[...] = jnp.dot(entries_ref[...], turned_ref[...], preferred_element_type=F32).astype(BF16)


def marker_body(after_ref, out_ref):
    out_ref[...] = jnp.zeros_like(out_ref)


def join_body(*refs):
    pass


def add_children(cubes, grids, slots, rows, children, plan_ref, pieces, ranged, touched, total):
    span = slots * rows
    base = span + children * rows
    panel = ranged.shape[1]
    chunks = total.shape[1] // panel
    child_places = 2 * cubes + grids + cubes * slots
    in_range = ranged.shape[0] // rows - 1
    for d, piece in pieces.items():
        at = rows_at(plan_ref[d], rows)
        touched[at, :] += piece[rows_at(slots + plan_ref[cubes + d], rows), :].astype(F32)
        for j in range(chunks):
            part = pl.ds(base + ((d & 1) * chunks + j) * rows, rows)
            total[at, pl.ds(j * panel, panel)] += piece[part, :].astype(F32)
        for k in range(children):
            place = plan_ref[child_places + d * children + k]

            @pl.when(place < in_range)
            def _():
                ranged[rows_at(place, rows), :] += piece[pl.ds(span + k * rows, rows), :].astype(F32)


def early_body(cubes, grids, slots, rows, children, plan_ref, entries_ref, *refs):
    pieces = dict(enumerate(refs[:-3]))
    ranged, touched, total = refs[-3:]
    places = 2 * cubes + grids
    none = entries_ref.shape[0] // rows
    ranged[...] = jnp.zeros_like(ranged)
    total[...] = jnp.zeros_like(total)
    for d in range(cubes):
        slot = plan_ref[d]
        touched[rows_at(slot, rows), :] = entries_ref[rows_at(jnp.minimum(slot, none - 1), rows), :].astype(F32)
    for d, piece in pieces.items():
        for k in range(slots):
            at = rows_at(plan_ref[places + d * slots + k], rows)
            ranged[at, :] = piece[pl.ds(k * rows, rows), :].astype(F32)
    add_children(cubes, grids, slots, rows, children, plan_ref, pieces, ranged, touched, total)


def schur_body(cubes, grids, slots, rows, children, plan_ref, turned_ref, before_ref, *refs):
    pieces = {cubes - 2: refs[0], cubes - 1: refs[1]}
    out_ref, panel_ref, ranged, touched, total, few, factor_ref = refs[5:]
    column = lax.axis_index("grid")
    own_rows, width = out_ref.shape
    depth = panel_ref.shape[0]
    places = 2 * cubes + grids
    in_range = width // rows
    for d, piece in pieces.items():
        for k in range(slots):
            place = plan_ref[places + d * slots + k]

            @pl.when(place < in_range)
            def _():
                ranged[rows_at(place, rows), :] += piece[pl.ds(k * rows, rows), :].astype(F32)

    add_children(cubes, grids, slots, rows, children, plan_ref, pieces, ranged, touched, total)
    for d in range(cubes):
        few[pl.ds(d * rows, rows), :] = touched[rows_at(plan_ref[d], rows), :].astype(BF16)
    redone = jnp.dot(few[...], turned_ref[...], preferred_element_type=F32).astype(BF16)
    factor_ref[pl.ds(0, own_rows), :] = before_ref[...]
    for d in range(cubes):
        factor_ref[rows_at(plan_ref[d], rows), :] = redone[d * rows : (d + 1) * rows, :]
    column_factor = jnp.dot(
        ranged[pl.ds(0, width), :].astype(BF16), turned_ref[...], preferred_element_type=F32
    ).astype(BF16)
    product = lax.dot_general(
        factor_ref[pl.ds(0, own_rows), :], column_factor, (((1,), (1,)), ((), ())), preferred_element_type=F32
    )
    out_ref[...] = (total[pl.ds(0, own_rows), :] - product).astype(BF16)
    if depth % 128 == 0:
        cols = pl.ds(pl.multiple_of(column * depth, depth), depth)
        panel_ref[...] = factor_ref[pl.ds(0, own_rows), cols].astype(F32).T.astype(BF16)
    else:
        for r in range(grids):

            @pl.when(column == r)
            def _():
                part = factor_ref[pl.ds(0, own_rows), pl.ds(r * depth, depth)]
                panel_ref[...] = part.astype(F32).T.astype(BF16)


def local(
    child_update, child_panel, panel_entries, panel_inverse, block_owner, child_dest, child_rows
):
    cubes = lax.axis_size("cube")
    grids = lax.axis_size("grid")
    chips = cubes // 2
    children, rows = child_rows.shape
    width = child_update.shape[1]
    depth = child_panel.shape[0]
    panel = panel_inverse.shape[0]
    own_rows = panel_entries.shape[1]
    slots = own_rows // rows // grids
    span = slots * rows
    base = span + children * rows
    sent = base + 2 * rows * (width // panel)
    like = jax.ShapeDtypeStruct
    small = own_rows * width <= 512 * 512
    kept = pltpu.VMEM if small else like

    def in_hbm(x):
        return pltpu.with_memory_space_constraint(x, pltpu.HBM)

    def join(first, *others):
        if small:
            first, *others = (
                pltpu.with_memory_space_constraint(x, pltpu.SMEM if x.dtype == I32 else pltpu.VMEM)
                for x in (first, *others)
            )
        return pl.pallas_call(
            join_body,
            out_shape=kept(first.shape, first.dtype),
            in_specs=[ANY] * (1 + len(others)),
            out_specs=ANY,
            input_output_aliases={0: 0},
        )(first, *others)

    def swap(x, axis, d):
        n = lax.axis_size(axis)
        return lax.ppermute(x, axis, [(i, i ^ d) for i in range(n)])

    rest_rows = (grids - 1) * span
    prepared = call(
        functools.partial(prepare_body, cubes, grids, span),
        [kept((base, depth), BF16)] * grids
        + [kept((rest_rows, depth), BF16)] * grids
        + [kept((cubes * rows, width), BF16), kept((panel, panel), BF16)],
        [ANY] * 7,
        [
            pltpu.SMEM(block_owner.shape, I32),
            pltpu.SMEM(child_dest.shape, I32),
            pltpu.VMEM(child_rows.shape, I32),
            pltpu.VMEM(child_update.shape, BF16),
            pltpu.VMEM(child_panel.shape[::-1], BF16),
            pltpu.VMEM(panel_entries.shape, BF16),
            pltpu.VMEM(panel_entries.shape[::-1], BF16),
            pltpu.SemaphoreType.DMA((6 + grids,)),
        ],
        2 * rows * rows * children * (width + depth),
        4 * own_rows * depth,
        limit=28,
    )(*(in_hbm(x) for x in (block_owner, child_dest, child_rows, child_update, child_panel.T, panel_entries, panel_inverse)))
    firsts, rests = list(prepared[:grids]), list(prepared[grids:-2])
    blocks, turned = prepared[-2:]
    for d in [*range(2, grids), 1]:
        firsts[d] = swap(firsts[d], "grid", d)
    plan = call(
        functools.partial(plan_body, cubes, grids, slots),
        [pltpu.SMEM((2 * cubes + grids + cubes * (slots + children),), I32)],
        [ANY, ANY],
        [
            pltpu.SMEM(block_owner.shape, I32),
            pltpu.SMEM(child_dest.shape, I32),
            pltpu.SMEM(block_owner.shape, I32),
            pltpu.SMEM((cubes,), I32),
            pltpu.SemaphoreType.DMA((2,)),
        ],
        100000,
        6000000,
        [SMEM],
    )(in_hbm(block_owner), in_hbm(child_dest))[0]
    marker = call(marker_body, [kept((8, 128), F32)], [VMEM], [], 1000, 0)(firsts[0])[0]
    for d in range(2, grids):
        rests[d] = swap(join(rests[d], marker), "grid", d)
    plan = pltpu.with_memory_space_constraint(plan, pltpu.SMEM)
    parts = [*range(2, grids), 0, 1]
    packed = call(
        functools.partial(pack_body, parts, rows, base),
        [kept((sent, panel), BF16)] * chips,
        [VMEM] * (1 + grids),
        [],
        1000,
        2 * chips * sent * panel,
    )(blocks, *(firsts[d] for d in parts))
    arrived = [packed[0]] + [swap(packed[i], "cube", 2 * i) for i in range(1, chips)]
    rests[1] = swap(join(rests[1], packed[0]), "grid", 1)
    entries, before = call(
        functools.partial(own_body, cubes, grids, span, rows),
        [kept((own_rows, panel), BF16), kept((own_rows, panel), BF16)],
        [SMEM] + [VMEM] * (2 + grids),
        [],
        2200000000,
        2 * own_rows * panel * panel,
    )(plan, turned, packed[0], *rests)
    arrived[-1] = join(arrived[-1], before)
    pieces = []
    for piece in arrived:
        pieces += [piece, swap(piece, "cube", 1)]
    sizes = (cubes, grids, slots, rows, children)
    shapes = [(width + rows, panel), (own_rows + rows, panel), (own_rows + rows, width)]
    early = call(
        functools.partial(early_body, *sizes),
        [kept(shape, F32) for shape in shapes],
        [SMEM] + [VMEM] * (cubes - 1),
        [],
        1000,
        4 * width * panel,
        limit=16 if small else 56,
    )(plan, entries, *pieces[:-2])
    return tuple(
        call(
            functools.partial(schur_body, *sizes),
            [like((own_rows, width), BF16), like((depth, own_rows), BF16)] + [kept(shape, F32) for shape in shapes],
            [SMEM] + [VMEM] * 7,
            [pltpu.VMEM((cubes * rows, panel), BF16), pltpu.VMEM((own_rows + rows, panel), BF16)],
            2 * own_rows * width * panel,
            2 * (own_rows * width + (own_rows + cubes * span) * panel),
            limit=16 if small else 56,
            aliases={5: 2, 6: 3, 7: 4},
        )(plan, turned, before, *pieces[-2:], *early)[:2]
    )


def solution(mesh):
    placed = (
        P("cube", "grid"),
        P("grid", "cube"),
        P("grid", "cube"),
        P(),
        P(),
        P(),
        P("cube", None),
    )
    return jax.shard_map(
        local,
        mesh=mesh,
        in_specs=placed,
        out_specs=(P("cube", "grid"), P("grid", "cube")),
        check_vma=False,
    )
```

```python
import functools

import jax
import jax.numpy as jnp
from jax import lax
from jax.experimental import pallas as pl
from jax.experimental.pallas import tpu as pltpu
from jax.sharding import PartitionSpec as P

F32 = jnp.float32
BF16 = jnp.bfloat16
I32 = jnp.int32
VMEM = pl.BlockSpec(memory_space=pltpu.VMEM)
SMEM = pl.BlockSpec(memory_space=pltpu.SMEM)
ANY = pl.BlockSpec(memory_space=pl.ANY)
MIB = 1024 * 1024
PACK_COST = 1500000000


def call(body, outs, in_specs, scratch, flops, moved, out_specs=None, limit=16, aliases={}):
    return pl.pallas_call(
        body,
        out_shape=outs,
        in_specs=in_specs,
        out_specs=[VMEM] * len(outs) if out_specs is None else out_specs,
        scratch_shapes=scratch,
        input_output_aliases=aliases,
        compiler_params=pltpu.CompilerParams(vmem_limit_bytes=limit * MIB),
        cost_estimate=pl.CostEstimate(flops=flops, bytes_accessed=moved, transcendentals=0),
    )


def rows_at(index, size):
    return pl.ds(pl.multiple_of(index * size, size), size)


def prepare_body(
    cubes, grids, span, owner_hbm, dest_hbm, rows_hbm, update_hbm, panel_hbm, entries_hbm, inverse_hbm, *refs
):
    firsts, rests, blocks_ref, turned_ref = refs[:grids], refs[grids : 2 * grids - 1], *refs[2 * grids - 1 : 2 * grids + 1]
    owner_ref, dest_ref, rows_ref, update_ref, panel_ref, entries_ref, flipped, sems = refs[2 * grids + 1 :]
    copies = [
        pltpu.make_async_copy(source, target, sems.at[i])
        for i, (source, target) in enumerate(
            (
                (entries_hbm, entries_ref),
                (panel_hbm, panel_ref),
                (rows_hbm, rows_ref),
                (update_hbm, update_ref),
                (owner_hbm, owner_ref),
                (dest_hbm, dest_ref),
            )
        )
    ]
    mine = lax.axis_index("cube")
    column = lax.axis_index("grid")
    depth = entries_ref.shape[0]
    for d in range(grids):
        part = inverse_hbm.at[rows_at(jnp.bitwise_xor(column, d), depth), :]
        copies.append(pltpu.make_async_copy(part, turned_ref.at[pl.ds(d * depth, depth), :], sems.at[6 + d]))
    for copy in copies:
        copy.start()
    children, rows = rows_ref.shape
    base = span + children * rows
    blocks_ref[...] = jnp.zeros_like(blocks_ref)
    copies[0].wait()
    flipped[...] = entries_ref[...].astype(F32).T.astype(BF16)
    for d in range(grids):
        piece = flipped[rows_at(jnp.bitwise_xor(column, d), span), :]
        firsts[d][pl.ds(0, span), :] = piece
        for e in range(grids):
            if e != d:
                k = d if d < e else d - 1
                if e == 1:
                    firsts[1][pl.ds(base + k * span, span), :] = piece
                else:
                    rests[max(e - 1, 0)][pl.ds(k * span, span), :] = piece
    for copy in copies[1:6]:
        copy.wait()
    count = children * rows
    want = jnp.concatenate([rows_ref[k : k + 1, :] + k * rows for k in range(children)], axis=1)
    put = (lax.broadcasted_iota(I32, (count, count), 0) == want).astype(BF16)
    placed = jnp.dot(put, panel_ref[...], preferred_element_type=F32).astype(BF16)
    for d in range(grids):
        firsts[d][pl.ds(span, count), :] = placed
    moved = jnp.dot(put, update_ref[...], preferred_element_type=F32).astype(BF16)
    for k in range(children):
        d = jnp.bitwise_xor(owner_ref[dest_ref[mine * children + k]], mine)
        blocks_ref[rows_at(d, rows), :] = moved[k * rows : (k + 1) * rows, :]
    for copy in copies[6:]:
        copy.wait()


def pack_body(parts, rows, base, blocks_ref, *refs):
    firsts, payloads = refs[: len(parts)], refs[len(parts) :]
    depth = firsts[0].shape[1]
    panel = payloads[0].shape[1]
    chunks = blocks_ref.shape[1] // panel
    for d, first in zip(parts, firsts):
        piece = first[...]
        for payload in payloads:
            payload[pl.ds(0, base), pl.ds(d * depth, depth)] = piece
    for i, payload in enumerate(payloads):
        for half in range(2):
            for j in range(chunks):
                at = base + (half * chunks + j) * rows
                block = blocks_ref[pl.ds((2 * i + half) * rows, rows), pl.ds(j * panel, panel)]
                payload[pl.ds(at, rows), :] = block


def complete_body(base, plan_ref, first_ref, *refs):
    depth = first_ref.shape[1]
    piece = first_ref[pl.ds(0, base), :]
    for payload in refs[len(refs) // 2 :]:
        payload[pl.ds(0, base), pl.ds(depth, depth)] = piece


def plan_body(cubes, grids, slots, owner_hbm, dest_hbm, out_ref, owner_ref, dest_ref, slot_ref, count_ref, sems):
    fetches = [
        pltpu.make_async_copy(owner_hbm, owner_ref, sems.at[0]),
        pltpu.make_async_copy(dest_hbm, dest_ref, sems.at[1]),
    ]
    for fetch in fetches:
        fetch.start()
    for fetch in fetches:
        fetch.wait()
    mine = lax.axis_index("cube")
    column = lax.axis_index("grid")
    blocks = owner_ref.shape[0]
    in_range = blocks // grids
    children = dest_ref.shape[0] // cubes
    none = grids * slots
    places = 2 * cubes + grids
    child_places = places + cubes * slots
    for r in range(grids):

        def count_own(i, seen):
            b = r * in_range + i
            own = owner_ref[b] == mine
            slot_ref[b] = jnp.where(own, r * slots + seen, none)
            return seen + own.astype(I32)

        out_ref[2 * cubes + r] = lax.fori_loop(0, in_range, count_own, I32(0), unroll=8)
    for d in range(cubes):
        source = jnp.bitwise_xor(mine, d)
        slot, which = I32(none), I32(0)
        for k in range(children):
            b = dest_ref[source * children + k]
            here = slot_ref[b]
            which = jnp.where(here < none, k, which)
            slot = jnp.minimum(slot, here)
            local_b = b - column * in_range
            inside = jnp.logical_and(local_b >= 0, local_b < in_range)
            out_ref[child_places + d * children + k] = jnp.where(inside, local_b, in_range)
        out_ref[d] = slot
        out_ref[cubes + d] = which
        count_ref[d] = 0
        for k in range(slots):
            out_ref[places + d * slots + k] = in_range

    def place(i, carry):
        d = jnp.bitwise_xor(owner_ref[column * in_range + i], mine)
        k = count_ref[d]
        out_ref[places + d * slots + k] = i
        count_ref[d] = k + 1
        return carry

    lax.fori_loop(0, in_range, place, 0, unroll=8)


def own_body(cubes, grids, span, rows, base, plan_ref, turned_ref, mine_ref, full_ref, *refs):
    rests = refs[: grids - 1]
    entries_ref, factor_ref = refs[grids - 1 :]
    column = lax.axis_index("grid")
    depth = rests[0].shape[1]
    for e in range(grids):
        r = jnp.bitwise_xor(column, e)
        ids = lax.broadcasted_iota(I32, (span, depth), 0)
        live = ids < plan_ref[2 * cubes + r] * rows
        for d in range(grids):
            if e == 0:
                piece = mine_ref[pl.ds(0, span), pl.ds(d * depth, depth)]
            else:
                k = d ^ e
                at = (k if k < d else k - 1) * span
                if d == 1:
                    piece = full_ref[pl.ds(base + at, span), :]
                else:
                    piece = rests[max(d - 1, 0)][pl.ds(at, span), :]
            piece = jnp.where(live, piece.astype(F32), 0.0).astype(BF16)
            entries_ref[rows_at(r, span), pl.ds(d * depth, depth)] = piece
    own = jnp.dot(entries_ref[...], turned_ref[...], preferred_element_type=F32)
    factor_ref[pl.ds(0, entries_ref.shape[0]), :] = own.astype(BF16)


def join_body(*refs):
    pass


def add_children(cubes, grids, slots, rows, children, plan_ref, pieces, ranged, touched, total):
    span = slots * rows
    base = span + children * rows
    panel = ranged.shape[1]
    chunks = total.shape[1] // panel
    child_places = 2 * cubes + grids + cubes * slots
    in_range = ranged.shape[0] // rows - 1
    for d, piece in pieces.items():
        at = rows_at(plan_ref[d], rows)
        touched[at, :] += piece[rows_at(slots + plan_ref[cubes + d], rows), :].astype(F32)
        for j in range(chunks):
            part = pl.ds(base + ((d & 1) * chunks + j) * rows, rows)
            total[at, pl.ds(j * panel, panel)] += piece[part, :].astype(F32)
        for k in range(children):
            place = plan_ref[child_places + d * children + k]

            @pl.when(place < in_range)
            def _():
                ranged[rows_at(place, rows), :] += piece[pl.ds(span + k * rows, rows), :].astype(F32)


def early_body(cubes, grids, slots, rows, children, plan_ref, entries_ref, *refs):
    pieces = dict(enumerate(refs[:-3]))
    ranged, touched, total = refs[-3:]
    places = 2 * cubes + grids
    none = entries_ref.shape[0] // rows
    ranged[...] = jnp.zeros_like(ranged)
    total[...] = jnp.zeros_like(total)
    for d in range(cubes):
        slot = plan_ref[d]
        touched[rows_at(slot, rows), :] = entries_ref[rows_at(jnp.minimum(slot, none - 1), rows), :].astype(F32)
    for d, piece in pieces.items():
        for k in range(slots):
            at = rows_at(plan_ref[places + d * slots + k], rows)
            ranged[at, :] = piece[pl.ds(k * rows, rows), :].astype(F32)
    add_children(cubes, grids, slots, rows, children, plan_ref, pieces, ranged, touched, total)


def schur_body(cubes, grids, slots, rows, children, steps, plan_ref, turned_ref, *refs):
    pieces = {cubes - 2: refs[0], cubes - 1: refs[1]}
    out_hbm, panel_hbm, ranged, touched, total, factor_ref, few, out_ref, panel_ref, sems = refs[6:]
    column = lax.axis_index("grid")
    own_rows, width = out_ref.shape
    depth = panel_ref.shape[0]
    places = 2 * cubes + grids
    in_range = width // rows
    for d, piece in pieces.items():
        for k in range(slots):
            place = plan_ref[places + d * slots + k]

            @pl.when(place < in_range)
            def _():
                ranged[rows_at(place, rows), :] += piece[pl.ds(k * rows, rows), :].astype(F32)

    add_children(cubes, grids, slots, rows, children, plan_ref, pieces, ranged, touched, total)
    for d in range(cubes):
        few[pl.ds(d * rows, rows), :] = touched[rows_at(plan_ref[d], rows), :].astype(BF16)
    redone = jnp.dot(few[...], turned_ref[...], preferred_element_type=F32).astype(BF16)
    column_factor = jnp.dot(
        ranged[pl.ds(0, width), :].astype(BF16), turned_ref[...], preferred_element_type=F32
    ).astype(BF16)
    for d in range(cubes):
        factor_ref[rows_at(plan_ref[d], rows), :] = redone[d * rows : (d + 1) * rows, :]
    chunk = own_rows // steps
    copies = []
    for i in range(steps):
        part = pl.ds(i * chunk, chunk)
        product = lax.dot_general(
            factor_ref[part, :], column_factor, (((1,), (1,)), ((), ())), preferred_element_type=F32
        )
        out_ref[part, :] = (total[part, :] - product).astype(BF16)
        copies.append(pltpu.make_async_copy(out_ref.at[part, :], out_hbm.at[part, :], sems.at[i]))
        copies[-1].start()
    if depth % 128 == 0:
        cols = pl.ds(pl.multiple_of(column * depth, depth), depth)
        panel_ref[...] = factor_ref[pl.ds(0, own_rows), cols].astype(F32).T.astype(BF16)
    else:
        for r in range(grids):

            @pl.when(column == r)
            def _():
                part = factor_ref[pl.ds(0, own_rows), pl.ds(r * depth, depth)]
                panel_ref[...] = part.astype(F32).T.astype(BF16)

    copies.append(pltpu.make_async_copy(panel_ref, panel_hbm, sems.at[steps]))
    copies[-1].start()
    for copy in copies:
        copy.wait()


def local(
    child_update, child_panel, panel_entries, panel_inverse, block_owner, child_dest, child_rows
):
    cubes = lax.axis_size("cube")
    grids = lax.axis_size("grid")
    chips = cubes // 2
    children, rows = child_rows.shape
    width = child_update.shape[1]
    depth = child_panel.shape[0]
    panel = panel_inverse.shape[0]
    own_rows = panel_entries.shape[1]
    slots = own_rows // rows // grids
    span = slots * rows
    base = span + children * rows
    sent = base + 2 * rows * (width // panel)
    like = jax.ShapeDtypeStruct
    small = own_rows * width <= 512 * 512
    kept = pltpu.VMEM if small else like

    def in_hbm(x):
        return pltpu.with_memory_space_constraint(x, pltpu.HBM)

    def join(first, *others):
        if small:
            first, *others = (
                pltpu.with_memory_space_constraint(x, pltpu.SMEM if x.dtype == I32 else pltpu.VMEM)
                for x in (first, *others)
            )
        return pl.pallas_call(
            join_body,
            out_shape=kept(first.shape, first.dtype),
            in_specs=[ANY] * (1 + len(others)),
            out_specs=ANY,
            input_output_aliases={0: 0},
        )(first, *others)

    def swap(x, axis, d):
        n = lax.axis_size(axis)
        return lax.ppermute(x, axis, [(i, i ^ d) for i in range(n)])

    rest_rows = (grids - 1) * span
    prepared = call(
        functools.partial(prepare_body, cubes, grids, span),
        [kept((base + (rest_rows if d == 1 else 0), depth), BF16) for d in range(grids)]
        + [kept((rest_rows, depth), BF16)] * (grids - 1)
        + [kept((cubes * rows, width), BF16), kept((panel, panel), BF16)],
        [ANY] * 7,
        [
            pltpu.SMEM(block_owner.shape, I32),
            pltpu.SMEM(child_dest.shape, I32),
            pltpu.VMEM(child_rows.shape, I32),
            pltpu.VMEM(child_update.shape, BF16),
            pltpu.VMEM(child_panel.shape[::-1], BF16),
            pltpu.VMEM(panel_entries.shape, BF16),
            pltpu.VMEM(panel_entries.shape[::-1], BF16),
            pltpu.SemaphoreType.DMA((6 + grids,)),
        ],
        2 * rows * rows * children * (width + depth),
        4 * own_rows * depth,
        limit=28,
    )(*(in_hbm(x) for x in (block_owner, child_dest, child_rows, child_update, child_panel.T, panel_entries, panel_inverse)))
    firsts, rests = list(prepared[:grids]), list(prepared[grids:-2])
    blocks, turned = prepared[-2:]
    for d in [*range(2, grids), 1]:
        firsts[d] = swap(firsts[d], "grid", d)
    plan = call(
        functools.partial(plan_body, cubes, grids, slots),
        [pltpu.SMEM((2 * cubes + grids + cubes * (slots + children),), I32)],
        [ANY, ANY],
        [
            pltpu.SMEM(block_owner.shape, I32),
            pltpu.SMEM(child_dest.shape, I32),
            pltpu.SMEM(block_owner.shape, I32),
            pltpu.SMEM((cubes,), I32),
            pltpu.SemaphoreType.DMA((2,)),
        ],
        100000,
        6000000,
        [SMEM],
    )(in_hbm(block_owner), in_hbm(child_dest))[0]
    for d in range(2, grids):
        rests[d - 1] = swap(join(rests[d - 1], plan), "grid", d)
    plan = pltpu.with_memory_space_constraint(plan, pltpu.SMEM)
    parts = [*range(2, grids), 0]
    packed = call(
        functools.partial(pack_body, parts, rows, base),
        [kept((sent, panel), BF16)] * chips,
        [VMEM] * (1 + len(parts)),
        [],
        PACK_COST,
        2 * chips * sent * panel,
    )(blocks, *(firsts[d] for d in parts))
    packed = call(
        functools.partial(complete_body, base),
        [kept((sent, panel), BF16)] * chips,
        [ANY] + [VMEM] * (1 + chips),
        [],
        1000,
        2 * chips * base * depth,
        aliases={2 + i: i for i in range(chips)},
    )(plan, firsts[1], *packed)
    arrived = [packed[0]] + [swap(packed[i], "cube", 2 * i) for i in range(1, chips)]
    entries, before = call(
        functools.partial(own_body, cubes, grids, span, rows, base),
        [kept((own_rows, panel), BF16), kept((own_rows + rows, panel), BF16)],
        [SMEM] + [VMEM] * (2 + grids),
        [],
        1650000000,
        2 * own_rows * panel * panel,
    )(plan, turned, packed[0], firsts[1], *rests)
    arrived[1] = join(arrived[1], before)
    pieces = []
    for piece in arrived:
        pieces += [piece, swap(piece, "cube", 1)]
    sizes = (cubes, grids, slots, rows, children)
    steps = 4
    shapes = [(width + rows, panel), (own_rows + rows, panel), (own_rows + rows, width)]
    early = call(
        functools.partial(early_body, *sizes),
        [kept(shape, F32) for shape in shapes],
        [SMEM] + [VMEM] * (cubes - 1),
        [],
        1000,
        4 * width * panel,
        limit=16 if small else 56,
    )(plan, entries, *pieces[:-2])
    return tuple(
        call(
            functools.partial(schur_body, *sizes, steps),
            [like((own_rows, width), BF16), like((depth, own_rows), BF16)]
            + [kept(shape, F32) for shape in shapes]
            + [kept((own_rows + rows, panel), BF16)],
            [SMEM] + [VMEM] * 7,
            [
                pltpu.VMEM((cubes * rows, panel), BF16),
                pltpu.VMEM((own_rows, width), BF16),
                pltpu.VMEM((depth, own_rows), BF16),
                pltpu.SemaphoreType.DMA((steps + 1,)),
            ],
            2 * own_rows * width * panel,
            2 * (own_rows * width + (own_rows + cubes * span) * panel),
            [ANY] * 2 + [VMEM] * 4,
            limit=16 if small else 56,
            aliases={4: 2, 5: 3, 6: 4, 7: 5},
        )(plan, turned, *pieces[-2:], *early, before)[:2]
    )


def solution(mesh):
    placed = (
        P("cube", "grid"),
        P("grid", "cube"),
        P("grid", "cube"),
        P(),
        P(),
        P(),
        P("cube", None),
    )
    return jax.shard_map(
        local,
        mesh=mesh,
        in_specs=placed,
        out_specs=(P("cube", "grid"), P("grid", "cube")),
        check_vma=False,
    )
```

```python
import functools

import jax
import jax.numpy as jnp
from jax import lax
from jax.experimental import pallas as pl
from jax.experimental.pallas import tpu as pltpu
from jax.sharding import PartitionSpec as P

F32 = jnp.float32
BF16 = jnp.bfloat16
I32 = jnp.int32
VMEM = pl.BlockSpec(memory_space=pltpu.VMEM)
SMEM = pl.BlockSpec(memory_space=pltpu.SMEM)
ANY = pl.BlockSpec(memory_space=pl.ANY)
MIB = 1024 * 1024
JOIN_COST = 1500000000


def call(body, outs, in_specs, scratch, flops, moved, out_specs=None, limit=16, aliases={}):
    return pl.pallas_call(
        body,
        out_shape=outs,
        in_specs=in_specs,
        out_specs=[VMEM] * len(outs) if out_specs is None else out_specs,
        scratch_shapes=scratch,
        input_output_aliases=aliases,
        compiler_params=pltpu.CompilerParams(vmem_limit_bytes=limit * MIB),
        cost_estimate=pl.CostEstimate(flops=flops, bytes_accessed=moved, transcendentals=0),
    )


def rows_at(index, size):
    return pl.ds(pl.multiple_of(index * size, size), size)


def prepare_body(
    cubes, grids, span, owner_hbm, dest_hbm, rows_hbm, update_hbm, panel_hbm, entries_hbm, inverse_hbm, *refs
):
    firsts, rests, blocks_ref, turned_ref = refs[:grids], refs[grids : 2 * grids], *refs[2 * grids : 2 * grids + 2]
    owner_ref, dest_ref, rows_ref, update_ref, panel_ref, entries_ref, flipped, sems = refs[2 * grids + 2 :]
    copies = [
        pltpu.make_async_copy(source, target, sems.at[i])
        for i, (source, target) in enumerate(
            (
                (entries_hbm, entries_ref),
                (panel_hbm, panel_ref),
                (rows_hbm, rows_ref),
                (update_hbm, update_ref),
                (owner_hbm, owner_ref),
                (dest_hbm, dest_ref),
            )
        )
    ]
    mine = lax.axis_index("cube")
    column = lax.axis_index("grid")
    depth = entries_ref.shape[0]
    for d in range(grids):
        part = inverse_hbm.at[rows_at(jnp.bitwise_xor(column, d), depth), :]
        copies.append(pltpu.make_async_copy(part, turned_ref.at[pl.ds(d * depth, depth), :], sems.at[6 + d]))
    for copy in copies:
        copy.start()
    children, rows = rows_ref.shape
    blocks_ref[...] = jnp.zeros_like(blocks_ref)
    copies[0].wait()
    flipped[...] = entries_ref[...].astype(F32).T.astype(BF16)
    for d in range(grids):
        piece = flipped[rows_at(jnp.bitwise_xor(column, d), span), :]
        firsts[d][pl.ds(0, span), :] = piece
        for e in range(grids):
            if e != d:
                k = d if d < e else d - 1
                rests[e][pl.ds(k * span, span), :] = piece
    for copy in copies[1:6]:
        copy.wait()
    for k in range(children):
        want = rows_ref[k : k + 1, :]
        put = (lax.broadcasted_iota(I32, (rows, rows), 0) == want).astype(BF16)
        part = pl.ds(k * rows, rows)
        placed = jnp.dot(put, panel_ref[part, :], preferred_element_type=F32).astype(BF16)
        for d in range(grids):
            firsts[d][pl.ds(span + k * rows, rows), :] = placed
        moved = jnp.dot(put, update_ref[part, :], preferred_element_type=F32).astype(BF16)
        d = jnp.bitwise_xor(owner_ref[dest_ref[mine * children + k]], mine)
        blocks_ref[rows_at(d, rows), :] = moved
    for copy in copies[6:]:
        copy.wait()


def pack_body(parts, rows, base, blocks_ref, *refs):
    firsts, payloads = refs[: len(parts)], refs[len(parts) :]
    depth = firsts[0].shape[1]
    panel = payloads[0].shape[1]
    chunks = blocks_ref.shape[1] // panel
    for d, first in zip(parts, firsts):
        piece = first[...]
        for payload in payloads:
            payload[pl.ds(0, base), pl.ds(d * depth, depth)] = piece
    for i, payload in enumerate(payloads):
        for half in range(2):
            for j in range(chunks):
                at = base + (half * chunks + j) * rows
                block = blocks_ref[pl.ds((2 * i + half) * rows, rows), pl.ds(j * panel, panel)]
                payload[pl.ds(at, rows), :] = block


def plan_body(cubes, grids, slots, owner_hbm, dest_hbm, out_ref, owner_ref, dest_ref, slot_ref, count_ref, sems):
    fetches = [
        pltpu.make_async_copy(owner_hbm, owner_ref, sems.at[0]),
        pltpu.make_async_copy(dest_hbm, dest_ref, sems.at[1]),
    ]
    for fetch in fetches:
        fetch.start()
    for fetch in fetches:
        fetch.wait()
    mine = lax.axis_index("cube")
    column = lax.axis_index("grid")
    blocks = owner_ref.shape[0]
    in_range = blocks // grids
    children = dest_ref.shape[0] // cubes
    none = grids * slots
    places = 2 * cubes + grids
    child_places = places + cubes * slots
    for r in range(grids):

        def count_own(i, seen):
            b = r * in_range + i
            own = owner_ref[b] == mine
            slot_ref[b] = jnp.where(own, r * slots + seen, none)
            return seen + own.astype(I32)

        out_ref[2 * cubes + r] = lax.fori_loop(0, in_range, count_own, I32(0), unroll=8)
    for d in range(cubes):
        source = jnp.bitwise_xor(mine, d)
        slot, which = I32(none), I32(0)
        for k in range(children):
            b = dest_ref[source * children + k]
            here = slot_ref[b]
            which = jnp.where(here < none, k, which)
            slot = jnp.minimum(slot, here)
            local_b = b - column * in_range
            inside = jnp.logical_and(local_b >= 0, local_b < in_range)
            out_ref[child_places + d * children + k] = jnp.where(inside, local_b, in_range)
        out_ref[d] = slot
        out_ref[cubes + d] = which
        count_ref[d] = 0
        for k in range(slots):
            out_ref[places + d * slots + k] = in_range

    def place(i, carry):
        d = jnp.bitwise_xor(owner_ref[column * in_range + i], mine)
        k = count_ref[d]
        out_ref[places + d * slots + k] = i
        count_ref[d] = k + 1
        return carry

    lax.fori_loop(0, in_range, place, 0, unroll=8)


def own_body(cubes, grids, span, rows, plan_ref, turned_ref, mine_ref, *refs):
    rests = refs[:grids]
    entries_ref, factor_ref = refs[grids:]
    column = lax.axis_index("grid")
    depth = rests[0].shape[1]
    for e in range(grids):
        r = jnp.bitwise_xor(column, e)
        ids = lax.broadcasted_iota(I32, (span, depth), 0)
        live = ids < plan_ref[2 * cubes + r] * rows
        for d in range(grids):
            if e == 0:
                piece = mine_ref[pl.ds(0, span), pl.ds(d * depth, depth)]
            else:
                k = d ^ e
                at = (k if k < d else k - 1) * span
                piece = rests[d][pl.ds(at, span), :]
            piece = jnp.where(live, piece.astype(F32), 0.0).astype(BF16)
            entries_ref[rows_at(r, span), pl.ds(d * depth, depth)] = piece
    factor_ref[...] = jnp.dot(entries_ref[...], turned_ref[...], preferred_element_type=F32).astype(BF16)


def marker_body(after_ref, out_ref):
    out_ref[...] = jnp.zeros_like(out_ref)


def join_body(*refs):
    pass


def add_children(cubes, grids, slots, rows, children, plan_ref, pieces, ranged, touched, total):
    span = slots * rows
    base = span + children * rows
    panel = ranged.shape[1]
    chunks = total.shape[1] // panel
    child_places = 2 * cubes + grids + cubes * slots
    in_range = ranged.shape[0] // rows - 1
    for d, piece in pieces.items():
        at = rows_at(plan_ref[d], rows)
        touched[at, :] += piece[rows_at(slots + plan_ref[cubes + d], rows), :].astype(F32)
        for j in range(chunks):
            part = pl.ds(base + ((d & 1) * chunks + j) * rows, rows)
            total[at, pl.ds(j * panel, panel)] += piece[part, :].astype(F32)
        for k in range(children):
            place = plan_ref[child_places + d * children + k]

            @pl.when(place < in_range)
            def _():
                ranged[rows_at(place, rows), :] += piece[pl.ds(span + k * rows, rows), :].astype(F32)


def early_body(cubes, grids, slots, rows, children, plan_ref, entries_ref, *refs):
    pieces = dict(enumerate(refs[:-3]))
    ranged, touched, total = refs[-3:]
    places = 2 * cubes + grids
    none = entries_ref.shape[0] // rows
    ranged[...] = jnp.zeros_like(ranged)
    total[...] = jnp.zeros_like(total)
    for d in range(cubes):
        slot = plan_ref[d]
        touched[rows_at(slot, rows), :] = entries_ref[rows_at(jnp.minimum(slot, none - 1), rows), :].astype(F32)
    for d, piece in pieces.items():
        for k in range(slots):
            at = rows_at(plan_ref[places + d * slots + k], rows)
            ranged[at, :] = piece[pl.ds(k * rows, rows), :].astype(F32)
    add_children(cubes, grids, slots, rows, children, plan_ref, pieces, ranged, touched, total)


def schur_body(cubes, grids, slots, rows, children, plan_ref, turned_ref, before_ref, *refs):
    pieces = {cubes - 2: refs[0], cubes - 1: refs[1]}
    out_ref, panel_ref, ranged, touched, total, few, factor_ref = refs[5:]
    column = lax.axis_index("grid")
    own_rows, width = out_ref.shape
    depth = panel_ref.shape[0]
    places = 2 * cubes + grids
    in_range = width // rows
    for d, piece in pieces.items():
        for k in range(slots):
            place = plan_ref[places + d * slots + k]

            @pl.when(place < in_range)
            def _():
                ranged[rows_at(place, rows), :] += piece[pl.ds(k * rows, rows), :].astype(F32)

    add_children(cubes, grids, slots, rows, children, plan_ref, pieces, ranged, touched, total)
    for d in range(cubes):
        few[pl.ds(d * rows, rows), :] = touched[rows_at(plan_ref[d], rows), :].astype(BF16)
    redone = jnp.dot(few[...], turned_ref[...], preferred_element_type=F32).astype(BF16)
    factor_ref[pl.ds(0, own_rows), :] = before_ref[...]
    for d in range(cubes):
        factor_ref[rows_at(plan_ref[d], rows), :] = redone[d * rows : (d + 1) * rows, :]
    column_factor = jnp.dot(
        ranged[pl.ds(0, width), :].astype(BF16), turned_ref[...], preferred_element_type=F32
    ).astype(BF16)
    product = lax.dot_general(
        factor_ref[pl.ds(0, own_rows), :], column_factor, (((1,), (1,)), ((), ())), preferred_element_type=F32
    )
    out_ref[...] = (total[pl.ds(0, own_rows), :] - product).astype(BF16)
    if depth % 128 == 0:
        cols = pl.ds(pl.multiple_of(column * depth, depth), depth)
        panel_ref[...] = factor_ref[pl.ds(0, own_rows), cols].astype(F32).T.astype(BF16)
    else:
        for r in range(grids):

            @pl.when(column == r)
            def _():
                part = factor_ref[pl.ds(0, own_rows), pl.ds(r * depth, depth)]
                panel_ref[...] = part.astype(F32).T.astype(BF16)


def local(
    child_update, child_panel, panel_entries, panel_inverse, block_owner, child_dest, child_rows
):
    cubes = lax.axis_size("cube")
    grids = lax.axis_size("grid")
    chips = cubes // 2
    children, rows = child_rows.shape
    width = child_update.shape[1]
    depth = child_panel.shape[0]
    panel = panel_inverse.shape[0]
    own_rows = panel_entries.shape[1]
    slots = own_rows // rows // grids
    span = slots * rows
    base = span + children * rows
    sent = base + 2 * rows * (width // panel)
    like = jax.ShapeDtypeStruct
    small = own_rows * width <= 512 * 512
    kept = pltpu.VMEM if small else like

    def in_hbm(x):
        return pltpu.with_memory_space_constraint(x, pltpu.HBM)

    def join(first, *others, cost=0):
        if small:
            first, *others = (
                pltpu.with_memory_space_constraint(x, pltpu.SMEM if x.dtype == I32 else pltpu.VMEM)
                for x in (first, *others)
            )
        return pl.pallas_call(
            join_body,
            out_shape=kept(first.shape, first.dtype),
            in_specs=[ANY] * (1 + len(others)),
            out_specs=ANY,
            input_output_aliases={0: 0},
            cost_estimate=pl.CostEstimate(flops=cost, bytes_accessed=0, transcendentals=0),
        )(first, *others)

    def swap(x, axis, d):
        n = lax.axis_size(axis)
        return lax.ppermute(x, axis, [(i, i ^ d) for i in range(n)])

    rest_rows = (grids - 1) * span
    prepared = call(
        functools.partial(prepare_body, cubes, grids, span),
        [kept((base, depth), BF16)] * grids
        + [kept((rest_rows, depth), BF16)] * grids
        + [kept((cubes * rows, width), BF16), kept((panel, panel), BF16)],
        [ANY] * 7,
        [
            pltpu.SMEM(block_owner.shape, I32),
            pltpu.SMEM(child_dest.shape, I32),
            pltpu.VMEM(child_rows.shape, I32),
            pltpu.VMEM(child_update.shape, BF16),
            pltpu.VMEM(child_panel.shape[::-1], BF16),
            pltpu.VMEM(panel_entries.shape, BF16),
            pltpu.VMEM(panel_entries.shape[::-1], BF16),
            pltpu.SemaphoreType.DMA((6 + grids,)),
        ],
        2 * rows * rows * children * (width + depth),
        4 * own_rows * depth,
        limit=28,
    )(*(in_hbm(x) for x in (block_owner, child_dest, child_rows, child_update, child_panel.T, panel_entries, panel_inverse)))
    firsts, rests = list(prepared[:grids]), list(prepared[grids:-2])
    blocks, turned = prepared[-2:]
    for d in [*range(2, grids), 1]:
        firsts[d] = swap(firsts[d], "grid", d)
    plan = call(
        functools.partial(plan_body, cubes, grids, slots),
        [pltpu.SMEM((2 * cubes + grids + cubes * (slots + children),), I32)],
        [ANY, ANY],
        [
            pltpu.SMEM(block_owner.shape, I32),
            pltpu.SMEM(child_dest.shape, I32),
            pltpu.SMEM(block_owner.shape, I32),
            pltpu.SMEM((cubes,), I32),
            pltpu.SemaphoreType.DMA((2,)),
        ],
        100000,
        6000000,
        [SMEM],
    )(in_hbm(block_owner), in_hbm(child_dest))[0]
    for d in range(3, grids):
        rests[d] = swap(join(rests[d], plan), "grid", d)
    plan = pltpu.with_memory_space_constraint(plan, pltpu.SMEM)
    parts = [*range(2, grids), 0, 1]
    packed = call(
        functools.partial(pack_body, parts, rows, base),
        [kept((sent, panel), BF16)] * chips,
        [VMEM] * (1 + grids),
        [],
        1000,
        2 * chips * sent * panel,
    )(blocks, *(firsts[d] for d in parts))
    rests[2] = swap(join(rests[2], packed[0]), "grid", 2)
    rests[1] = swap(join(rests[1], rests[-1]), "grid", 1)
    arrived = [packed[0]] + [swap(packed[i], "cube", 2 * i) for i in range(1, chips)]
    rests[-1] = join(rests[-1], plan, cost=JOIN_COST)
    entries, before = call(
        functools.partial(own_body, cubes, grids, span, rows),
        [kept((own_rows, panel), BF16), kept((own_rows, panel), BF16)],
        [SMEM] + [VMEM] * (2 + grids),
        [],
        300000000,
        2 * own_rows * panel * panel,
    )(plan, turned, packed[0], *rests)
    arrived[-1] = join(arrived[-1], *rests[1:])
    pieces = []
    for piece in arrived:
        pieces += [piece, swap(piece, "cube", 1)]
    sizes = (cubes, grids, slots, rows, children)
    shapes = [(width + rows, panel), (own_rows + rows, panel), (own_rows + rows, width)]
    early = call(
        functools.partial(early_body, *sizes),
        [kept(shape, F32) for shape in shapes],
        [SMEM] + [VMEM] * (cubes - 1),
        [],
        1000,
        4 * width * panel,
        limit=16 if small else 56,
    )(plan, entries, *pieces[:-2])
    return tuple(
        call(
            functools.partial(schur_body, *sizes),
            [like((own_rows, width), BF16), like((depth, own_rows), BF16)] + [kept(shape, F32) for shape in shapes],
            [SMEM] + [VMEM] * 7,
            [pltpu.VMEM((cubes * rows, panel), BF16), pltpu.VMEM((own_rows + rows, panel), BF16)],
            2 * own_rows * width * panel,
            2 * (own_rows * width + (own_rows + cubes * span) * panel),
            limit=16 if small else 56,
            aliases={5: 2, 6: 3, 7: 4},
        )(plan, turned, before, *pieces[-2:], *early)[:2]
    )


def solution(mesh):
    placed = (
        P("cube", "grid"),
        P("grid", "cube"),
        P("grid", "cube"),
        P(),
        P(),
        P(),
        P("cube", None),
    )
    return jax.shard_map(
        local,
        mesh=mesh,
        in_specs=placed,
        out_specs=(P("cube", "grid"), P("grid", "cube")),
        check_vma=False,
    )
```

```python
import functools

import jax
import jax.numpy as jnp
from jax import lax
from jax.experimental import pallas as pl
from jax.experimental.pallas import tpu as pltpu
from jax.sharding import PartitionSpec as P

F32 = jnp.float32
BF16 = jnp.bfloat16
I32 = jnp.int32
VMEM = pl.BlockSpec(memory_space=pltpu.VMEM)
SMEM = pl.BlockSpec(memory_space=pltpu.SMEM)
ANY = pl.BlockSpec(memory_space=pl.ANY)
MIB = 1024 * 1024
JOIN_COST = 1500000000


def call(body, outs, in_specs, scratch, flops, moved, out_specs=None, limit=16, aliases={}):
    return pl.pallas_call(
        body,
        out_shape=outs,
        in_specs=in_specs,
        out_specs=[VMEM] * len(outs) if out_specs is None else out_specs,
        scratch_shapes=scratch,
        input_output_aliases=aliases,
        compiler_params=pltpu.CompilerParams(vmem_limit_bytes=limit * MIB),
        cost_estimate=pl.CostEstimate(flops=flops, bytes_accessed=moved, transcendentals=0),
    )


def rows_at(index, size):
    return pl.ds(pl.multiple_of(index * size, size), size)


def first_body(grids, span, rows_hbm, panel_hbm, entries_hbm, *refs):
    firsts, flipped = refs[:grids], refs[grids]
    rows_ref, panel_ref, entries_ref, sems = refs[grids + 1 :]
    copies = [
        pltpu.make_async_copy(source, target, sems.at[i])
        for i, (source, target) in enumerate(
            ((entries_hbm, entries_ref), (panel_hbm, panel_ref), (rows_hbm, rows_ref))
        )
    ]
    for copy in copies:
        copy.start()
    column = lax.axis_index("grid")
    children, rows = rows_ref.shape
    copies[0].wait()
    flipped[...] = entries_ref[...].astype(F32).T.astype(BF16)
    for d in range(grids):
        firsts[d][pl.ds(0, span), :] = flipped[rows_at(jnp.bitwise_xor(column, d), span), :]
    for copy in copies[1:]:
        copy.wait()
    for k in range(children):
        want = rows_ref[k : k + 1, :]
        put = (lax.broadcasted_iota(I32, (rows, rows), 0) == want).astype(BF16)
        part = pl.ds(k * rows, rows)
        placed = jnp.dot(put, panel_ref[part, :], preferred_element_type=F32).astype(BF16)
        for d in range(grids):
            firsts[d][pl.ds(span + k * rows, rows), :] = placed


def second_body(
    cubes, grids, span, owner_hbm, dest_hbm, rows_hbm, update_hbm, inverse_hbm, flipped, *refs
):
    rests, blocks_ref, turned_ref = refs[:grids], *refs[grids : grids + 2]
    owner_ref, dest_ref, rows_ref, update_ref, sems = refs[grids + 2 :]
    copies = [
        pltpu.make_async_copy(source, target, sems.at[i])
        for i, (source, target) in enumerate(
            (
                (rows_hbm, rows_ref),
                (update_hbm, update_ref),
                (owner_hbm, owner_ref),
                (dest_hbm, dest_ref),
            )
        )
    ]
    mine = lax.axis_index("cube")
    column = lax.axis_index("grid")
    depth = flipped.shape[1]
    for d in range(grids):
        part = inverse_hbm.at[rows_at(jnp.bitwise_xor(column, d), depth), :]
        copies.append(pltpu.make_async_copy(part, turned_ref.at[pl.ds(d * depth, depth), :], sems.at[4 + d]))
    for copy in copies:
        copy.start()
    children, rows = rows_ref.shape
    blocks_ref[...] = jnp.zeros_like(blocks_ref)
    for d in range(grids):
        piece = flipped[rows_at(jnp.bitwise_xor(column, d), span), :]
        for e in range(grids):
            if e != d:
                k = d if d < e else d - 1
                rests[e][pl.ds(k * span, span), :] = piece
    for copy in copies[:4]:
        copy.wait()
    for k in range(children):
        want = rows_ref[k : k + 1, :]
        put = (lax.broadcasted_iota(I32, (rows, rows), 0) == want).astype(BF16)
        part = pl.ds(k * rows, rows)
        moved = jnp.dot(put, update_ref[part, :], preferred_element_type=F32).astype(BF16)
        d = jnp.bitwise_xor(owner_ref[dest_ref[mine * children + k]], mine)
        blocks_ref[rows_at(d, rows), :] = moved
    for copy in copies[4:]:
        copy.wait()


def pack_body(parts, rows, base, blocks_ref, *refs):
    firsts, payloads = refs[: len(parts)], refs[len(parts) :]
    depth = firsts[0].shape[1]
    panel = payloads[0].shape[1]
    chunks = blocks_ref.shape[1] // panel
    for d, first in zip(parts, firsts):
        piece = first[...]
        for payload in payloads:
            payload[pl.ds(0, base), pl.ds(d * depth, depth)] = piece
    for i, payload in enumerate(payloads):
        for half in range(2):
            for j in range(chunks):
                at = base + (half * chunks + j) * rows
                block = blocks_ref[pl.ds((2 * i + half) * rows, rows), pl.ds(j * panel, panel)]
                payload[pl.ds(at, rows), :] = block


def plan_body(cubes, grids, slots, owner_hbm, dest_hbm, after_ref, out_ref, owner_ref, dest_ref, slot_ref, count_ref, sems):
    fetches = [
        pltpu.make_async_copy(owner_hbm, owner_ref, sems.at[0]),
        pltpu.make_async_copy(dest_hbm, dest_ref, sems.at[1]),
    ]
    for fetch in fetches:
        fetch.start()
    for fetch in fetches:
        fetch.wait()
    mine = lax.axis_index("cube")
    column = lax.axis_index("grid")
    blocks = owner_ref.shape[0]
    in_range = blocks // grids
    children = dest_ref.shape[0] // cubes
    none = grids * slots
    places = 2 * cubes + grids
    child_places = places + cubes * slots
    for r in range(grids):

        def count_own(i, seen):
            b = r * in_range + i
            own = owner_ref[b] == mine
            slot_ref[b] = jnp.where(own, r * slots + seen, none)
            return seen + own.astype(I32)

        out_ref[2 * cubes + r] = lax.fori_loop(0, in_range, count_own, I32(0), unroll=8)
    for d in range(cubes):
        source = jnp.bitwise_xor(mine, d)
        slot, which = I32(none), I32(0)
        for k in range(children):
            b = dest_ref[source * children + k]
            here = slot_ref[b]
            which = jnp.where(here < none, k, which)
            slot = jnp.minimum(slot, here)
            local_b = b - column * in_range
            inside = jnp.logical_and(local_b >= 0, local_b < in_range)
            out_ref[child_places + d * children + k] = jnp.where(inside, local_b, in_range)
        out_ref[d] = slot
        out_ref[cubes + d] = which
        count_ref[d] = 0
        for k in range(slots):
            out_ref[places + d * slots + k] = in_range

    def place(i, carry):
        d = jnp.bitwise_xor(owner_ref[column * in_range + i], mine)
        k = count_ref[d]
        out_ref[places + d * slots + k] = i
        count_ref[d] = k + 1
        return carry

    lax.fori_loop(0, in_range, place, 0, unroll=8)


def own_body(cubes, grids, span, rows, plan_ref, turned_ref, mine_ref, *refs):
    rests = refs[:grids]
    entries_ref, factor_ref = refs[grids:]
    column = lax.axis_index("grid")
    depth = rests[0].shape[1]
    for e in range(grids):
        r = jnp.bitwise_xor(column, e)
        ids = lax.broadcasted_iota(I32, (span, depth), 0)
        live = ids < plan_ref[2 * cubes + r] * rows
        for d in range(grids):
            if e == 0:
                piece = mine_ref[pl.ds(0, span), pl.ds(d * depth, depth)]
            else:
                k = d ^ e
                at = (k if k < d else k - 1) * span
                piece = rests[d][pl.ds(at, span), :]
            piece = jnp.where(live, piece.astype(F32), 0.0).astype(BF16)
            entries_ref[rows_at(r, span), pl.ds(d * depth, depth)] = piece
    own = jnp.dot(entries_ref[...], turned_ref[...], preferred_element_type=F32)
    factor_ref[pl.ds(0, entries_ref.shape[0]), :] = own.astype(BF16)


def marker_body(after_ref, out_ref):
    out_ref[...] = jnp.zeros_like(out_ref)


def join_body(*refs):
    pass


def add_children(cubes, grids, slots, rows, children, plan_ref, pieces, ranged, touched, total):
    span = slots * rows
    base = span + children * rows
    panel = ranged.shape[1]
    chunks = total.shape[1] // panel
    child_places = 2 * cubes + grids + cubes * slots
    in_range = ranged.shape[0] // rows - 1
    for d, piece in pieces.items():
        at = rows_at(plan_ref[d], rows)
        touched[at, :] += piece[rows_at(slots + plan_ref[cubes + d], rows), :].astype(F32)
        for j in range(chunks):
            part = pl.ds(base + ((d & 1) * chunks + j) * rows, rows)
            total[at, pl.ds(j * panel, panel)] += piece[part, :].astype(F32)
        for k in range(children):
            place = plan_ref[child_places + d * children + k]

            @pl.when(place < in_range)
            def _():
                ranged[rows_at(place, rows), :] += piece[pl.ds(span + k * rows, rows), :].astype(F32)


def early_body(cubes, grids, slots, rows, children, plan_ref, entries_ref, *refs):
    pieces = dict(enumerate(refs[:-3]))
    ranged, touched, total = refs[-3:]
    places = 2 * cubes + grids
    none = entries_ref.shape[0] // rows
    ranged[...] = jnp.zeros_like(ranged)
    total[...] = jnp.zeros_like(total)
    for d in range(cubes):
        slot = plan_ref[d]
        touched[rows_at(slot, rows), :] = entries_ref[rows_at(jnp.minimum(slot, none - 1), rows), :].astype(F32)
    for d, piece in pieces.items():
        for k in range(slots):
            at = rows_at(plan_ref[places + d * slots + k], rows)
            ranged[at, :] = piece[pl.ds(k * rows, rows), :].astype(F32)
    add_children(cubes, grids, slots, rows, children, plan_ref, pieces, ranged, touched, total)


def schur_body(cubes, grids, slots, rows, children, plan_ref, turned_ref, *refs):
    pieces = {cubes - 2: refs[0], cubes - 1: refs[1]}
    out_ref, panel_ref, ranged, touched, total, factor_ref, few = refs[6:]
    column = lax.axis_index("grid")
    own_rows, width = out_ref.shape
    depth = panel_ref.shape[0]
    places = 2 * cubes + grids
    in_range = width // rows
    for d, piece in pieces.items():
        for k in range(slots):
            place = plan_ref[places + d * slots + k]

            @pl.when(place < in_range)
            def _():
                ranged[rows_at(place, rows), :] += piece[pl.ds(k * rows, rows), :].astype(F32)

    add_children(cubes, grids, slots, rows, children, plan_ref, pieces, ranged, touched, total)
    for d in range(cubes):
        few[pl.ds(d * rows, rows), :] = touched[rows_at(plan_ref[d], rows), :].astype(BF16)
    redone = jnp.dot(few[...], turned_ref[...], preferred_element_type=F32).astype(BF16)
    for d in range(cubes):
        factor_ref[rows_at(plan_ref[d], rows), :] = redone[d * rows : (d + 1) * rows, :]
    column_factor = jnp.dot(
        ranged[pl.ds(0, width), :].astype(BF16), turned_ref[...], preferred_element_type=F32
    ).astype(BF16)
    product = lax.dot_general(
        factor_ref[pl.ds(0, own_rows), :], column_factor, (((1,), (1,)), ((), ())), preferred_element_type=F32
    )
    out_ref[...] = (total[pl.ds(0, own_rows), :] - product).astype(BF16)
    if depth % 128 == 0:
        cols = pl.ds(pl.multiple_of(column * depth, depth), depth)
        panel_ref[...] = factor_ref[pl.ds(0, own_rows), cols].astype(F32).T.astype(BF16)
    else:
        for r in range(grids):

            @pl.when(column == r)
            def _():
                part = factor_ref[pl.ds(0, own_rows), pl.ds(r * depth, depth)]
                panel_ref[...] = part.astype(F32).T.astype(BF16)


def local(
    child_update, child_panel, panel_entries, panel_inverse, block_owner, child_dest, child_rows
):
    cubes = lax.axis_size("cube")
    grids = lax.axis_size("grid")
    chips = cubes // 2
    children, rows = child_rows.shape
    width = child_update.shape[1]
    depth = child_panel.shape[0]
    panel = panel_inverse.shape[0]
    own_rows = panel_entries.shape[1]
    slots = own_rows // rows // grids
    span = slots * rows
    base = span + children * rows
    sent = base + 2 * rows * (width // panel)
    like = jax.ShapeDtypeStruct
    small = own_rows * width <= 512 * 512
    kept = pltpu.VMEM if small else like

    def in_hbm(x):
        return pltpu.with_memory_space_constraint(x, pltpu.HBM)

    def join(first, *others, cost=0):
        if small:
            first, *others = (
                pltpu.with_memory_space_constraint(x, pltpu.SMEM if x.dtype == I32 else pltpu.VMEM)
                for x in (first, *others)
            )
        return pl.pallas_call(
            join_body,
            out_shape=kept(first.shape, first.dtype),
            in_specs=[ANY] * (1 + len(others)),
            out_specs=ANY,
            input_output_aliases={0: 0},
            cost_estimate=pl.CostEstimate(flops=cost, bytes_accessed=0, transcendentals=0),
        )(first, *others)

    def swap(x, axis, d):
        n = lax.axis_size(axis)
        return lax.ppermute(x, axis, [(i, i ^ d) for i in range(n)])

    rest_rows = (grids - 1) * span
    *firsts, flipped = call(
        functools.partial(first_body, grids, span),
        [kept((base, depth), BF16)] * grids + [kept((own_rows, depth), BF16)],
        [ANY] * 3,
        [
            pltpu.VMEM(child_rows.shape, I32),
            pltpu.VMEM(child_panel.shape[::-1], BF16),
            pltpu.VMEM(panel_entries.shape, BF16),
            pltpu.SemaphoreType.DMA((3,)),
        ],
        2 * rows * rows * children * depth,
        4 * own_rows * depth,
        limit=28,
    )(in_hbm(child_rows), in_hbm(child_panel.T), in_hbm(panel_entries))
    *rests, blocks, turned = call(
        functools.partial(second_body, cubes, grids, span),
        [kept((rest_rows, depth), BF16)] * grids
        + [kept((cubes * rows, width), BF16), kept((panel, panel), BF16)],
        [ANY] * 5 + [VMEM],
        [
            pltpu.SMEM(block_owner.shape, I32),
            pltpu.SMEM(child_dest.shape, I32),
            pltpu.VMEM(child_rows.shape, I32),
            pltpu.VMEM(child_update.shape, BF16),
            pltpu.SemaphoreType.DMA((4 + grids,)),
        ],
        2 * rows * rows * children * width,
        4 * own_rows * depth,
        limit=28,
    )(*(in_hbm(x) for x in (block_owner, child_dest, child_rows, child_update, panel_inverse)), flipped)
    for d in [*range(2, grids), 1]:
        firsts[d] = swap(firsts[d], "grid", d)
    for d in range(3, grids):
        rests[d] = swap(rests[d], "grid", d)
    parts = [*range(2, grids), 0, 1]
    packed = call(
        functools.partial(pack_body, parts, rows, base),
        [kept((sent, panel), BF16)] * chips,
        [VMEM] * (1 + grids),
        [],
        1000,
        2 * chips * sent * panel,
    )(blocks, *(firsts[d] for d in parts))
    arrived_rest = rests[-1]
    rests[2] = swap(join(rests[2], packed[0]), "grid", 2)
    rests[1] = swap(join(rests[1], rests[-1]), "grid", 1)
    arrived = [packed[0]] + [swap(packed[i], "cube", 2 * i) for i in range(1, chips)]
    rests[-1] = join(rests[-1], packed[0], cost=JOIN_COST)
    last = pltpu.with_memory_space_constraint(arrived_rest, pltpu.VMEM) if small else arrived_rest
    plan = call(
        functools.partial(plan_body, cubes, grids, slots),
        [pltpu.SMEM((2 * cubes + grids + cubes * (slots + children),), I32)],
        [ANY] * 3,
        [
            pltpu.SMEM(block_owner.shape, I32),
            pltpu.SMEM(child_dest.shape, I32),
            pltpu.SMEM(block_owner.shape, I32),
            pltpu.SMEM((cubes,), I32),
            pltpu.SemaphoreType.DMA((2,)),
        ],
        100000,
        6000000,
        [SMEM],
    )(in_hbm(block_owner), in_hbm(child_dest), last)[0]
    plan = pltpu.with_memory_space_constraint(plan, pltpu.SMEM)
    entries, before = call(
        functools.partial(own_body, cubes, grids, span, rows),
        [kept((own_rows, panel), BF16), kept((own_rows + rows, panel), BF16)],
        [SMEM] + [VMEM] * (2 + grids),
        [],
        300000000,
        2 * own_rows * panel * panel,
    )(plan, turned, packed[0], *rests)
    arrived[-1] = join(arrived[-1], *rests[1:])
    pieces = []
    for piece in arrived:
        pieces += [piece, swap(piece, "cube", 1)]
    sizes = (cubes, grids, slots, rows, children)
    shapes = [(width + rows, panel), (own_rows + rows, panel), (own_rows + rows, width)]
    early = call(
        functools.partial(early_body, *sizes),
        [kept(shape, F32) for shape in shapes],
        [SMEM] + [VMEM] * (cubes - 1),
        [],
        1000,
        4 * width * panel,
        limit=16 if small else 56,
    )(plan, entries, *pieces[:-2])
    return tuple(
        call(
            functools.partial(schur_body, *sizes),
            [like((own_rows, width), BF16), like((depth, own_rows), BF16)]
            + [kept(shape, F32) for shape in shapes]
            + [kept((own_rows + rows, panel), BF16)],
            [SMEM] + [VMEM] * 7,
            [pltpu.VMEM((cubes * rows, panel), BF16)],
            2 * own_rows * width * panel,
            2 * (own_rows * width + (own_rows + cubes * span) * panel),
            limit=16 if small else 56,
            aliases={4: 2, 5: 3, 6: 4, 7: 5},
        )(plan, turned, *pieces[-2:], *early, before)[:2]
    )


def solution(mesh):
    placed = (
        P("cube", "grid"),
        P("grid", "cube"),
        P("grid", "cube"),
        P(),
        P(),
        P(),
        P("cube", None),
    )
    return jax.shard_map(
        local,
        mesh=mesh,
        in_specs=placed,
        out_specs=(P("cube", "grid"), P("grid", "cube")),
        check_vma=False,
    )
```

```python
import functools

import jax
import jax.numpy as jnp
from jax import lax
from jax.experimental import pallas as pl
from jax.experimental.pallas import tpu as pltpu
from jax.sharding import PartitionSpec as P

F32 = jnp.float32
BF16 = jnp.bfloat16
I32 = jnp.int32
VMEM = pl.BlockSpec(memory_space=pltpu.VMEM)
SMEM = pl.BlockSpec(memory_space=pltpu.SMEM)
ANY = pl.BlockSpec(memory_space=pl.ANY)
MIB = 1024 * 1024
JOIN_COST = 1500000000


def call(body, outs, in_specs, scratch, flops, moved, out_specs=None, limit=16, aliases={}):
    return pl.pallas_call(
        body,
        out_shape=outs,
        in_specs=in_specs,
        out_specs=[VMEM] * len(outs) if out_specs is None else out_specs,
        scratch_shapes=scratch,
        input_output_aliases=aliases,
        compiler_params=pltpu.CompilerParams(vmem_limit_bytes=limit * MIB),
        cost_estimate=pl.CostEstimate(flops=flops, bytes_accessed=moved, transcendentals=0),
    )


def rows_at(index, size):
    return pl.ds(pl.multiple_of(index * size, size), size)


def first_body(grids, span, rows_hbm, panel_hbm, entries_hbm, *refs):
    firsts, flipped = refs[:grids], refs[grids]
    rows_ref, panel_ref, entries_ref, sems = refs[grids + 1 :]
    copies = [
        pltpu.make_async_copy(source, target, sems.at[i])
        for i, (source, target) in enumerate(
            ((entries_hbm, entries_ref), (panel_hbm, panel_ref), (rows_hbm, rows_ref))
        )
    ]
    for copy in copies:
        copy.start()
    column = lax.axis_index("grid")
    children, rows = rows_ref.shape
    copies[0].wait()
    flipped[...] = entries_ref[...].astype(F32).T.astype(BF16)
    for d in range(grids):
        firsts[d][pl.ds(0, span), :] = flipped[rows_at(jnp.bitwise_xor(column, d), span), :]
    for copy in copies[1:]:
        copy.wait()
    for k in range(children):
        want = rows_ref[k : k + 1, :]
        put = (lax.broadcasted_iota(I32, (rows, rows), 0) == want).astype(BF16)
        part = pl.ds(k * rows, rows)
        placed = jnp.dot(put, panel_ref[part, :], preferred_element_type=F32).astype(BF16)
        for d in range(grids):
            firsts[d][pl.ds(span + k * rows, rows), :] = placed


def second_body(
    cubes, grids, span, owner_hbm, dest_hbm, rows_hbm, update_hbm, inverse_hbm, flipped, *refs
):
    rests, blocks_ref, turned_ref = refs[:grids], *refs[grids : grids + 2]
    owner_ref, dest_ref, rows_ref, update_ref, sems = refs[grids + 2 :]
    copies = [
        pltpu.make_async_copy(source, target, sems.at[i])
        for i, (source, target) in enumerate(
            (
                (rows_hbm, rows_ref),
                (update_hbm, update_ref),
                (owner_hbm, owner_ref),
                (dest_hbm, dest_ref),
            )
        )
    ]
    mine = lax.axis_index("cube")
    column = lax.axis_index("grid")
    depth = flipped.shape[1]
    for d in range(grids):
        part = inverse_hbm.at[rows_at(jnp.bitwise_xor(column, d), depth), :]
        copies.append(pltpu.make_async_copy(part, turned_ref.at[pl.ds(d * depth, depth), :], sems.at[4 + d]))
    for copy in copies:
        copy.start()
    children, rows = rows_ref.shape
    blocks_ref[...] = jnp.zeros_like(blocks_ref)
    for d in range(grids):
        piece = flipped[rows_at(jnp.bitwise_xor(column, d), span), :]
        for e in range(grids):
            if e != d:
                k = d if d < e else d - 1
                rests[e][pl.ds(k * span, span), :] = piece
    for copy in copies[:4]:
        copy.wait()
    for k in range(children):
        want = rows_ref[k : k + 1, :]
        put = (lax.broadcasted_iota(I32, (rows, rows), 0) == want).astype(BF16)
        part = pl.ds(k * rows, rows)
        moved = jnp.dot(put, update_ref[part, :], preferred_element_type=F32).astype(BF16)
        d = jnp.bitwise_xor(owner_ref[dest_ref[mine * children + k]], mine)
        blocks_ref[rows_at(d, rows), :] = moved
    for copy in copies[4:]:
        copy.wait()


def pack_body(parts, rows, base, blocks_ref, *refs):
    firsts, payloads = refs[: len(parts)], refs[len(parts) :]
    depth = firsts[0].shape[1]
    panel = payloads[0].shape[1]
    chunks = blocks_ref.shape[1] // panel
    for d, first in zip(parts, firsts):
        piece = first[...]
        for payload in payloads:
            payload[pl.ds(0, base), pl.ds(d * depth, depth)] = piece
    for i, payload in enumerate(payloads):
        for half in range(2):
            for j in range(chunks):
                at = base + (half * chunks + j) * rows
                block = blocks_ref[pl.ds((2 * i + half) * rows, rows), pl.ds(j * panel, panel)]
                payload[pl.ds(at, rows), :] = block


def plan_body(cubes, grids, slots, owner_hbm, dest_hbm, after_ref, out_ref, owner_ref, dest_ref, slot_ref, count_ref, sems):
    fetches = [
        pltpu.make_async_copy(owner_hbm, owner_ref, sems.at[0]),
        pltpu.make_async_copy(dest_hbm, dest_ref, sems.at[1]),
    ]
    for fetch in fetches:
        fetch.start()
    for fetch in fetches:
        fetch.wait()
    mine = lax.axis_index("cube")
    column = lax.axis_index("grid")
    blocks = owner_ref.shape[0]
    in_range = blocks // grids
    children = dest_ref.shape[0] // cubes
    none = grids * slots
    places = 2 * cubes + grids
    child_places = places + cubes * slots
    for r in range(grids):

        def count_own(i, seen):
            b = r * in_range + i
            own = owner_ref[b] == mine
            slot_ref[b] = jnp.where(own, r * slots + seen, none)
            return seen + own.astype(I32)

        out_ref[2 * cubes + r] = lax.fori_loop(0, in_range, count_own, I32(0), unroll=8)
    for d in range(cubes):
        source = jnp.bitwise_xor(mine, d)
        slot, which = I32(none), I32(0)
        for k in range(children):
            b = dest_ref[source * children + k]
            here = slot_ref[b]
            which = jnp.where(here < none, k, which)
            slot = jnp.minimum(slot, here)
            local_b = b - column * in_range
            inside = jnp.logical_and(local_b >= 0, local_b < in_range)
            out_ref[child_places + d * children + k] = jnp.where(inside, local_b, in_range)
        out_ref[d] = slot
        out_ref[cubes + d] = which
        count_ref[d] = 0
        for k in range(slots):
            out_ref[places + d * slots + k] = in_range

    def place(i, carry):
        d = jnp.bitwise_xor(owner_ref[column * in_range + i], mine)
        k = count_ref[d]
        out_ref[places + d * slots + k] = i
        count_ref[d] = k + 1
        return carry

    lax.fori_loop(0, in_range, place, 0, unroll=8)


def own_body(cubes, grids, span, rows, plan_ref, turned_ref, mine_ref, *refs):
    rests = refs[:grids]
    entries_ref, factor_ref = refs[grids:]
    column = lax.axis_index("grid")
    depth = rests[0].shape[1]
    for e in range(grids):
        r = jnp.bitwise_xor(column, e)
        ids = lax.broadcasted_iota(I32, (span, depth), 0)
        live = ids < plan_ref[2 * cubes + r] * rows
        for d in range(grids):
            if e == 0:
                piece = mine_ref[pl.ds(0, span), pl.ds(d * depth, depth)]
            else:
                k = d ^ e
                at = (k if k < d else k - 1) * span
                piece = rests[d][pl.ds(at, span), :]
            piece = jnp.where(live, piece.astype(F32), 0.0).astype(BF16)
            entries_ref[rows_at(r, span), pl.ds(d * depth, depth)] = piece
    own = jnp.dot(entries_ref[...], turned_ref[...], preferred_element_type=F32)
    factor_ref[pl.ds(0, entries_ref.shape[0]), :] = own.astype(BF16)


def marker_body(after_ref, out_ref):
    out_ref[...] = jnp.zeros_like(out_ref)


def join_body(*refs):
    pass


def add_children(cubes, grids, slots, rows, children, plan_ref, pieces, ranged, touched, total):
    span = slots * rows
    base = span + children * rows
    panel = ranged.shape[1]
    chunks = total.shape[1] // panel
    child_places = 2 * cubes + grids + cubes * slots
    in_range = ranged.shape[0] // rows - 1
    for d, piece in pieces.items():
        at = rows_at(plan_ref[d], rows)
        touched[at, :] += piece[rows_at(slots + plan_ref[cubes + d], rows), :].astype(F32)
        for j in range(chunks):
            part = pl.ds(base + ((d & 1) * chunks + j) * rows, rows)
            total[at, pl.ds(j * panel, panel)] += piece[part, :].astype(F32)
        for k in range(children):
            place = plan_ref[child_places + d * children + k]

            @pl.when(place < in_range)
            def _():
                ranged[rows_at(place, rows), :] += piece[pl.ds(span + k * rows, rows), :].astype(F32)


def early_body(cubes, grids, slots, rows, children, plan_ref, entries_ref, *refs):
    pieces = dict(enumerate(refs[:-3]))
    ranged, touched, total = refs[-3:]
    places = 2 * cubes + grids
    none = entries_ref.shape[0] // rows
    ranged[...] = jnp.zeros_like(ranged)
    total[...] = jnp.zeros_like(total)
    for d in range(cubes):
        slot = plan_ref[d]
        touched[rows_at(slot, rows), :] = entries_ref[rows_at(jnp.minimum(slot, none - 1), rows), :].astype(F32)
    for d, piece in pieces.items():
        for k in range(slots):
            at = rows_at(plan_ref[places + d * slots + k], rows)
            ranged[at, :] = piece[pl.ds(k * rows, rows), :].astype(F32)
    add_children(cubes, grids, slots, rows, children, plan_ref, pieces, ranged, touched, total)


def schur_body(cubes, grids, slots, rows, children, plan_ref, turned_ref, *refs):
    pieces = {cubes - 2: refs[0], cubes - 1: refs[1]}
    out_ref, panel_ref, ranged, touched, total, factor_ref, few = refs[6:]
    column = lax.axis_index("grid")
    own_rows, width = out_ref.shape
    depth = panel_ref.shape[0]
    places = 2 * cubes + grids
    in_range = width // rows
    for d, piece in pieces.items():
        for k in range(slots):
            place = plan_ref[places + d * slots + k]

            @pl.when(place < in_range)
            def _():
                ranged[rows_at(place, rows), :] += piece[pl.ds(k * rows, rows), :].astype(F32)

    add_children(cubes, grids, slots, rows, children, plan_ref, pieces, ranged, touched, total)
    for d in range(cubes):
        few[pl.ds(d * rows, rows), :] = touched[rows_at(plan_ref[d], rows), :].astype(BF16)
    redone = jnp.dot(few[...], turned_ref[...], preferred_element_type=F32).astype(BF16)
    for d in range(cubes):
        factor_ref[rows_at(plan_ref[d], rows), :] = redone[d * rows : (d + 1) * rows, :]
    column_factor = jnp.dot(
        ranged[pl.ds(0, width), :].astype(BF16), turned_ref[...], preferred_element_type=F32
    ).astype(BF16)
    product = lax.dot_general(
        factor_ref[pl.ds(0, own_rows), :], column_factor, (((1,), (1,)), ((), ())), preferred_element_type=F32
    )
    out_ref[...] = (total[pl.ds(0, own_rows), :] - product).astype(BF16)
    if depth % 128 == 0:
        cols = pl.ds(pl.multiple_of(column * depth, depth), depth)
        panel_ref[...] = factor_ref[pl.ds(0, own_rows), cols].astype(F32).T.astype(BF16)
    else:
        for r in range(grids):

            @pl.when(column == r)
            def _():
                part = factor_ref[pl.ds(0, own_rows), pl.ds(r * depth, depth)]
                panel_ref[...] = part.astype(F32).T.astype(BF16)


def local(
    child_update, child_panel, panel_entries, panel_inverse, block_owner, child_dest, child_rows
):
    cubes = lax.axis_size("cube")
    grids = lax.axis_size("grid")
    chips = cubes // 2
    children, rows = child_rows.shape
    width = child_update.shape[1]
    depth = child_panel.shape[0]
    panel = panel_inverse.shape[0]
    own_rows = panel_entries.shape[1]
    slots = own_rows // rows // grids
    span = slots * rows
    base = span + children * rows
    sent = base + 2 * rows * (width // panel)
    like = jax.ShapeDtypeStruct
    small = own_rows * width <= 512 * 512
    kept = pltpu.VMEM if small else like

    def in_hbm(x):
        return pltpu.with_memory_space_constraint(x, pltpu.HBM)

    def join(first, *others, cost=0):
        if small:
            first, *others = (
                pltpu.with_memory_space_constraint(x, pltpu.SMEM if x.dtype == I32 else pltpu.VMEM)
                for x in (first, *others)
            )
        return pl.pallas_call(
            join_body,
            out_shape=kept(first.shape, first.dtype),
            in_specs=[ANY] * (1 + len(others)),
            out_specs=ANY,
            input_output_aliases={0: 0},
            cost_estimate=pl.CostEstimate(flops=cost, bytes_accessed=0, transcendentals=0),
        )(first, *others)

    def swap(x, axis, d):
        n = lax.axis_size(axis)
        return lax.ppermute(x, axis, [(i, i ^ d) for i in range(n)])

    rest_rows = (grids - 1) * span
    *firsts, flipped = call(
        functools.partial(first_body, grids, span),
        [kept((base, depth), BF16)] * grids + [kept((own_rows, depth), BF16)],
        [ANY] * 3,
        [
            pltpu.VMEM(child_rows.shape, I32),
            pltpu.VMEM(child_panel.shape[::-1], BF16),
            pltpu.VMEM(panel_entries.shape, BF16),
            pltpu.SemaphoreType.DMA((3,)),
        ],
        2 * rows * rows * children * depth,
        4 * own_rows * depth,
        limit=28,
    )(in_hbm(child_rows), in_hbm(child_panel.T), in_hbm(panel_entries))
    *rests, blocks, turned = call(
        functools.partial(second_body, cubes, grids, span),
        [kept((rest_rows, depth), BF16)] * grids
        + [kept((cubes * rows, width), BF16), kept((panel, panel), BF16)],
        [ANY] * 5 + [VMEM],
        [
            pltpu.SMEM(block_owner.shape, I32),
            pltpu.SMEM(child_dest.shape, I32),
            pltpu.VMEM(child_rows.shape, I32),
            pltpu.VMEM(child_update.shape, BF16),
            pltpu.SemaphoreType.DMA((4 + grids,)),
        ],
        2 * rows * rows * children * width,
        4 * own_rows * depth,
        limit=28,
    )(*(in_hbm(x) for x in (block_owner, child_dest, child_rows, child_update, panel_inverse)), flipped)
    for d in [*range(2, grids), 1]:
        firsts[d] = swap(firsts[d], "grid", d)
    for d in range(3, grids):
        rests[d] = swap(rests[d], "grid", d)
    parts = [*range(grids - 1, 1, -1), 0, 1]
    packed = call(
        functools.partial(pack_body, parts, rows, base),
        [kept((sent, panel), BF16)] * chips,
        [VMEM] * (1 + grids),
        [],
        1000,
        2 * chips * sent * panel,
    )(blocks, *(firsts[d] for d in parts))
    arrived_rest = rests[-1]
    rests[2] = swap(join(rests[2], packed[0]), "grid", 2)
    rests[1] = swap(join(rests[1], rests[-1]), "grid", 1)
    arrived = [packed[0]] + [swap(packed[i], "cube", 2 * i) for i in range(1, chips)]
    rests[-1] = join(rests[-1], packed[0], cost=JOIN_COST)
    last = pltpu.with_memory_space_constraint(arrived_rest, pltpu.VMEM) if small else arrived_rest
    plan = call(
        functools.partial(plan_body, cubes, grids, slots),
        [pltpu.SMEM((2 * cubes + grids + cubes * (slots + children),), I32)],
        [ANY] * 3,
        [
            pltpu.SMEM(block_owner.shape, I32),
            pltpu.SMEM(child_dest.shape, I32),
            pltpu.SMEM(block_owner.shape, I32),
            pltpu.SMEM((cubes,), I32),
            pltpu.SemaphoreType.DMA((2,)),
        ],
        100000,
        6000000,
        [SMEM],
    )(in_hbm(block_owner), in_hbm(child_dest), last)[0]
    plan = pltpu.with_memory_space_constraint(plan, pltpu.SMEM)
    entries, before = call(
        functools.partial(own_body, cubes, grids, span, rows),
        [kept((own_rows, panel), BF16), kept((own_rows + rows, panel), BF16)],
        [SMEM] + [VMEM] * (2 + grids),
        [],
        300000000,
        2 * own_rows * panel * panel,
    )(plan, turned, packed[0], *rests)
    arrived[-1] = join(arrived[-1], *rests[1:])
    pieces = []
    for piece in arrived:
        pieces += [piece, swap(piece, "cube", 1)]
    sizes = (cubes, grids, slots, rows, children)
    shapes = [(width + rows, panel), (own_rows + rows, panel), (own_rows + rows, width)]
    early = call(
        functools.partial(early_body, *sizes),
        [kept(shape, F32) for shape in shapes],
        [SMEM] + [VMEM] * (cubes - 1),
        [],
        1000,
        4 * width * panel,
        limit=16 if small else 56,
    )(plan, entries, *pieces[:-2])
    return tuple(
        call(
            functools.partial(schur_body, *sizes),
            [like((own_rows, width), BF16), like((depth, own_rows), BF16)]
            + [kept(shape, F32) for shape in shapes]
            + [kept((own_rows + rows, panel), BF16)],
            [SMEM] + [VMEM] * 7,
            [pltpu.VMEM((cubes * rows, panel), BF16)],
            2 * own_rows * width * panel,
            2 * (own_rows * width + (own_rows + cubes * span) * panel),
            limit=16 if small else 56,
            aliases={4: 2, 5: 3, 6: 4, 7: 5},
        )(plan, turned, *pieces[-2:], *early, before)[:2]
    )


def solution(mesh):
    placed = (
        P("cube", "grid"),
        P("grid", "cube"),
        P("grid", "cube"),
        P(),
        P(),
        P(),
        P("cube", None),
    )
    return jax.shard_map(
        local,
        mesh=mesh,
        in_specs=placed,
        out_specs=(P("cube", "grid"), P("grid", "cube")),
        check_vma=False,
    )
```
